32 devices in a mesh: groups: 2 (over y), expert: 4 (over z), decode: 4 (over x, core), tensor: 1.
Axes of the slice: x: 2, y: 2, z: 4, core: 2. Of those that a mesh axis runs over, the one named last changes fastest.
Arguments:
- resid: bfloat16 [1024, 2560], P(('groups', 'expert')), parts along dimension 0, may hold values from -6 to 6
- moe_gain: float32 [2560], replicated, may hold values from 0.25 to 1.75
- attn_gain: float32 [2560], replicated, may hold values from 0.25 to 1.75
- gate_score: float32 [1024], P(('groups', 'expert')), parts along dimension 0, may hold values from 0.2 to 1
- expert_ids: int32 [1024, 1], P(('groups', 'expert')), parts along dimension 0, may hold values from 0 to 1
- w_gate: bfloat16 [4, 2560, 2048], P('expert', None, ('decode', 'tensor')), may hold values from -0.125 to 0.125
- w_up: bfloat16 [4, 2560, 2048], P('expert', None, ('decode', 'tensor')), may hold values from -0.125 to 0.125
- w_down: bfloat16 [4, 2048, 2560], P('expert', ('decode', 'tensor')), may hold values from -0.09375 to 0.09375
- shared_gate: bfloat16 [2560, 4096], P('expert', ('decode', 'tensor')), may hold values from -0.125 to 0.125
- shared_up: bfloat16 [2560, 4096], P('expert', ('decode', 'tensor')), may hold values from -0.125 to 0.125
- shared_down: bfloat16 [4096, 2560], P(('decode', 'tensor'), 'expert'), may hold values from -0.09375 to 0.09375
- w_kv: bfloat16 [2560, 2048], P('expert', ('decode', 'tensor')), may hold values from -0.125 to 0.125
- req_owner: int32 [8, 4], P(('groups', 'expert')), parts along dimension 0, may hold values from 0 to 3, each once within a row
- req_blocks: int32 [8, 4], P(('groups', 'expert')), parts along dimension 0, may hold values from 1 to 4, 8 in all within a row
Outputs:
- layer_out: bfloat16 [1024, 2560], P(('groups', 'expert'), ('decode', 'tensor')), parts along dimension 0
- kv_handed: bfloat16 [8, 4, 64, 4, 512], P(('groups', 'expert'), 'decode', None, None, 'tensor'), parts along dimension 0
The draws below stay inside these ranges and needn't reach their ends.
There are 2 independent parts, one for each index of `groups`. The reference program is written for one: setup_inputs(seed, part) draws one part's arguments, and reference() takes and returns one part's arrays. A program takes and returns all parts, laid end to end along the dimension named above; an argument that names none is the same for every part. Nothing has to cross between parts.
Inputs may be any that keep to these rules, and one draw needn't show every extreme that they name: `req_owner`: each shard's requests go to distinct decode owners. `req_blocks`: the 4 requests of a shard hold 8 blocks together.
All inputs are finite; a program needn't handle non-finite values.
Results may differ from the reference program's by a relative error of at most 0.018.
Values may be sent and summed in bfloat16 or wider, within the bound.
No kernel may reach another device: no remote copies, remote signals or barrier semaphores. Data moves between devices by JAX's collectives and lax.ppermute only.
A program may use at most 64 MiB of HBM per device.

```python
import math
import jax
import jax.numpy as jnp
import numpy as np
from jax import lax

D = 2560
FH = 4096
SH = 4096
KVH = 8
HD = 128
BLOCK = 16
TOK_DEV = 128
EXPERTS = 2
CAP = 128
BLOCKS_DEV = 8
QCAP = 4
TOKENS = 512
N_EXPERT = 4
N_DECODE = 4
N_TENSOR = 1


def steps_of(key, shape, shards, smallest, top_value):
    level, own = 1.0, jax.random.fold_in(key, 6)
    for position, parts in shards:
        heights = jnp.exp(jax.random.uniform(jax.random.fold_in(own, position), (parts,), jnp.float32, smallest / len(shards), top_value / len(shards)))
        level = level * jnp.repeat(heights, shape[position] // parts).reshape([-1 if axis == position else 1 for axis in range(len(shape))])
    return level


def picks_of(rng, rows, amount, top, lift):
    ranking = jax.random.permutation(jax.random.fold_in(rng, 1), amount)
    pull = ranking
    for power in range(3):
        pull = pull * pull // amount
    pull = pull * lift // amount
    lots = jax.random.randint(jax.random.fold_in(rng, 2), (rows, amount), 0, 4096) + pull
    sure = jax.random.permutation(jax.random.fold_in(rng, 3), rows)[jnp.arange(amount) % rows]
    lots = jnp.where(jnp.arange(rows)[:, None] == sure[None, :], 1 << 14, lots)
    score = lots * amount + jnp.arange(amount)
    return lax.top_k(score.astype(jnp.int32), top)[1].astype(jnp.int32)


def split_up(amount, total, reach, slope):
    weights = [(1 << 20) // math.isqrt(rank ** slope) + 1 for rank in range(2, amount + 1)]
    spare, counts = total - reach - (amount - 1), [1] * (amount - 1)
    while spare > 0:
        movable = [i for i in range(amount - 1) if counts[i] < reach]
        pool, remaining = sum([weights[i] for i in movable]), spare
        for i in movable:
            addition = min(reach - counts[i], max(1, remaining * weights[i] // pool), spare)
            counts[i] = counts[i] + addition
            spare = spare - addition
    return np.array([reach] + counts)


def uneven(key, amount, total, limit, skew):
    if amount == 2:
        one = jax.random.randint(key, (), max(1, total - limit), min(limit, total - 1) + 1)
        return jnp.stack([one, total - one])
    lengths = jnp.asarray(split_up(amount, total, limit, skew), jnp.int32)
    couples = (amount - 1) // 2
    source_of, taker = lengths[1:1 + 2 * couples:2], lengths[2:2 + 2 * couples:2]
    margin = jnp.minimum(source_of - 1, limit - taker)
    shifted = jax.random.randint(jax.random.fold_in(key, 1), (couples,), 0, 1 << 20) % (margin + 1)
    lengths = lengths.at[1:1 + 2 * couples:2].set(source_of - shifted).at[2:2 + 2 * couples:2].set(taker + shifted)
    return lengths[jax.random.permutation(jax.random.fold_in(key, 2), amount)]


def noise(key, extent, deviation, bound, shards=(), kind=jnp.bfloat16):
    level = steps_of(key, extent, shards, -0.22, 0.18) if shards else 1.0
    values = jax.random.normal(key, extent, jnp.float32) * deviation * level
    return jnp.minimum(jnp.maximum(values, -bound), bound).astype(kind)


def setup_inputs(seed: int = 0, part: int = 0) -> dict:
    streams_of = jax.random.split(jax.random.key(seed), 15)
    part_splits = jax.random.split(jax.random.fold_in(streams_of[14], part), 15)
    resid = noise(part_splits[0], (TOKENS, D), 1.0, 6.0, ((0, 4),))
    moe_gain = jnp.clip(1.0 + 0.15 * jax.random.normal(streams_of[1], (D,), jnp.float32), 0.25, 1.75)
    attn_gain = jnp.clip(1.0 + 0.15 * jax.random.normal(streams_of[2], (D,), jnp.float32), 0.25, 1.75)
    gate_score = jnp.clip(0.2 + 0.8 * jax.random.uniform(part_splits[3], (TOKENS,), jnp.float32) ** steps_of(part_splits[3], (TOKENS,), ((0, 4),), -0.2, 0.2), 0.2, 1.0)
    expert_ids = picks_of(part_splits[4], TOKENS, EXPERTS, 1, 4096)
    w_gate = noise(streams_of[5], (N_EXPERT, D, FH // 2), D ** -0.5, 0.125, ((0, 4), (2, 4)))
    w_up = noise(streams_of[6], (N_EXPERT, D, FH // 2), D ** -0.5, 0.125, ((0, 4), (2, 4)))
    w_down = noise(streams_of[7], (N_EXPERT, FH // 2, D), FH ** -0.5, 0.09375, ((0, 4), (1, 4)))
    shared_gate = noise(streams_of[8], (D, SH), D ** -0.5, 0.125, ((0, 4), (1, 4)))
    shared_up = noise(streams_of[9], (D, SH), D ** -0.5, 0.125, ((0, 4), (1, 4)))
    shared_down = noise(streams_of[10], (SH, D), SH ** -0.5, 0.09375, ((0, 4), (1, 4)))
    w_kv = noise(streams_of[11], (D, KVH * 2 * HD), D ** -0.5, 0.125, ((0, 4), (1, 4)))
    req_owner = jax.vmap(lambda own: jax.random.permutation(own, N_DECODE))(jax.random.split(part_splits[12], N_EXPERT)).reshape((N_EXPERT, N_DECODE)).astype(jnp.int32)
    req_blocks = jax.vmap(lambda own: uneven(own, N_DECODE, BLOCKS_DEV, QCAP, 1))(jax.random.split(part_splits[13], N_EXPERT)).reshape((N_EXPERT, N_DECODE)).astype(jnp.int32)
    return {"resid": resid, "moe_gain": moe_gain, "attn_gain": attn_gain, "gate_score": gate_score, "expert_ids": expert_ids, "w_gate": w_gate, "w_up": w_up, "w_down": w_down, "shared_gate": shared_gate, "shared_up": shared_up, "shared_down": shared_down, "w_kv": w_kv, "req_owner": req_owner, "req_blocks": req_blocks}


def rms_scale(values, gain):
    return values * lax.rsqrt(lax.optimization_barrier(jnp.mean(values * values, axis=-1, keepdims=True)) + 1e-05) * gain

def reference(resid, moe_gain, attn_gain, gate_score, expert_ids, w_gate, w_up, w_down, shared_gate, shared_up, shared_down, w_kv, req_owner, req_blocks):
    moe_in = rms_scale(resid.astype(jnp.float32), moe_gain).astype(jnp.bfloat16)
    shard_ids = expert_ids[:, 0].reshape(N_EXPERT, TOK_DEV)
    onehot = (shard_ids[:, :, None] == jnp.arange(EXPERTS, dtype=jnp.int32)[None, None, :]).astype(jnp.int32)
    slots = lax.optimization_barrier(jnp.sum((jnp.cumsum(onehot, axis=1) - 1) * onehot, axis=2))
    kept = slots < CAP
    sources = jnp.arange(N_EXPERT, dtype=jnp.int32)[:, None]
    dump_row = EXPERTS * N_EXPERT * CAP
    target = jnp.where(kept, (shard_ids * N_EXPERT + sources) * CAP + slots, dump_row).reshape(-1).astype(jnp.int32)
    buffer = jnp.zeros((dump_row + 1, D), jnp.bfloat16).at[target].set(moe_in)
    buffer = buffer[:dump_row].reshape(EXPERTS, N_EXPERT * CAP, D)
    slice_count = N_DECODE * N_TENSOR
    half_width = FH // 2
    slice_width = half_width // slice_count
    gate_pairs = w_gate.reshape(EXPERTS, 2, D, half_width)
    up_pairs = w_up.reshape(EXPERTS, 2, D, half_width)
    down_pairs = w_down.reshape(EXPERTS, 2, slice_count, slice_width, D)

    def expert_rows(operands):
        inputs, gate_two, up_two, down_two = operands
        total = jnp.zeros((N_EXPERT * CAP, D), jnp.float32)
        for half in range(2):
            gate_val = jnp.dot(inputs, gate_two[half], preferred_element_type=jnp.float32)
            up_val = jnp.dot(inputs, up_two[half], preferred_element_type=jnp.float32)
            hidden = (jax.nn.silu(gate_val) * up_val).astype(jnp.bfloat16)
            hidden = hidden.reshape(N_EXPERT * CAP, slice_count, slice_width).astype(jnp.float32)
            partial_terms = jnp.einsum('rsh,shd->srd', hidden, down_two[half].astype(jnp.float32)).astype(jnp.bfloat16)
            partial_terms = lax.optimization_barrier(partial_terms)
            total = total + lax.optimization_barrier(jnp.sum(partial_terms.astype(jnp.float32), axis=0))
        return total
    combined = lax.map(expert_rows, (buffer, gate_pairs, up_pairs, down_pairs))
    combined = jnp.concatenate([combined.reshape(dump_row, D), jnp.zeros((1, D), jnp.float32)], axis=0)
    routed = combined[target] * gate_score[:, None]
    shared_gate_val = jnp.dot(moe_in, shared_gate, preferred_element_type=jnp.float32)
    shared_up_val = jnp.dot(moe_in, shared_up, preferred_element_type=jnp.float32)
    shared_hidden = (jax.nn.silu(shared_gate_val) * shared_up_val).astype(jnp.bfloat16)
    shared_out = jnp.dot(shared_hidden, shared_down, preferred_element_type=jnp.float32)
    layer_out = (resid.astype(jnp.float32) + shared_out + routed).astype(jnp.bfloat16)
    attn_in = rms_scale(layer_out.astype(jnp.float32), attn_gain).astype(jnp.bfloat16)
    key_value = jnp.dot(attn_in, w_kv, preferred_element_type=jnp.float32).astype(jnp.bfloat16)
    group_width = KVH * 2 * HD // N_DECODE
    kv_blocks = key_value.reshape(N_EXPERT, BLOCKS_DEV, BLOCK, N_DECODE, group_width).astype(jnp.float32)
    starts = jnp.cumsum(req_blocks, axis=1) - req_blocks
    owner_index = jnp.arange(N_DECODE, dtype=jnp.int32)
    slot_index = jnp.arange(QCAP, dtype=jnp.int32)
    block_index = jnp.arange(BLOCKS_DEV, dtype=jnp.int32)
    chosen = req_owner[:, :, None, None, None] == owner_index[None, None, :, None, None]
    chosen = chosen & (slot_index[None, None, None, :, None] < req_blocks[:, :, None, None, None])
    chosen = chosen & (block_index[None, None, None, None, :] == starts[:, :, None, None, None] + slot_index[None, None, None, :, None])
    choose = lax.optimization_barrier(jnp.sum(chosen.astype(jnp.float32), axis=1))
    handed = jnp.einsum('soqb,sbige->soqige', choose, kv_blocks)
    kv_handed = handed.reshape(N_EXPERT, N_DECODE, QCAP * BLOCK, N_DECODE, group_width).astype(jnp.bfloat16)
    return (layer_out, kv_handed)
```

```python
import jax
import jax.numpy as jnp
from jax import lax
from jax.sharding import PartitionSpec as P

BLOCK = 16
QCAP = 4


def rms_scale(values, gain):
    return values * lax.rsqrt(jnp.mean(values * values, axis=-1, keepdims=True) + 1e-05) * gain


def unpermute(slot_values, row_index):
    padded = jnp.concatenate(
        [slot_values, jnp.zeros((1, slot_values.shape[1]), jnp.float32)], axis=0
    )
    return padded[row_index]


def hand_over(key_value, req_owner, req_blocks):
    tok_rows, kv_width = key_value.shape
    owner_count = req_owner.shape[1]
    block_count = tok_rows // BLOCK
    owners = req_owner[0]
    counts = req_blocks[0]
    starts = jnp.cumsum(counts) - counts
    owner_index = jnp.arange(owner_count, dtype=jnp.int32)
    slot_index = jnp.arange(QCAP, dtype=jnp.int32)
    block_index = jnp.arange(block_count, dtype=jnp.int32)
    chosen = owners[:, None, None, None] == owner_index[None, :, None, None]
    chosen = chosen & (slot_index[None, None, :, None] < counts[:, None, None, None])
    chosen = chosen & (
        block_index[None, None, None, :]
        == starts[:, None, None, None] + slot_index[None, None, :, None]
    )
    choose = jnp.sum(chosen.astype(jnp.int32), axis=0).astype(jnp.bfloat16)
    kv_blocks = key_value.reshape(block_count, BLOCK, kv_width)
    sending = jnp.einsum(
        "oqb,bjw->qjow", choose, kv_blocks, preferred_element_type=jnp.float32
    ).astype(jnp.bfloat16)
    sending = sending.reshape(QCAP * BLOCK, owner_count, kv_width)
    received = lax.all_to_all(sending, "decode", split_axis=1, concat_axis=1, tiled=True)
    kv_handed = received.reshape(1, 1, QCAP * BLOCK, owner_count, kv_width)
    return kv_handed


def wide_plan(
    resid,
    moe_gain,
    attn_gain,
    gate_score,
    expert_ids,
    w_gate,
    w_up,
    w_down,
    shared_gate,
    shared_up,
    shared_down,
    w_kv,
    req_owner,
    req_blocks,
):
    tok_rows, feature_width = resid.shape
    expert_count = lax.axis_size("expert")
    pair_count = expert_count // 2
    capacity = 2 * tok_rows // pair_count
    group_size = lax.axis_size(("decode", "tensor"))
    piece_width = feature_width // group_size
    feature_start = lax.axis_index(("decode", "tensor")) * piece_width
    moe_in = rms_scale(resid.astype(jnp.float32), moe_gain).astype(jnp.bfloat16)
    routes = expert_ids[:, 0]
    onehot = (routes[:, None] == jnp.arange(pair_count, dtype=jnp.int32)[None, :]).astype(jnp.int32)
    slots = jnp.sum((jnp.cumsum(onehot, axis=0) - 1) * onehot, axis=1)
    kept = slots < capacity
    position = routes * capacity + slots
    row_index = jnp.where(kept, position, pair_count * capacity)
    selector = (
        position[None, :] == jnp.arange(pair_count * capacity, dtype=jnp.int32)[:, None]
    ) & kept[None, :]
    select_bf = selector.astype(jnp.bfloat16)
    packed = jnp.dot(select_bf, moe_in, preferred_element_type=jnp.float32).astype(jnp.bfloat16)
    packed = packed.reshape(pair_count, capacity, feature_width)
    outgoing = jnp.repeat(packed, 2, axis=0)
    incoming = lax.all_to_all(outgoing, "expert", split_axis=0, concat_axis=0, tiled=True)
    flat_in = incoming.reshape(expert_count * capacity, feature_width)
    gate_val = jnp.dot(flat_in, w_gate[0], preferred_element_type=jnp.float32)
    up_val = jnp.dot(flat_in, w_up[0], preferred_element_type=jnp.float32)
    hidden = (jax.nn.silu(gate_val) * up_val).astype(jnp.bfloat16)
    partial_flat = jnp.dot(hidden, w_down[0], preferred_element_type=jnp.float32).astype(
        jnp.bfloat16
    )
    returned = lax.all_to_all(
        partial_flat.reshape(expert_count, capacity, feature_width),
        "expert",
        split_axis=0,
        concat_axis=0,
        tiled=True,
    )
    pair_sums = jnp.sum(
        returned.reshape(pair_count, 2, capacity, feature_width).astype(jnp.float32), axis=1
    )
    routed_full = (
        unpermute(pair_sums.reshape(pair_count * capacity, feature_width), row_index)
        * gate_score[:, None]
    )
    columns = moe_in
    shared_gate_val = jnp.dot(
        columns,
        lax.all_gather(shared_gate, "expert", axis=0, tiled=True),
        preferred_element_type=jnp.float32,
    )
    shared_up_val = jnp.dot(
        columns,
        lax.all_gather(shared_up, "expert", axis=0, tiled=True),
        preferred_element_type=jnp.float32,
    )
    shared_hidden = (jax.nn.silu(shared_gate_val) * shared_up_val).astype(jnp.bfloat16)
    shared_out = jnp.dot(
        shared_hidden,
        lax.all_gather(shared_down, "expert", axis=1, tiled=True),
        preferred_element_type=jnp.float32,
    )
    total_terms = routed_full + shared_out
    summed_share = lax.psum_scatter(
        total_terms.astype(jnp.bfloat16), ("decode", "tensor"), scatter_dimension=1, tiled=True
    ).astype(jnp.float32)
    resid_share = lax.dynamic_slice_in_dim(resid, feature_start, piece_width, 1)
    layer_out = (resid_share.astype(jnp.float32) + summed_share).astype(jnp.bfloat16)
    full_rows = lax.all_gather(layer_out, ("decode", "tensor"), axis=1, tiled=True)
    attn_in = rms_scale(full_rows.astype(jnp.float32), attn_gain).astype(jnp.bfloat16)
    kv_width = w_kv.shape[1]
    columns = attn_in
    key_value = jnp.dot(
        columns,
        lax.all_gather(w_kv, "expert", axis=0, tiled=True),
        preferred_element_type=jnp.float32,
    ).astype(jnp.bfloat16)
    return layer_out, hand_over(key_value, req_owner, req_blocks)


SWAP_CORE = [(0, 1), (1, 0), (2, 3), (3, 2)]
SWAP_CHIP = [(0, 2), (2, 0), (1, 3), (3, 1)]
SWAP_GROUP = [(0, 1), (1, 0)]


def to_shift(values, shift):
    count = lax.axis_size("expert")
    return lax.ppermute(values, "expert", [(i, (i + shift) % count) for i in range(count)])


def place(target, values, row, column):
    return lax.dynamic_update_slice(target, values, (row, column))


def near_plan(
    resid,
    moe_gain,
    attn_gain,
    gate_score,
    expert_ids,
    w_gate,
    w_up,
    w_down,
    shared_gate,
    shared_up,
    shared_down,
    w_kv,
    req_owner,
    req_blocks,
):
    bf16, f32 = jnp.bfloat16, jnp.float32
    rows, width = resid.shape
    expert_count = lax.axis_size("expert")
    pair_count = expert_count // 2
    capacity = 2 * rows // pair_count
    group_size = lax.axis_size("decode")
    piece = width // group_size
    zone = lax.axis_index("expert")
    slot = lax.axis_index("decode")
    group = lax.axis_index("groups")
    near_rows = shared_gate.shape[0]
    half_rows = near_rows // 2
    hidden_piece = shared_gate.shape[1] // expert_count
    half_hidden = hidden_piece // 2
    shifts = (2, 1, 3)

    moe_in = rms_scale(resid.astype(f32), moe_gain).astype(bf16)
    mine = lax.dynamic_slice_in_dim(moe_in, slot * piece, piece, 1)

    routes = expert_ids[:, 0]
    onehot = (routes[:, None] == jnp.arange(pair_count, dtype=jnp.int32)[None, :]).astype(jnp.int32)
    slots = jnp.sum((jnp.cumsum(onehot, axis=0) - 1) * onehot, axis=1)
    kept = slots < capacity
    scale = jnp.where(kept, gate_score, 0.0)
    picks = jnp.where(
        routes[None, :] == jnp.arange(pair_count, dtype=jnp.int32)[:, None], scale[None, :], 0.0
    )
    all_picks = lax.all_gather(picks, "expert", axis=0)
    my_picks = lax.dynamic_index_in_dim(all_picks, zone // 2, 1, keepdims=False)

    arrived = {s: to_shift(mine, s) for s in shifts}
    blocks = {0: moe_in}
    for s in shifts:
        own = arrived[s]
        across = lax.ppermute(own, "decode", SWAP_CHIP)
        beside = lax.ppermute(own, "decode", SWAP_CORE)
        far = lax.ppermute(across, "decode", SWAP_CORE)
        block = jnp.zeros((rows, width), bf16)
        for j, part in ((0, own), (2, across), (1, beside), (3, far)):
            block = place(block, part, 0, (slot ^ j) * piece)
        blocks[s] = block
    tokens = jnp.concatenate([blocks[s] for s in range(expert_count)], axis=0)

    def gate_up(row, count, owner):
        return jnp.concatenate(
            [
                lax.dynamic_slice(w, (row, owner * hidden_piece), (count, hidden_piece))
                for w in (shared_gate, shared_up)
            ],
            axis=1,
        )

    near_weights = jnp.zeros((width, 2 * hidden_piece), bf16)
    near_weights = place(near_weights, gate_up(0, near_rows, zone), zone * near_rows, 0)
    for s in shifts:
        sent = gate_up(group * half_rows, half_rows, (zone + s) % expert_count)
        got = to_shift(sent, s)
        other = lax.ppermute(got, "groups", SWAP_GROUP)
        base = ((zone - s) % expert_count) * near_rows
        near_weights = place(near_weights, got, base + group * half_rows, 0)
        near_weights = place(near_weights, other, base + (1 - group) * half_rows, 0)

    down = jnp.zeros((group_size * hidden_piece, piece), bf16)
    for k in range(group_size):
        target = slot ^ k
        sent = lax.dynamic_slice(
            shared_down, (target * hidden_piece + group * half_hidden, 0), (half_hidden, piece)
        )
        pairs = [
            (z * group_size + d, (d ^ k) * group_size + z)
            for z in range(expert_count)
            for d in range(group_size)
        ]
        got = lax.ppermute(sent, ("expert", "decode"), pairs)
        other = lax.ppermute(got, "groups", SWAP_GROUP)
        base = (zone ^ k) * hidden_piece
        down = place(down, got, base + group * half_hidden, 0)
        down = place(down, other, base + (1 - group) * half_hidden, 0)

    kv_weights = lax.all_gather(w_kv, "expert", axis=0, tiled=True)

    gate_val = jnp.dot(tokens, w_gate[0], preferred_element_type=f32)
    up_val = jnp.dot(tokens, w_up[0], preferred_element_type=f32)
    hidden = (jax.nn.silu(gate_val) * up_val).astype(bf16)
    row_scale = jnp.concatenate(
        [
            lax.dynamic_index_in_dim(my_picks, (zone - s) % expert_count, 0, keepdims=False)
            for s in range(expert_count)
        ]
    )
    partial = (
        jnp.dot(hidden, w_down[0], preferred_element_type=f32) * row_scale[:, None]
    ).astype(bf16)

    def part_of(j):
        return lax.dynamic_slice_in_dim(partial, (slot ^ j) * piece, piece, 1)

    beside = lax.ppermute(jnp.concatenate([part_of(1), part_of(3)], axis=1), "decode", SWAP_CORE)
    keep = part_of(0).astype(f32) + beside[:, :piece].astype(f32)
    pass_on = (part_of(2).astype(f32) + beside[:, piece:].astype(f32)).astype(bf16)
    routed = keep + lax.ppermute(pass_on, "decode", SWAP_CHIP).astype(f32)

    both = jnp.dot(tokens, near_weights, preferred_element_type=f32)
    own = (jax.nn.silu(both[:, :hidden_piece]) * both[:, hidden_piece:]).astype(bf16)
    across = lax.ppermute(own, "decode", SWAP_CHIP)
    beside = lax.ppermute(own, "decode", SWAP_CORE)
    far = lax.ppermute(across, "decode", SWAP_CORE)
    shared_hidden = jnp.zeros((expert_count * rows, group_size * hidden_piece), bf16)
    for j, part in ((0, own), (2, across), (1, beside), (3, far)):
        shared_hidden = place(shared_hidden, part, 0, (slot ^ j) * hidden_piece)
    total = routed + jnp.dot(shared_hidden, down, preferred_element_type=f32)

    summed = total[:rows]
    sending = total.astype(bf16)
    for s in shifts:
        summed = summed + to_shift(sending[s * rows : (s + 1) * rows], -s).astype(f32)
    resid_share = lax.dynamic_slice_in_dim(resid, slot * piece, piece, 1)
    layer_out = (resid_share.astype(f32) + summed).astype(bf16)

    across = lax.ppermute(layer_out, "decode", SWAP_CHIP)
    beside = lax.ppermute(layer_out, "decode", SWAP_CORE)
    far = lax.ppermute(across, "decode", SWAP_CORE)
    full_rows = jnp.zeros((rows, width), bf16)
    for j, part in ((0, layer_out), (2, across), (1, beside), (3, far)):
        full_rows = place(full_rows, part, 0, (slot ^ j) * piece)
    attn_in = rms_scale(full_rows.astype(f32), attn_gain).astype(bf16)
    key_value = jnp.dot(attn_in, kv_weights, preferred_element_type=f32).astype(bf16)
    return layer_out, hand_over(key_value, req_owner, req_blocks)


def on_device(*operands):
    resid = operands[0]
    zones = lax.axis_size("expert")
    holders = lax.axis_size("decode")
    fits = 2 * resid.shape[0] // (zones // 2) >= resid.shape[0]
    square = zones == holders == 4 and lax.axis_size("tensor") == 1
    if fits and square and lax.axis_size("groups") == 2:
        return near_plan(*operands)
    return wide_plan(*operands)


def solution(mesh):
    return jax.shard_map(
        on_device,
        mesh=mesh,
        in_specs=(
            P(("groups", "expert"), None),
            P(),
            P(),
            P(("groups", "expert")),
            P(("groups", "expert"), None),
            P("expert", None, ("decode", "tensor")),
            P("expert", None, ("decode", "tensor")),
            P("expert", ("decode", "tensor"), None),
            P("expert", ("decode", "tensor")),
            P("expert", ("decode", "tensor")),
            P(("decode", "tensor"), "expert"),
            P("expert", ("decode", "tensor")),
            P(("groups", "expert"), None),
            P(("groups", "expert"), None),
        ),
        out_specs=(
            P(("groups", "expert"), ("decode", "tensor")),
            P(("groups", "expert"), "decode", None, None, "tensor"),
        ),
        check_vma=False,
    )
```

```python
import jax
import jax.numpy as jnp
from jax import lax
from jax.experimental import pallas as pl
from jax.experimental.pallas import tpu as pltpu
from jax.sharding import PartitionSpec as P

BLOCK = 16
QCAP = 4


def rms_scale(values, gain):
    return values * lax.rsqrt(jnp.mean(values * values, axis=-1, keepdims=True) + 1e-05) * gain


def unpermute(slot_values, row_index):
    padded = jnp.concatenate(
        [slot_values, jnp.zeros((1, slot_values.shape[1]), jnp.float32)], axis=0
    )
    return padded[row_index]


def hand_over(key_value, req_owner, req_blocks):
    tok_rows, kv_width = key_value.shape
    owner_count = req_owner.shape[1]
    block_count = tok_rows // BLOCK
    owners = req_owner[0]
    counts = req_blocks[0]
    starts = jnp.cumsum(counts) - counts
    owner_index = jnp.arange(owner_count, dtype=jnp.int32)
    slot_index = jnp.arange(QCAP, dtype=jnp.int32)
    block_index = jnp.arange(block_count, dtype=jnp.int32)
    chosen = owners[:, None, None, None] == owner_index[None, :, None, None]
    chosen = chosen & (slot_index[None, None, :, None] < counts[:, None, None, None])
    chosen = chosen & (
        block_index[None, None, None, :]
        == starts[:, None, None, None] + slot_index[None, None, :, None]
    )
    choose = jnp.sum(chosen.astype(jnp.int32), axis=0).astype(jnp.bfloat16)
    kv_blocks = key_value.reshape(block_count, BLOCK, kv_width)
    sending = jnp.einsum(
        "oqb,bjw->qjow", choose, kv_blocks, preferred_element_type=jnp.float32
    ).astype(jnp.bfloat16)
    sending = sending.reshape(QCAP * BLOCK, owner_count, kv_width)
    received = lax.all_to_all(sending, "decode", split_axis=1, concat_axis=1, tiled=True)
    kv_handed = received.reshape(1, 1, QCAP * BLOCK, owner_count, kv_width)
    return kv_handed


def wide_plan(
    resid,
    moe_gain,
    attn_gain,
    gate_score,
    expert_ids,
    w_gate,
    w_up,
    w_down,
    shared_gate,
    shared_up,
    shared_down,
    w_kv,
    req_owner,
    req_blocks,
):
    tok_rows, feature_width = resid.shape
    expert_count = lax.axis_size("expert")
    pair_count = expert_count // 2
    capacity = 2 * tok_rows // pair_count
    group_size = lax.axis_size(("decode", "tensor"))
    piece_width = feature_width // group_size
    feature_start = lax.axis_index(("decode", "tensor")) * piece_width
    moe_in = rms_scale(resid.astype(jnp.float32), moe_gain).astype(jnp.bfloat16)
    routes = expert_ids[:, 0]
    onehot = (routes[:, None] == jnp.arange(pair_count, dtype=jnp.int32)[None, :]).astype(jnp.int32)
    slots = jnp.sum((jnp.cumsum(onehot, axis=0) - 1) * onehot, axis=1)
    kept = slots < capacity
    position = routes * capacity + slots
    row_index = jnp.where(kept, position, pair_count * capacity)
    selector = (
        position[None, :] == jnp.arange(pair_count * capacity, dtype=jnp.int32)[:, None]
    ) & kept[None, :]
    select_bf = selector.astype(jnp.bfloat16)
    packed = jnp.dot(select_bf, moe_in, preferred_element_type=jnp.float32).astype(jnp.bfloat16)
    packed = packed.reshape(pair_count, capacity, feature_width)
    outgoing = jnp.repeat(packed, 2, axis=0)
    incoming = lax.all_to_all(outgoing, "expert", split_axis=0, concat_axis=0, tiled=True)
    flat_in = incoming.reshape(expert_count * capacity, feature_width)
    gate_val = jnp.dot(flat_in, w_gate[0], preferred_element_type=jnp.float32)
    up_val = jnp.dot(flat_in, w_up[0], preferred_element_type=jnp.float32)
    hidden = (jax.nn.silu(gate_val) * up_val).astype(jnp.bfloat16)
    partial_flat = jnp.dot(hidden, w_down[0], preferred_element_type=jnp.float32).astype(
        jnp.bfloat16
    )
    returned = lax.all_to_all(
        partial_flat.reshape(expert_count, capacity, feature_width),
        "expert",
        split_axis=0,
        concat_axis=0,
        tiled=True,
    )
    pair_sums = jnp.sum(
        returned.reshape(pair_count, 2, capacity, feature_width).astype(jnp.float32), axis=1
    )
    routed_full = (
        unpermute(pair_sums.reshape(pair_count * capacity, feature_width), row_index)
        * gate_score[:, None]
    )
    columns = moe_in
    shared_gate_val = jnp.dot(
        columns,
        lax.all_gather(shared_gate, "expert", axis=0, tiled=True),
        preferred_element_type=jnp.float32,
    )
    shared_up_val = jnp.dot(
        columns,
        lax.all_gather(shared_up, "expert", axis=0, tiled=True),
        preferred_element_type=jnp.float32,
    )
    shared_hidden = (jax.nn.silu(shared_gate_val) * shared_up_val).astype(jnp.bfloat16)
    shared_out = jnp.dot(
        shared_hidden,
        lax.all_gather(shared_down, "expert", axis=1, tiled=True),
        preferred_element_type=jnp.float32,
    )
    total_terms = routed_full + shared_out
    summed_share = lax.psum_scatter(
        total_terms.astype(jnp.bfloat16), ("decode", "tensor"), scatter_dimension=1, tiled=True
    ).astype(jnp.float32)
    resid_share = lax.dynamic_slice_in_dim(resid, feature_start, piece_width, 1)
    layer_out = (resid_share.astype(jnp.float32) + summed_share).astype(jnp.bfloat16)
    full_rows = lax.all_gather(layer_out, ("decode", "tensor"), axis=1, tiled=True)
    attn_in = rms_scale(full_rows.astype(jnp.float32), attn_gain).astype(jnp.bfloat16)
    kv_width = w_kv.shape[1]
    columns = attn_in
    key_value = jnp.dot(
        columns,
        lax.all_gather(w_kv, "expert", axis=0, tiled=True),
        preferred_element_type=jnp.float32,
    ).astype(jnp.bfloat16)
    return layer_out, hand_over(key_value, req_owner, req_blocks)


SWAP_CORE = [(0, 1), (1, 0), (2, 3), (3, 2)]
SWAP_CHIP = [(0, 2), (2, 0), (1, 3), (3, 1)]
SWAP_FAR = [(0, 3), (3, 0), (1, 2), (2, 1)]
SWAP_GROUP = [(0, 1), (1, 0)]
SHIFTS = (2, 1, 3)
BF16 = jnp.bfloat16
F32 = jnp.float32
VMEM = pl.BlockSpec(memory_space=pltpu.VMEM)
SMEM = pl.BlockSpec(memory_space=pltpu.SMEM)
ANY = pl.BlockSpec(memory_space=pl.ANY)
META = 16


def call(body, outs, in_specs, scratch=(), flops=0, moved=0, name=None):
    return pl.pallas_call(
        body,
        out_shape=[jax.ShapeDtypeStruct(shape, kind) for shape, kind in outs],
        in_specs=in_specs,
        out_specs=[VMEM] * len(outs),
        scratch_shapes=list(scratch),
        compiler_params=pltpu.CompilerParams(vmem_limit_bytes=48 << 20),
        cost_estimate=pl.CostEstimate(flops=flops, bytes_accessed=moved, transcendentals=0),
        name=name,
    )


def to_shift(values, shift):
    count = lax.axis_size("expert")
    return lax.ppermute(values, "expert", [(i, (i + shift) % count) for i in range(count)])


def after(values, *others):
    return lax.optimization_barrier((values,) + others)[0]


def spread(values):
    across = lax.ppermute(values, "decode", SWAP_CHIP)
    beside = lax.ppermute(values, "decode", SWAP_CORE)
    far = lax.ppermute(across, "decode", SWAP_CORE)
    return values, beside, across, far


def lanes(index, size):
    return pl.ds(pl.multiple_of(index * size, 128), size)


def dot(a, b):
    return jnp.dot(a, b, preferred_element_type=F32)


def norm_kernel(capacity, place, resid, gain, score, ids_row, ids_column, moe_in, message):
    rows, width = resid.shape
    piece = message.shape[1]
    values = resid[...].astype(F32)
    power = jnp.mean(values * values, axis=-1, keepdims=True)
    moe_in[...] = (values * lax.rsqrt(power + 1e-05) * gain[...]).astype(BF16)
    message[:rows, :] = moe_in[:, lanes(place[1], piece)]
    earlier = lax.broadcasted_iota(jnp.int32, (rows, rows), 0) < lax.broadcasted_iota(
        jnp.int32, (rows, rows), 1
    )
    same = (ids_column[...] == ids_row[...]) & earlier
    slots = jnp.sum(same.astype(F32), axis=0, keepdims=True)
    scale = jnp.where(slots < capacity, score[...], 0.0)
    high = scale.astype(BF16)
    rest = scale - high.astype(F32)
    middle = rest.astype(BF16)
    low = (rest - middle.astype(F32)).astype(BF16)
    message[rows:, :] = jnp.zeros((META, piece), BF16)
    for i, part in enumerate((high, middle, low, ids_row[...].astype(F32).astype(BF16))):
        message[rows:, i * rows : (i + 1) * rows] = jnp.broadcast_to(part, (META, rows))


def pack_kernel(place, gate, up, down, own, *rest):
    messages, downs, sem = rest[:3], rest[3:7], rest[7]
    zone, slot, group = place[0], place[1], place[2]
    count = 4
    near = gate.shape[0]
    hidden = gate.shape[1] // count
    half = hidden // 2
    copies = []

    def move(source, target):
        copies.append(pltpu.make_async_copy(source, target, sem.at[len(copies)]))

    for i, shift in enumerate(SHIFTS):
        start = lax.rem(zone + shift, count) * hidden + group * half
        for j, weights in enumerate((gate, up)):
            move(
                weights.at[:, pl.ds(pl.multiple_of(start, 128), half)],
                messages[i].at[:, j * half : (j + 1) * half],
            )
    for k in range(count):
        start = (slot ^ k) * hidden + group * half
        move(down.at[pl.ds(pl.multiple_of(start, 128), half), :], downs[k])
    for part in range(2):
        start = zone * hidden + (group ^ part) * half
        for j, weights in enumerate((gate, up)):
            move(
                weights.at[:, pl.ds(pl.multiple_of(start, 128), half)],
                own.at[:, (2 * part + j) * half : (2 * part + j + 1) * half],
            )
    for copy in copies:
        copy.start()
    for copy in copies:
        copy.wait()


def routed_kernel(place, moe_in, own, *rest):
    pieces = rest[:12]
    gate, up, down, tokens, send, keep, hidden = rest[12:]
    zone, slot = place[0], place[1]
    rows = moe_in.shape[0]
    piece = own.shape[1]
    tokens[:rows, :] = moe_in[...]
    for i, shift in enumerate(SHIFTS):
        for j in range(4):
            tokens[shift * rows : (shift + 1) * rows, lanes(slot ^ j, piece)] = pieces[4 * i + j][
                :rows, :
            ]
    width = hidden.shape[1]
    step = 256
    for n in range(width // step):
        cols = slice(n * step, (n + 1) * step)
        gate_val = dot(tokens[...], gate[0, :, cols])
        up_val = dot(tokens[...], up[0, :, cols])
        hidden[:, cols] = (gate_val / (1.0 + jnp.exp(-gate_val)) * up_val).astype(BF16)
    diagonal = lax.broadcasted_iota(jnp.int32, (rows, rows), 0) == lax.broadcasted_iota(
        jnp.int32, (rows, rows), 1
    )
    mine = (zone // 2).astype(F32)
    scales = []
    for shift in range(4):
        source = own if shift == 0 else pieces[4 * SHIFTS.index(shift)]
        info = source[rows : rows + META, :].astype(F32)[:1]
        value = info[:, :rows] + info[:, rows : 2 * rows] + info[:, 2 * rows : 3 * rows]
        value = jnp.where(info[:, 3 * rows : 4 * rows] == mine, value, 0.0)
        scales.append(
            jnp.sum(jnp.where(diagonal, value, 0.0), axis=1, keepdims=True)
        )
    scale = jnp.concatenate(scales, axis=0)
    for target, first, parts in ((send, 1, (1, 3)), (keep, 0, (0, 2))):
        for i, j in enumerate(parts):
            value = dot(hidden[...], down[0, :, lanes(slot ^ j, piece)]) * scale
            target[:, i * piece : (i + 1) * piece] = value.astype(BF16)


def gate_up_kernel(place, tokens, own, *rest):
    got, other, hidden = rest[:3], rest[3:6], rest[6]
    zone, group = place[0], place[2]
    near = own.shape[0]
    width = own.shape[1] // 2
    half = width // 2
    for part, pieces in ((0, got), (1, other)):
        both = dot(tokens[:, lanes(zone, near)], own[:, part * width : (part + 1) * width])
        for i, shift in enumerate(SHIFTS):
            source = lax.rem(zone - shift + 4, 4)
            both = both + dot(tokens[:, lanes(source, near)], pieces[i][...])
        gate_val, up_val = both[:, :half], both[:, half:]
        hidden[:, lanes(group ^ part, half)] = (
            gate_val / (1.0 + jnp.exp(-gate_val)) * up_val
        ).astype(BF16)


def down_kernel(place, keep, crossed, *rest):
    pieces, got, other = rest[:4], rest[4:8], rest[8:12]
    own, sends, hidden, weights = rest[12], rest[13:16], rest[16], rest[17]
    zone, slot, group = place[0], place[1], place[2]
    width = pieces[0].shape[1]
    half = width // 2
    rows = own.shape[0]
    for j in range(4):
        hidden[:, lanes(slot ^ j, width)] = pieces[j][...]
    for k in range(4):
        base = (zone ^ k) * width
        weights[pl.ds(pl.multiple_of(base + group * half, 128), half), :] = got[k][...]
        weights[pl.ds(pl.multiple_of(base + (1 - group) * half, 128), half), :] = other[k][...]
    for block in range(4):
        span = slice(block * rows, (block + 1) * rows)
        value = keep[span, :].astype(F32) + crossed[span, :].astype(F32)
        value = value + dot(hidden[span, :], weights[...])
        if block == 0:
            own[...] = value
        else:
            sends[SHIFTS.index(block)][...] = value.astype(BF16)


def layer_kernel(place, resid, own, a, b, c, out):
    piece = own.shape[1]
    value = own[...] + a[...].astype(F32) + b[...].astype(F32) + c[...].astype(F32)
    value = value + resid[:, lanes(place[1], piece)].astype(F32)
    out[...] = value.astype(BF16)


def kv_kernel(place, owner, blocks, gain, a, b, c, d, mine, theirs, *rest):
    outs, full, key_value = rest[:4], rest[4], rest[5]
    slot, group = place[1], place[2]
    piece = a.shape[1]
    for j, part in enumerate((a, b, c, d)):
        full[:, lanes(slot ^ j, piece)] = part[...].astype(F32)
    values = full[...]
    power = jnp.mean(values * values, axis=-1, keepdims=True)
    attn_in = (values * lax.rsqrt(power + 1e-05) * gain[...]).astype(BF16)
    half = mine.shape[1]
    for part, weights in ((0, mine), (1, theirs)):
        key_value[:, lanes(group ^ part, half)] = dot(attn_in, weights[...]).astype(BF16)
    held = full.shape[0] // BLOCK
    width = key_value.shape[1]
    for j in range(4):
        start, amount, begin = 0, 0, 0
        for r in range(4):
            here = owner[0, r] == (slot ^ j)
            amount = jnp.where(here, blocks[0, r], amount)
            begin = jnp.where(here, start, begin)
            start = start + blocks[0, r]
        for q in range(QCAP):
            row = jnp.clip(begin + q, 0, held - 1) * BLOCK
            chosen = key_value[pl.ds(pl.multiple_of(row, BLOCK), BLOCK), :]
            outs[j][q * BLOCK : (q + 1) * BLOCK, :] = jnp.where(
                q < amount, chosen, jnp.zeros((BLOCK, width), BF16)
            )


def hand_kernel(place, a, b, c, d, out):
    parts = [part[...].astype(F32) for part in (a, b, c, d)]
    ordered = []
    for source in range(4):
        j = place[1] ^ source
        value = jnp.where(j == 0, parts[0], parts[1])
        ordered.append(jnp.where(j < 2, value, jnp.where(j == 2, parts[2], parts[3])))
    out[...] = jnp.stack(ordered, axis=1).astype(BF16)


def near_plan(
    resid,
    moe_gain,
    attn_gain,
    gate_score,
    expert_ids,
    w_gate,
    w_up,
    w_down,
    shared_gate,
    shared_up,
    shared_down,
    w_kv,
    req_owner,
    req_blocks,
):
    rows, width = resid.shape
    zones = lax.axis_size("expert")
    slots = lax.axis_size("decode")
    capacity = 2 * rows // (zones // 2)
    piece = width // slots
    near = shared_gate.shape[0]
    hidden = shared_gate.shape[1] // zones
    half = hidden // 2
    total_rows = zones * rows
    routed_width = w_gate.shape[2]
    kv_width = w_kv.shape[1]
    group = lax.axis_index("groups")
    place = jnp.stack(
        [lax.axis_index("expert"), lax.axis_index("decode"), group]
    ).astype(jnp.int32)

    moe_in, message = call(
        lambda *refs: norm_kernel(capacity, *refs),
        [((rows, width), BF16), ((rows + META, piece), BF16)],
        [SMEM] + [VMEM] * 5,
        name="norm",
    )(
        place,
        resid,
        moe_gain.reshape(1, width),
        gate_score.reshape(1, rows),
        expert_ids.reshape(1, rows),
        expert_ids,
    )
    packed = call(
        pack_kernel,
        [((near, 2 * hidden), BF16)] + [((near, hidden), BF16)] * 3 + [((half, piece), BF16)] * 4,
        [SMEM] + [ANY] * 3,
        [pltpu.SemaphoreType.DMA((14,))],
        name="pack",
    )(place, shared_gate, shared_up, shared_down)
    own_weights, weight_messages, down_messages = packed[0], packed[1:4], packed[4:8]

    arrived = [to_shift(message, s) for s in SHIFTS]
    pieces = [part for values in arrived for part in spread(values)]

    got = [to_shift(values, s) for values, s in zip(weight_messages, SHIFTS)]
    other = [lax.ppermute(values, "groups", SWAP_GROUP) for values in got]

    down_got, down_other = [], []
    down_messages = lax.optimization_barrier(tuple(down_messages) + (got[0],))[:4]
    for k in range(slots):
        pairs = [
            (z * slots + d, (d ^ k) * slots + z) for z in range(zones) for d in range(slots)
        ]
        values = lax.ppermute(down_messages[k], ("expert", "decode"), pairs)
        down_got.append(values)
        down_other.append(lax.ppermute(values, "groups", SWAP_GROUP))

    kv_half = lax.dynamic_slice_in_dim(w_kv, group * (kv_width // 2), kv_width // 2, 1)
    kv_half = after(kv_half, arrived[0])
    kv_mine = lax.all_gather(kv_half, "expert", axis=0, tiled=True)
    kv_theirs = lax.ppermute(kv_mine, "groups", SWAP_GROUP)

    tokens, send, keep = call(
        routed_kernel,
        [((total_rows, width), BF16), ((total_rows, 2 * piece), BF16), ((total_rows, 2 * piece), BF16)],
        [SMEM] + [VMEM] * 17,
        [pltpu.VMEM((total_rows, routed_width), BF16)],
        flops=6 * total_rows * width * routed_width,
        moved=14 << 20,
        name="routed",
    )(place, moe_in, message, *pieces, w_gate, w_up, w_down)
    beside = lax.ppermute(send, "decode", SWAP_CORE)
    keep_sum = keep.astype(F32) + beside.astype(F32)
    crossed = lax.ppermute(keep_sum[:, piece:].astype(BF16), "decode", SWAP_CHIP)

    (shared_hidden,) = call(
        gate_up_kernel,
        [((total_rows, hidden), BF16)],
        [SMEM] + [VMEM] * 8,
        flops=4 * total_rows * width * hidden,
        moved=6 << 20,
        name="gate_up",
    )(place, tokens, own_weights, *got, *other)
    hidden_pieces = spread(shared_hidden)
    summed = call(
        down_kernel,
        [((rows, piece), F32)] + [((rows, piece), BF16)] * 3,
        [SMEM] + [VMEM] * 14,
        [
            pltpu.VMEM((total_rows, slots * hidden), BF16),
            pltpu.VMEM((slots * hidden, piece), BF16),
        ],
        flops=2 * total_rows * slots * hidden * piece,
        moved=5 << 20,
        name="down",
    )(place, keep_sum[:, :piece], crossed, *hidden_pieces, *down_got, *down_other)
    returned = [to_shift(values, -s) for values, s in zip(summed[1:], SHIFTS)]
    (layer_out,) = call(
        layer_kernel, [((rows, piece), BF16)], [SMEM] + [VMEM] * 5, name="layer"
    )(place, resid, summed[0], *returned)

    handed = call(
        kv_kernel,
        [((QCAP * BLOCK, kv_width), BF16)] * 4,
        [SMEM] * 3 + [VMEM] * 7,
        [pltpu.VMEM((rows, width), F32), pltpu.VMEM((rows, kv_width), BF16)],
        flops=2 * rows * width * kv_width,
        moved=4 << 20,
        name="kv",
    )(
        place,
        req_owner,
        req_blocks,
        attn_gain.reshape(1, width),
        *spread(layer_out),
        kv_mine,
        kv_theirs,
    )
    received = [handed[0]] + [
        lax.ppermute(values, "decode", pairs)
        for values, pairs in zip(handed[1:], (SWAP_CORE, SWAP_CHIP, SWAP_FAR))
    ]
    (kv_handed,) = call(
        hand_kernel,
        [((QCAP * BLOCK, slots, kv_width), BF16)],
        [SMEM] + [VMEM] * 4,
        name="hand",
    )(place, *received)
    return layer_out, kv_handed[None, None]


def on_device(*operands):
    resid = operands[0]
    zones = lax.axis_size("expert")
    holders = lax.axis_size("decode")
    fits = 2 * resid.shape[0] // (zones // 2) >= resid.shape[0]
    square = zones == holders == 4 and lax.axis_size("tensor") == 1
    if fits and square and lax.axis_size("groups") == 2:
        return near_plan(*operands)
    return wide_plan(*operands)


def solution(mesh):
    return jax.shard_map(
        on_device,
        mesh=mesh,
        in_specs=(
            P(("groups", "expert"), None),
            P(),
            P(),
            P(("groups", "expert")),
            P(("groups", "expert"), None),
            P("expert", None, ("decode", "tensor")),
            P("expert", None, ("decode", "tensor")),
            P("expert", ("decode", "tensor"), None),
            P("expert", ("decode", "tensor")),
            P("expert", ("decode", "tensor")),
            P(("decode", "tensor"), "expert"),
            P("expert", ("decode", "tensor")),
            P(("groups", "expert"), None),
            P(("groups", "expert"), None),
        ),
        out_specs=(
            P(("groups", "expert"), ("decode", "tensor")),
            P(("groups", "expert"), "decode", None, None, "tensor"),
        ),
        check_vma=False,
    )
```

```python
import jax
import jax.numpy as jnp
from jax import lax
from jax.experimental import pallas as pl
from jax.experimental.pallas import tpu as pltpu
from jax.sharding import PartitionSpec as P

BLOCK = 16
QCAP = 4


def rms_scale(values, gain):
    return values * lax.rsqrt(jnp.mean(values * values, axis=-1, keepdims=True) + 1e-05) * gain


def unpermute(slot_values, row_index):
    padded = jnp.concatenate(
        [slot_values, jnp.zeros((1, slot_values.shape[1]), jnp.float32)], axis=0
    )
    return padded[row_index]


def hand_over(key_value, req_owner, req_blocks):
    tok_rows, kv_width = key_value.shape
    owner_count = req_owner.shape[1]
    block_count = tok_rows // BLOCK
    owners = req_owner[0]
    counts = req_blocks[0]
    starts = jnp.cumsum(counts) - counts
    owner_index = jnp.arange(owner_count, dtype=jnp.int32)
    slot_index = jnp.arange(QCAP, dtype=jnp.int32)
    block_index = jnp.arange(block_count, dtype=jnp.int32)
    chosen = owners[:, None, None, None] == owner_index[None, :, None, None]
    chosen = chosen & (slot_index[None, None, :, None] < counts[:, None, None, None])
    chosen = chosen & (
        block_index[None, None, None, :]
        == starts[:, None, None, None] + slot_index[None, None, :, None]
    )
    choose = jnp.sum(chosen.astype(jnp.int32), axis=0).astype(jnp.bfloat16)
    kv_blocks = key_value.reshape(block_count, BLOCK, kv_width)
    sending = jnp.einsum(
        "oqb,bjw->qjow", choose, kv_blocks, preferred_element_type=jnp.float32
    ).astype(jnp.bfloat16)
    sending = sending.reshape(QCAP * BLOCK, owner_count, kv_width)
    received = lax.all_to_all(sending, "decode", split_axis=1, concat_axis=1, tiled=True)
    kv_handed = received.reshape(1, 1, QCAP * BLOCK, owner_count, kv_width)
    return kv_handed


def wide_plan(
    resid,
    moe_gain,
    attn_gain,
    gate_score,
    expert_ids,
    w_gate,
    w_up,
    w_down,
    shared_gate,
    shared_up,
    shared_down,
    w_kv,
    req_owner,
    req_blocks,
):
    tok_rows, feature_width = resid.shape
    expert_count = lax.axis_size("expert")
    pair_count = expert_count // 2
    capacity = 2 * tok_rows // pair_count
    group_size = lax.axis_size(("decode", "tensor"))
    piece_width = feature_width // group_size
    feature_start = lax.axis_index(("decode", "tensor")) * piece_width
    moe_in = rms_scale(resid.astype(jnp.float32), moe_gain).astype(jnp.bfloat16)
    routes = expert_ids[:, 0]
    onehot = (routes[:, None] == jnp.arange(pair_count, dtype=jnp.int32)[None, :]).astype(jnp.int32)
    slots = jnp.sum((jnp.cumsum(onehot, axis=0) - 1) * onehot, axis=1)
    kept = slots < capacity
    position = routes * capacity + slots
    row_index = jnp.where(kept, position, pair_count * capacity)
    selector = (
        position[None, :] == jnp.arange(pair_count * capacity, dtype=jnp.int32)[:, None]
    ) & kept[None, :]
    select_bf = selector.astype(jnp.bfloat16)
    packed = jnp.dot(select_bf, moe_in, preferred_element_type=jnp.float32).astype(jnp.bfloat16)
    packed = packed.reshape(pair_count, capacity, feature_width)
    outgoing = jnp.repeat(packed, 2, axis=0)
    incoming = lax.all_to_all(outgoing, "expert", split_axis=0, concat_axis=0, tiled=True)
    flat_in = incoming.reshape(expert_count * capacity, feature_width)
    gate_val = jnp.dot(flat_in, w_gate[0], preferred_element_type=jnp.float32)
    up_val = jnp.dot(flat_in, w_up[0], preferred_element_type=jnp.float32)
    hidden = (jax.nn.silu(gate_val) * up_val).astype(jnp.bfloat16)
    partial_flat = jnp.dot(hidden, w_down[0], preferred_element_type=jnp.float32).astype(
        jnp.bfloat16
    )
    returned = lax.all_to_all(
        partial_flat.reshape(expert_count, capacity, feature_width),
        "expert",
        split_axis=0,
        concat_axis=0,
        tiled=True,
    )
    pair_sums = jnp.sum(
        returned.reshape(pair_count, 2, capacity, feature_width).astype(jnp.float32), axis=1
    )
    routed_full = (
        unpermute(pair_sums.reshape(pair_count * capacity, feature_width), row_index)
        * gate_score[:, None]
    )
    columns = moe_in
    shared_gate_val = jnp.dot(
        columns,
        lax.all_gather(shared_gate, "expert", axis=0, tiled=True),
        preferred_element_type=jnp.float32,
    )
    shared_up_val = jnp.dot(
        columns,
        lax.all_gather(shared_up, "expert", axis=0, tiled=True),
        preferred_element_type=jnp.float32,
    )
    shared_hidden = (jax.nn.silu(shared_gate_val) * shared_up_val).astype(jnp.bfloat16)
    shared_out = jnp.dot(
        shared_hidden,
        lax.all_gather(shared_down, "expert", axis=1, tiled=True),
        preferred_element_type=jnp.float32,
    )
    total_terms = routed_full + shared_out
    summed_share = lax.psum_scatter(
        total_terms.astype(jnp.bfloat16), ("decode", "tensor"), scatter_dimension=1, tiled=True
    ).astype(jnp.float32)
    resid_share = lax.dynamic_slice_in_dim(resid, feature_start, piece_width, 1)
    layer_out = (resid_share.astype(jnp.float32) + summed_share).astype(jnp.bfloat16)
    full_rows = lax.all_gather(layer_out, ("decode", "tensor"), axis=1, tiled=True)
    attn_in = rms_scale(full_rows.astype(jnp.float32), attn_gain).astype(jnp.bfloat16)
    kv_width = w_kv.shape[1]
    columns = attn_in
    key_value = jnp.dot(
        columns,
        lax.all_gather(w_kv, "expert", axis=0, tiled=True),
        preferred_element_type=jnp.float32,
    ).astype(jnp.bfloat16)
    return layer_out, hand_over(key_value, req_owner, req_blocks)


SWAP_CORE = [(0, 1), (1, 0), (2, 3), (3, 2)]
SWAP_CHIP = [(0, 2), (2, 0), (1, 3), (3, 1)]
SWAP_FAR = [(0, 3), (3, 0), (1, 2), (2, 1)]
SWAP_GROUP = [(0, 1), (1, 0)]
SHIFTS = (2, 1, 3)
BF16 = jnp.bfloat16
F32 = jnp.float32
VMEM = pl.BlockSpec(memory_space=pltpu.VMEM)
SMEM = pl.BlockSpec(memory_space=pltpu.SMEM)
ANY = pl.BlockSpec(memory_space=pl.ANY)
META = 16


def call(body, outs, in_specs, scratch=(), flops=0, moved=0, name=None, vmem=8):
    return pl.pallas_call(
        body,
        out_shape=[jax.ShapeDtypeStruct(shape, kind) for shape, kind in outs],
        in_specs=in_specs,
        out_specs=[VMEM] * len(outs),
        scratch_shapes=list(scratch),
        compiler_params=pltpu.CompilerParams(vmem_limit_bytes=vmem << 20),
        cost_estimate=pl.CostEstimate(flops=flops, bytes_accessed=moved, transcendentals=0),
        name=name,
    )


def to_shift(values, shift):
    count = lax.axis_size("expert")
    return lax.ppermute(values, "expert", [(i, (i + shift) % count) for i in range(count)])


def after(values, *others):
    return lax.optimization_barrier((values,) + others)[0]


def spread(values):
    across = lax.ppermute(values, "decode", SWAP_CHIP)
    beside = lax.ppermute(values, "decode", SWAP_CORE)
    far = lax.ppermute(across, "decode", SWAP_CORE)
    return values, beside, across, far


def lanes(index, size):
    return pl.ds(pl.multiple_of(index * size, 128), size)


def dot(a, b):
    return jnp.dot(a, b, preferred_element_type=F32)


def first_kernel(
    capacity, place, resid, gain, score, ids, gate, up, down, kv, moe_in, message, share, own, *rest
):
    messages, downs, kv_half, sem = rest[:3], rest[3:7], rest[7], rest[8]
    zone, slot, group = place[0], place[1], place[2]
    count = 4
    hidden = gate.shape[1] // count
    half = hidden // 2
    copies = []

    def move(source, target):
        copies.append(pltpu.make_async_copy(source, target, sem.at[len(copies)]))

    for i, shift in enumerate(SHIFTS):
        start = lax.rem(zone + shift, count) * hidden + group * half
        for j, weights in enumerate((gate, up)):
            move(
                weights.at[:, pl.ds(pl.multiple_of(start, 128), half)],
                messages[i].at[:, j * half : (j + 1) * half],
            )
    for k in range(count):
        start = (slot ^ k) * hidden + group * half
        move(down.at[pl.ds(pl.multiple_of(start, 128), half), :], downs[k])
    start = group * kv_half.shape[1]
    move(kv.at[:, pl.ds(pl.multiple_of(start, 128), kv_half.shape[1])], kv_half)
    for part in range(2):
        start = zone * hidden + (group ^ part) * half
        for j, weights in enumerate((gate, up)):
            move(
                weights.at[:, pl.ds(pl.multiple_of(start, 128), half)],
                own.at[:, (2 * part + j) * half : (2 * part + j + 1) * half],
            )
    for copy in copies:
        copy.start()

    rows, width = resid.shape
    piece = message.shape[1]
    values = resid[...].astype(F32)
    power = jnp.mean(values * values, axis=-1, keepdims=True)
    moe_in[...] = (values * lax.rsqrt(power + 1e-05) * gain[...]).astype(BF16)
    message[:rows, :] = moe_in[:, lanes(slot, piece)]
    share[...] = resid[:, lanes(slot, piece)]
    first = lax.broadcasted_iota(jnp.int32, (rows, rows), 0)
    second = lax.broadcasted_iota(jnp.int32, (rows, rows), 1)
    across = jnp.broadcast_to(ids[...].astype(F32), (rows, rows))
    along = jnp.sum(jnp.where(first == second, across, 0.0), axis=1, keepdims=True)
    same = (along == across) & (first < second)
    slots = jnp.sum(jnp.where(same, 1.0, 0.0), axis=0, keepdims=True)
    scale = jnp.where(slots < capacity, score[...], 0.0)
    high = scale.astype(BF16)
    rest = scale - high.astype(F32)
    middle = rest.astype(BF16)
    low = (rest - middle.astype(F32)).astype(BF16)
    message[rows:, :] = jnp.zeros((META, piece), BF16)
    for i, part in enumerate((high, middle, low, ids[...].astype(F32).astype(BF16))):
        message[rows:, i * rows : (i + 1) * rows] = jnp.broadcast_to(part, (META, rows))
    for copy in copies:
        copy.wait()


def silu(values):
    return values / (1.0 + jnp.exp(-values))


def routed_up_kernel(place, moe_in, *rest):
    pieces = rest[:12]
    gate, up, tokens, hidden = rest[12:]
    slot = place[1]
    rows = moe_in.shape[0]
    piece = pieces[0].shape[1]
    tokens[:rows, :] = moe_in[...]
    for i, shift in enumerate(SHIFTS):
        for j in range(4):
            tokens[shift * rows : (shift + 1) * rows, lanes(slot ^ j, piece)] = pieces[4 * i + j][
                :rows, :
            ]
    width = hidden.shape[1]
    step = 256
    for n in range(width // step):
        cols = slice(n * step, (n + 1) * step)
        gate_val = dot(tokens[...], gate[0, :, cols])
        up_val = dot(tokens[...], up[0, :, cols])
        hidden[:, cols] = (silu(gate_val) * up_val).astype(BF16)


def routed_down_kernel(place, hidden, *rest):
    messages, down, send, keep = rest[:4], rest[4], rest[5], rest[6]
    zone, slot = place[0], place[1]
    rows = messages[0].shape[0] - META
    piece = messages[0].shape[1]
    diagonal = lax.broadcasted_iota(jnp.int32, (rows, rows), 0) == lax.broadcasted_iota(
        jnp.int32, (rows, rows), 1
    )
    mine = (zone // 2).astype(F32)
    scales = []
    for source in messages:
        info = source[rows : rows + META, :].astype(F32)[:1]
        value = info[:, :rows] + info[:, rows : 2 * rows] + info[:, 2 * rows : 3 * rows]
        value = jnp.where(info[:, 3 * rows : 4 * rows] == mine, value, 0.0)
        scales.append(jnp.sum(jnp.where(diagonal, value, 0.0), axis=1, keepdims=True))
    scale = jnp.concatenate(scales, axis=0)
    for target, parts in ((send, (1, 3)), (keep, (0, 2))):
        for i, j in enumerate(parts):
            value = dot(hidden[...], down[0, :, lanes(slot ^ j, piece)]) * scale
            target[:, i * piece : (i + 1) * piece] = value.astype(BF16)


def gate_up_half(place, tokens, own, pieces, part):
    zone = place[0]
    near = own.shape[0]
    width = own.shape[1] // 2
    half = width // 2
    both = dot(tokens[:, lanes(zone, near)], own[:, part * width : (part + 1) * width])
    for i, shift in enumerate(SHIFTS):
        source = lax.rem(zone - shift + 4, 4)
        both = both + dot(tokens[:, lanes(source, near)], pieces[i][...])
    return (silu(both[:, :half]) * both[:, half:]).astype(BF16)


def gate_up_first_kernel(place, tokens, own, a, b, c, hidden):
    hidden[...] = gate_up_half(place, tokens, own, (a, b, c), 0)


def gate_up_second_kernel(place, tokens, own, first, a, b, c, hidden):
    half = first.shape[1]
    hidden[:, lanes(place[2], half)] = first[...]
    hidden[:, lanes(1 - place[2], half)] = gate_up_half(place, tokens, own, (a, b, c), 1)


def down_kernel(place, keep, crossed, *rest):
    pieces, got, other = rest[:4], rest[4:8], rest[8:12]
    own, sends, hidden, weights = rest[12], rest[13:16], rest[16], rest[17]
    zone, slot, group = place[0], place[1], place[2]
    width = pieces[0].shape[1]
    half = width // 2
    rows = own.shape[0]
    for j in range(4):
        hidden[:, lanes(slot ^ j, width)] = pieces[j][...]
    for k in range(4):
        base = (zone ^ k) * width
        weights[pl.ds(pl.multiple_of(base + group * half, 128), half), :] = got[k][...]
        weights[pl.ds(pl.multiple_of(base + (1 - group) * half, 128), half), :] = other[k][...]
    for block in range(4):
        span = slice(block * rows, (block + 1) * rows)
        value = keep[span, :].astype(F32) + crossed[span, :].astype(F32)
        value = value + dot(hidden[span, :], weights[...])
        if block == 0:
            own[...] = value
        else:
            sends[SHIFTS.index(block)][...] = value.astype(BF16)


def layer_kernel(resid, own, a, b, c, out):
    value = own[...] + a[...].astype(F32) + b[...].astype(F32) + c[...].astype(F32)
    value = value + resid[...].astype(F32)
    out[...] = value.astype(BF16)


def kv_kernel(place, owner, blocks, gain, a, b, c, d, own, *rest):
    got, other, outs = rest[:3], rest[3:6], rest[6:10]
    full, key_value, ready = rest[10:]
    zone, slot, group = place[0], place[1], place[2]
    piece = a.shape[1]
    for j, part in enumerate((a, b, c, d)):
        full[:, lanes(slot ^ j, piece)] = part[...].astype(F32)
    values = full[...]
    power = jnp.mean(values * values, axis=-1, keepdims=True)
    ready[...] = (values * lax.rsqrt(power + 1e-05) * gain[...]).astype(BF16)
    near = own.shape[0]
    half = own.shape[1] // 2
    for part, pieces in ((0, got), (1, other)):
        value = dot(ready[:, lanes(zone, near)], own[:, lanes(group ^ part, half)])
        for i, shift in enumerate(SHIFTS):
            source = lax.rem(zone - shift + 4, 4)
            value = value + dot(ready[:, lanes(source, near)], pieces[i][...])
        key_value[:, lanes(group ^ part, half)] = value.astype(BF16)
    held = full.shape[0] // BLOCK
    width = key_value.shape[1]
    for j in range(4):
        start, amount, begin = 0, 0, 0
        for r in range(4):
            here = owner[0, r] == (slot ^ j)
            amount = jnp.where(here, blocks[0, r], amount)
            begin = jnp.where(here, start, begin)
            start = start + blocks[0, r]
        for q in range(QCAP):
            row = jnp.clip(begin + q, 0, held - 1) * BLOCK
            chosen = key_value[pl.ds(pl.multiple_of(row, BLOCK), BLOCK), :]
            outs[j][q * BLOCK : (q + 1) * BLOCK, :] = jnp.where(
                q < amount, chosen, jnp.zeros((BLOCK, width), BF16)
            )


def hand_kernel(place, a, b, c, d, out):
    parts = [part[...].astype(F32) for part in (a, b, c, d)]
    ordered = []
    for source in range(4):
        j = place[1] ^ source
        value = jnp.where(j == 0, parts[0], parts[1])
        ordered.append(jnp.where(j < 2, value, jnp.where(j == 2, parts[2], parts[3])))
    out[...] = jnp.stack(ordered, axis=1).astype(BF16)


def near_plan(
    resid,
    moe_gain,
    attn_gain,
    gate_score,
    expert_ids,
    w_gate,
    w_up,
    w_down,
    shared_gate,
    shared_up,
    shared_down,
    w_kv,
    req_owner,
    req_blocks,
):
    rows, width = resid.shape
    zones = lax.axis_size("expert")
    slots = lax.axis_size("decode")
    capacity = 2 * rows // (zones // 2)
    piece = width // slots
    near = shared_gate.shape[0]
    hidden = shared_gate.shape[1] // zones
    half = hidden // 2
    total_rows = zones * rows
    routed_width = w_gate.shape[2]
    kv_width = w_kv.shape[1]
    group = lax.axis_index("groups")
    place = jnp.stack(
        [lax.axis_index("expert"), lax.axis_index("decode"), group]
    ).astype(jnp.int32)

    first = call(
        lambda *refs: first_kernel(capacity, *refs),
        [
            ((rows, width), BF16),
            ((rows + META, piece), BF16),
            ((rows, piece), BF16),
            ((near, 2 * hidden), BF16),
        ]
        + [((near, hidden), BF16)] * 3
        + [((half, piece), BF16)] * 4
        + [((near, kv_width // 2), BF16)],
        [SMEM] + [VMEM] * 4 + [ANY] * 4,
        [pltpu.SemaphoreType.DMA((15,))],
        moved=6 << 20,
        name="first",
        vmem=58,
    )(
        place,
        resid,
        moe_gain.reshape(1, width),
        gate_score.reshape(1, rows),
        expert_ids.reshape(1, rows),
        shared_gate,
        shared_up,
        shared_down,
        w_kv,
    )
    moe_in, message, resid_share, own_weights = first[:4]
    weight_messages, down_messages, kv_half = first[4:7], first[7:11], first[11]

    arrived = [to_shift(message, s) for s in SHIFTS]
    pieces = [part for values in arrived for part in spread(values)]

    got = [to_shift(values, s) for values, s in zip(weight_messages, SHIFTS)]
    other = [lax.ppermute(values, "groups", SWAP_GROUP) for values in got]

    down_got, down_other = [], []
    down_messages = lax.optimization_barrier(tuple(down_messages) + tuple(got) + (other[0],))[:4]
    for k in range(slots):
        pairs = [
            (z * slots + d, (d ^ k) * slots + z) for z in range(zones) for d in range(slots)
        ]
        values = lax.ppermute(down_messages[k], ("expert", "decode"), pairs)
        down_got.append(values)
        down_other.append(lax.ppermute(values, "groups", SWAP_GROUP))

    kv_half = after(kv_half, *got)
    kv_got = [to_shift(kv_half, s) for s in SHIFTS]
    kv_other = [lax.ppermute(values, "groups", SWAP_GROUP) for values in kv_got]

    tokens, routed_hidden = call(
        routed_up_kernel,
        [((total_rows, width), BF16), ((total_rows, routed_width), BF16)],
        [SMEM] + [VMEM] * 15,
        flops=4 * total_rows * width * routed_width,
        moved=10 << 20,
        name="routed_up",
        vmem=22,
    )(after(place, got[0]), moe_in, *pieces, w_gate, w_up)
    send, keep = call(
        routed_down_kernel,
        [((total_rows, 2 * piece), BF16), ((total_rows, 2 * piece), BF16)],
        [SMEM] + [VMEM] * 6,
        flops=2 * total_rows * width * routed_width,
        moved=6 << 20,
        name="routed_down",
        vmem=16,
    )(
        after(place, other[0], *got),
        routed_hidden,
        message,
        *[arrived[SHIFTS.index(s)] for s in range(1, zones)],
        w_down,
    )
    beside = lax.ppermute(send, "decode", SWAP_CORE)
    keep_sum = keep.astype(F32) + beside.astype(F32)
    crossed = lax.ppermute(keep_sum[:, piece:].astype(BF16), "decode", SWAP_CHIP)

    (first_half,) = call(
        gate_up_first_kernel,
        [((total_rows, half), BF16)],
        [SMEM] + [VMEM] * 5,
        flops=2 * total_rows * width * hidden,
        moved=4 << 20,
        name="gate_up_first",
        vmem=12,
    )(place, tokens, own_weights, *got)
    (shared_hidden,) = call(
        gate_up_second_kernel,
        [((total_rows, hidden), BF16)],
        [SMEM] + [VMEM] * 6,
        flops=2 * total_rows * width * hidden,
        moved=4 << 20,
        name="gate_up_second",
        vmem=12,
    )(after(place, kv_got[0]), tokens, own_weights, first_half, *other)
    hidden_pieces = spread(shared_hidden)
    summed = call(
        down_kernel,
        [((rows, piece), F32)] + [((rows, piece), BF16)] * 3,
        [SMEM] + [VMEM] * 14,
        [
            pltpu.VMEM((total_rows, slots * hidden), BF16),
            pltpu.VMEM((slots * hidden, piece), BF16),
        ],
        name="down",
        vmem=14,
    )(after(place, *kv_got), keep_sum[:, :piece], crossed, *hidden_pieces, *down_got, *down_other)
    returned = [to_shift(values, -s) for values, s in zip(summed[1:], SHIFTS)]
    (layer_out,) = call(
        layer_kernel, [((rows, piece), BF16)], [VMEM] * 5, name="layer"
    )(resid_share, summed[0], *returned)

    handed = call(
        kv_kernel,
        [((QCAP * BLOCK, kv_width), BF16)] * 4,
        [SMEM] * 3 + [VMEM] * 12,
        [
            pltpu.VMEM((rows, width), F32),
            pltpu.VMEM((rows, kv_width), BF16),
            pltpu.VMEM((rows, width), BF16),
        ],
        name="kv",
        vmem=10,
    )(
        place,
        req_owner,
        req_blocks,
        attn_gain.reshape(1, width),
        *spread(layer_out),
        w_kv,
        *kv_got,
        *kv_other,
    )
    received = [handed[0]] + [
        lax.ppermute(values, "decode", pairs)
        for values, pairs in zip(handed[1:], (SWAP_CORE, SWAP_CHIP, SWAP_FAR))
    ]
    (kv_handed,) = call(
        hand_kernel,
        [((QCAP * BLOCK, slots, kv_width), BF16)],
        [SMEM] + [VMEM] * 4,
        name="hand",
    )(place, *received)
    return layer_out, kv_handed[None, None]


def on_device(*operands):
    resid = operands[0]
    zones = lax.axis_size("expert")
    holders = lax.axis_size("decode")
    fits = 2 * resid.shape[0] // (zones // 2) >= resid.shape[0]
    square = zones == holders == 4 and lax.axis_size("tensor") == 1
    if fits and square and lax.axis_size("groups") == 2:
        return near_plan(*operands)
    return wide_plan(*operands)


def solution(mesh):
    return jax.shard_map(
        on_device,
        mesh=mesh,
        in_specs=(
            P(("groups", "expert"), None),
            P(),
            P(),
            P(("groups", "expert")),
            P(("groups", "expert"), None),
            P("expert", None, ("decode", "tensor")),
            P("expert", None, ("decode", "tensor")),
            P("expert", ("decode", "tensor"), None),
            P("expert", ("decode", "tensor")),
            P("expert", ("decode", "tensor")),
            P(("decode", "tensor"), "expert"),
            P("expert", ("decode", "tensor")),
            P(("groups", "expert"), None),
            P(("groups", "expert"), None),
        ),
        out_specs=(
            P(("groups", "expert"), ("decode", "tensor")),
            P(("groups", "expert"), "decode", None, None, "tensor"),
        ),
        check_vma=False,
    )
```

```python
import jax
import jax.numpy as jnp
from jax import lax
from jax.experimental import pallas as pl
from jax.experimental.pallas import tpu as pltpu
from jax.sharding import PartitionSpec as P

BLOCK = 16
QCAP = 4


def rms_scale(values, gain):
    return values * lax.rsqrt(jnp.mean(values * values, axis=-1, keepdims=True) + 1e-05) * gain


def unpermute(slot_values, row_index):
    padded = jnp.concatenate(
        [slot_values, jnp.zeros((1, slot_values.shape[1]), jnp.float32)], axis=0
    )
    return padded[row_index]


def hand_over(key_value, req_owner, req_blocks):
    tok_rows, kv_width = key_value.shape
    owner_count = req_owner.shape[1]
    block_count = tok_rows // BLOCK
    owners = req_owner[0]
    counts = req_blocks[0]
    starts = jnp.cumsum(counts) - counts
    owner_index = jnp.arange(owner_count, dtype=jnp.int32)
    slot_index = jnp.arange(QCAP, dtype=jnp.int32)
    block_index = jnp.arange(block_count, dtype=jnp.int32)
    chosen = owners[:, None, None, None] == owner_index[None, :, None, None]
    chosen = chosen & (slot_index[None, None, :, None] < counts[:, None, None, None])
    chosen = chosen & (
        block_index[None, None, None, :]
        == starts[:, None, None, None] + slot_index[None, None, :, None]
    )
    choose = jnp.sum(chosen.astype(jnp.int32), axis=0).astype(jnp.bfloat16)
    kv_blocks = key_value.reshape(block_count, BLOCK, kv_width)
    sending = jnp.einsum(
        "oqb,bjw->qjow", choose, kv_blocks, preferred_element_type=jnp.float32
    ).astype(jnp.bfloat16)
    sending = sending.reshape(QCAP * BLOCK, owner_count, kv_width)
    received = lax.all_to_all(sending, "decode", split_axis=1, concat_axis=1, tiled=True)
    kv_handed = received.reshape(1, 1, QCAP * BLOCK, owner_count, kv_width)
    return kv_handed


def wide_plan(
    resid,
    moe_gain,
    attn_gain,
    gate_score,
    expert_ids,
    w_gate,
    w_up,
    w_down,
    shared_gate,
    shared_up,
    shared_down,
    w_kv,
    req_owner,
    req_blocks,
):
    tok_rows, feature_width = resid.shape
    expert_count = lax.axis_size("expert")
    pair_count = expert_count // 2
    capacity = 2 * tok_rows // pair_count
    group_size = lax.axis_size(("decode", "tensor"))
    piece_width = feature_width // group_size
    feature_start = lax.axis_index(("decode", "tensor")) * piece_width
    moe_in = rms_scale(resid.astype(jnp.float32), moe_gain).astype(jnp.bfloat16)
    routes = expert_ids[:, 0]
    onehot = (routes[:, None] == jnp.arange(pair_count, dtype=jnp.int32)[None, :]).astype(jnp.int32)
    slots = jnp.sum((jnp.cumsum(onehot, axis=0) - 1) * onehot, axis=1)
    kept = slots < capacity
    position = routes * capacity + slots
    row_index = jnp.where(kept, position, pair_count * capacity)
    selector = (
        position[None, :] == jnp.arange(pair_count * capacity, dtype=jnp.int32)[:, None]
    ) & kept[None, :]
    select_bf = selector.astype(jnp.bfloat16)
    packed = jnp.dot(select_bf, moe_in, preferred_element_type=jnp.float32).astype(jnp.bfloat16)
    packed = packed.reshape(pair_count, capacity, feature_width)
    outgoing = jnp.repeat(packed, 2, axis=0)
    incoming = lax.all_to_all(outgoing, "expert", split_axis=0, concat_axis=0, tiled=True)
    flat_in = incoming.reshape(expert_count * capacity, feature_width)
    gate_val = jnp.dot(flat_in, w_gate[0], preferred_element_type=jnp.float32)
    up_val = jnp.dot(flat_in, w_up[0], preferred_element_type=jnp.float32)
    hidden = (jax.nn.silu(gate_val) * up_val).astype(jnp.bfloat16)
    partial_flat = jnp.dot(hidden, w_down[0], preferred_element_type=jnp.float32).astype(
        jnp.bfloat16
    )
    returned = lax.all_to_all(
        partial_flat.reshape(expert_count, capacity, feature_width),
        "expert",
        split_axis=0,
        concat_axis=0,
        tiled=True,
    )
    pair_sums = jnp.sum(
        returned.reshape(pair_count, 2, capacity, feature_width).astype(jnp.float32), axis=1
    )
    routed_full = (
        unpermute(pair_sums.reshape(pair_count * capacity, feature_width), row_index)
        * gate_score[:, None]
    )
    columns = moe_in
    shared_gate_val = jnp.dot(
        columns,
        lax.all_gather(shared_gate, "expert", axis=0, tiled=True),
        preferred_element_type=jnp.float32,
    )
    shared_up_val = jnp.dot(
        columns,
        lax.all_gather(shared_up, "expert", axis=0, tiled=True),
        preferred_element_type=jnp.float32,
    )
    shared_hidden = (jax.nn.silu(shared_gate_val) * shared_up_val).astype(jnp.bfloat16)
    shared_out = jnp.dot(
        shared_hidden,
        lax.all_gather(shared_down, "expert", axis=1, tiled=True),
        preferred_element_type=jnp.float32,
    )
    total_terms = routed_full + shared_out
    summed_share = lax.psum_scatter(
        total_terms.astype(jnp.bfloat16), ("decode", "tensor"), scatter_dimension=1, tiled=True
    ).astype(jnp.float32)
    resid_share = lax.dynamic_slice_in_dim(resid, feature_start, piece_width, 1)
    layer_out = (resid_share.astype(jnp.float32) + summed_share).astype(jnp.bfloat16)
    full_rows = lax.all_gather(layer_out, ("decode", "tensor"), axis=1, tiled=True)
    attn_in = rms_scale(full_rows.astype(jnp.float32), attn_gain).astype(jnp.bfloat16)
    kv_width = w_kv.shape[1]
    columns = attn_in
    key_value = jnp.dot(
        columns,
        lax.all_gather(w_kv, "expert", axis=0, tiled=True),
        preferred_element_type=jnp.float32,
    ).astype(jnp.bfloat16)
    return layer_out, hand_over(key_value, req_owner, req_blocks)


SWAP_CORE = [(0, 1), (1, 0), (2, 3), (3, 2)]
SWAP_CHIP = [(0, 2), (2, 0), (1, 3), (3, 1)]
SWAP_FAR = [(0, 3), (3, 0), (1, 2), (2, 1)]
SWAP_GROUP = [(0, 1), (1, 0)]
SHIFTS = (2, 1, 3)
BF16 = jnp.bfloat16
F32 = jnp.float32
VMEM = pl.BlockSpec(memory_space=pltpu.VMEM)
SMEM = pl.BlockSpec(memory_space=pltpu.SMEM)
ANY = pl.BlockSpec(memory_space=pl.ANY)
META = 16


def call(body, outs, in_specs, scratch=(), flops=0, moved=0, name=None, vmem=8):
    return pl.pallas_call(
        body,
        out_shape=[jax.ShapeDtypeStruct(shape, kind) for shape, kind in outs],
        in_specs=in_specs,
        out_specs=[VMEM] * len(outs),
        scratch_shapes=list(scratch),
        compiler_params=pltpu.CompilerParams(vmem_limit_bytes=vmem << 20),
        cost_estimate=pl.CostEstimate(flops=flops, bytes_accessed=moved, transcendentals=0),
        name=name,
    )


def to_shift(values, shift):
    count = lax.axis_size("expert")
    return lax.ppermute(values, "expert", [(i, (i + shift) % count) for i in range(count)])


def after(values, *others):
    return lax.optimization_barrier((values,) + others)[0]


def swap_groups(values):
    return lax.ppermute(values, "groups", SWAP_GROUP)


def spread(values):
    across = lax.ppermute(values, "decode", SWAP_CHIP)
    beside = lax.ppermute(values, "decode", SWAP_CORE)
    far = lax.ppermute(across, "decode", SWAP_CORE)
    return values, beside, across, far


def lanes(index, size):
    return pl.ds(pl.multiple_of(index * size, 128), size)


def dot(a, b):
    return jnp.dot(a, b, preferred_element_type=F32)


def first_kernel(
    capacity, place, resid, gain, score, ids, gate, up, down, kv, moe_in, message, share, own, *rest
):
    messages, downs, kv_half, own_down, sem = rest[:3], rest[3:6], rest[6], rest[7], rest[8]
    zone, slot, group = place[0], place[1], place[2]
    count = 4
    hidden = gate.shape[1] // count
    half = hidden // 2
    copies = []

    def move(source, target):
        copies.append(pltpu.make_async_copy(source, target, sem.at[len(copies)]))

    for i, shift in enumerate(SHIFTS):
        start = lax.rem(zone + shift, count) * hidden + group * half
        for j, weights in enumerate((gate, up)):
            move(
                weights.at[:, pl.ds(pl.multiple_of(start, 128), half)],
                messages[i].at[:, j * half : (j + 1) * half],
            )
    for i, shift in enumerate(SHIFTS):
        start = lax.rem(zone + shift, count) * hidden + group * half
        move(down.at[pl.ds(pl.multiple_of(start, 128), half), :], downs[i])
    move(down.at[pl.ds(pl.multiple_of(zone * hidden, 128), hidden), :], own_down)
    start = group * kv_half.shape[1]
    move(kv.at[:, pl.ds(pl.multiple_of(start, 128), kv_half.shape[1])], kv_half)
    for part in range(2):
        start = zone * hidden + (group ^ part) * half
        for j, weights in enumerate((gate, up)):
            move(
                weights.at[:, pl.ds(pl.multiple_of(start, 128), half)],
                own.at[:, (2 * part + j) * half : (2 * part + j + 1) * half],
            )
    for copy in copies:
        copy.start()

    rows, width = resid.shape
    piece = message.shape[1]
    values = resid[...].astype(F32)
    power = jnp.mean(values * values, axis=-1, keepdims=True)
    moe_in[...] = (values * lax.rsqrt(power + 1e-05) * gain[...]).astype(BF16)
    message[:rows, :] = moe_in[:, lanes(slot, piece)]
    share[...] = resid[:, lanes(slot, piece)]
    first = lax.broadcasted_iota(jnp.int32, (rows, rows), 0)
    second = lax.broadcasted_iota(jnp.int32, (rows, rows), 1)
    across = jnp.broadcast_to(ids[...].astype(F32), (rows, rows))
    along = jnp.sum(jnp.where(first == second, across, 0.0), axis=1, keepdims=True)
    same = (along == across) & (first < second)
    slots = jnp.sum(jnp.where(same, 1.0, 0.0), axis=0, keepdims=True)
    scale = jnp.where(slots < capacity, score[...], 0.0)
    high = scale.astype(BF16)
    rest = scale - high.astype(F32)
    middle = rest.astype(BF16)
    low = (rest - middle.astype(F32)).astype(BF16)
    message[rows:, :] = jnp.zeros((META, piece), BF16)
    for i, part in enumerate((high, middle, low, ids[...].astype(F32).astype(BF16))):
        message[rows:, i * rows : (i + 1) * rows] = jnp.broadcast_to(part, (META, rows))
    for copy in copies:
        copy.wait()


def silu(values):
    return values / (1.0 + jnp.exp(-values))


def join_kernel(*refs):
    out, row = refs[-1], 0
    for part in refs[:-1]:
        out[row : row + part.shape[0], :] = part[...]
        row += part.shape[0]


def join(*parts):
    rows = sum(part.shape[0] for part in parts)
    return call(
        join_kernel, [((rows, parts[0].shape[1]), BF16)], [VMEM] * len(parts), name="join"
    )(*parts)[0]


def half_kernel(place, moe_in, *rest):
    own, across, out = rest[:3], rest[3:6], rest[6]
    rows = moe_in.shape[0]
    piece = out.shape[1] // 2
    out[:rows, :piece] = moe_in[:, lanes(place[1], piece)]
    out[:rows, piece:] = moe_in[:, lanes(place[1] ^ 2, piece)]
    for i, shift in enumerate(SHIFTS):
        span = slice(shift * rows, (shift + 1) * rows)
        out[span, :piece] = own[i][:rows, :]
        out[span, piece:] = across[i][:rows, :]


def routed_up_kernel(place, mine, theirs, gate, up, tokens, hidden):
    slot = place[1]
    piece = mine.shape[1] // 2
    for j in range(4):
        source = theirs if j % 2 else mine
        tokens[:, lanes(slot ^ j, piece)] = source[:, (j // 2) * piece : (j // 2 + 1) * piece]
    width = hidden.shape[1]
    step = 256
    for n in range(width // step):
        cols = slice(n * step, (n + 1) * step)
        gate_val = dot(tokens[...], gate[0, :, cols])
        up_val = dot(tokens[...], up[0, :, cols])
        hidden[:, cols] = (silu(gate_val) * up_val).astype(BF16)


def routed_down_kernel(place, hidden, *rest):
    messages, down, out = rest[:4], rest[4], rest[5]
    zone = place[0]
    rows = messages[0].shape[0] - META
    piece = messages[0].shape[1]
    diagonal = lax.broadcasted_iota(jnp.int32, (rows, rows), 0) == lax.broadcasted_iota(
        jnp.int32, (rows, rows), 1
    )
    mine = (zone // 2).astype(F32)
    scales = []
    for source in messages:
        info = source[rows : rows + META, :].astype(F32)[:1]
        value = info[:, :rows] + info[:, rows : 2 * rows] + info[:, 2 * rows : 3 * rows]
        value = jnp.where(info[:, 3 * rows : 4 * rows] == mine, value, 0.0)
        scales.append(jnp.sum(jnp.where(diagonal, value, 0.0), axis=1, keepdims=True))
    scale = jnp.concatenate(scales, axis=0)
    for n in range(out.shape[1] // piece):
        cols = slice(n * piece, (n + 1) * piece)
        out[:, cols] = (dot(hidden[...], down[0, :, cols]) * scale).astype(BF16)


def gate_up_half(place, tokens, own, pieces, part):
    zone = place[0]
    near = own.shape[0]
    width = own.shape[1] // 2
    half = width // 2
    both = dot(tokens[:, lanes(zone, near)], own[:, part * width : (part + 1) * width])
    for i, shift in enumerate(SHIFTS):
        source = lax.rem(zone - shift + 4, 4)
        both = both + dot(tokens[:, lanes(source, near)], pieces[i][...])
    return (silu(both[:, :half]) * both[:, half:]).astype(BF16)


def gate_up_first_kernel(place, tokens, own, a, b, c, hidden):
    hidden[...] = gate_up_half(place, tokens, own, (a, b, c), 0)


def gate_up_second_kernel(place, tokens, own, first, rest, hidden):
    half = first.shape[1]
    near = own.shape[0]
    a, b, c = [rest.at[i * near : (i + 1) * near, :] for i in range(3)]
    hidden[:, lanes(place[2], half)] = first[...]
    hidden[:, lanes(1 - place[2], half)] = gate_up_half(place, tokens, own, (a, b, c), 1)


def down_kernel(place, routed, hidden, own, other, a, b, c, send, keep, weights):
    zone, slot, group = place[0], place[1], place[2]
    piece = own.shape[1]
    half = own.shape[0] // 2
    weights[:, lanes(zone, piece)] = own[...]
    for i, (shift, part) in enumerate(zip(SHIFTS, (a, b, c))):
        cols = lanes(lax.rem(zone - shift + 4, 4), piece)
        weights[pl.ds(pl.multiple_of(group * half, 128), half), cols] = part[...]
        weights[pl.ds(pl.multiple_of((1 - group) * half, 128), half), cols] = other[
            i * half : (i + 1) * half, :
        ]
    for target, parts in ((send, (1, 3)), (keep, (0, 2))):
        for i, j in enumerate(parts):
            cols = lanes(slot ^ j, piece)
            value = routed[:, cols].astype(F32) + dot(hidden[...], weights[:, cols])
            target[:, i * piece : (i + 1) * piece] = value.astype(target.dtype)


def pass_kernel(keep, beside, *outs):
    rows, piece = outs[0].shape
    for shard in range(4):
        span = slice(shard * rows, (shard + 1) * rows)
        value = keep[span, :].astype(F32) + beside[span, :].astype(F32)
        outs[shard][...] = value[:, :piece]
        outs[4 + shard][...] = value[:, piece:].astype(BF16)


def add_kernel(a, b, out):
    out[...] = (a[...] + b[...].astype(F32)).astype(BF16)


def layer_kernel(resid, own, crossed, a, b, c, out):
    value = own[...] + crossed[...].astype(F32) + a[...].astype(F32) + b[...].astype(F32) + c[...].astype(F32)
    value = value + resid[...].astype(F32)
    out[...] = value.astype(BF16)


def kv_kernel(place, owner, blocks, gain, a, b, c, d, own, *rest):
    got, outs = rest[:3], rest[4:8]
    full, key_value, ready = rest[8:]
    rows = own.shape[0]
    other = [rest[3].at[i * rows : (i + 1) * rows, :] for i in range(3)]
    zone, slot, group = place[0], place[1], place[2]
    piece = a.shape[1]
    for j, part in enumerate((a, b, c, d)):
        full[:, lanes(slot ^ j, piece)] = part[...].astype(F32)
    values = full[...]
    power = jnp.mean(values * values, axis=-1, keepdims=True)
    ready[...] = (values * lax.rsqrt(power + 1e-05) * gain[...]).astype(BF16)
    near = own.shape[0]
    half = own.shape[1] // 2
    for part, pieces in ((0, got), (1, other)):
        value = dot(ready[:, lanes(zone, near)], own[:, lanes(group ^ part, half)])
        for i, shift in enumerate(SHIFTS):
            source = lax.rem(zone - shift + 4, 4)
            value = value + dot(ready[:, lanes(source, near)], pieces[i][...])
        key_value[:, lanes(group ^ part, half)] = value.astype(BF16)
    held = full.shape[0] // BLOCK
    width = key_value.shape[1]
    for j in range(4):
        start, amount, begin = 0, 0, 0
        for r in range(4):
            here = owner[0, r] == (slot ^ j)
            amount = jnp.where(here, blocks[0, r], amount)
            begin = jnp.where(here, start, begin)
            start = start + blocks[0, r]
        for q in range(QCAP):
            row = jnp.clip(begin + q, 0, held - 1) * BLOCK
            chosen = key_value[pl.ds(pl.multiple_of(row, BLOCK), BLOCK), :]
            outs[j][q * BLOCK : (q + 1) * BLOCK, :] = jnp.where(
                q < amount, chosen, jnp.zeros((BLOCK, width), BF16)
            )


def hand_kernel(place, a, b, c, d, out):
    parts = [part[...].astype(F32) for part in (a, b, c, d)]
    ordered = []
    for source in range(4):
        j = place[1] ^ source
        value = jnp.where(j == 0, parts[0], parts[1])
        ordered.append(jnp.where(j < 2, value, jnp.where(j == 2, parts[2], parts[3])))
    out[...] = jnp.stack(ordered, axis=1).astype(BF16)


def near_plan(
    resid,
    moe_gain,
    attn_gain,
    gate_score,
    expert_ids,
    w_gate,
    w_up,
    w_down,
    shared_gate,
    shared_up,
    shared_down,
    w_kv,
    req_owner,
    req_blocks,
):
    rows, width = resid.shape
    zones = lax.axis_size("expert")
    slots = lax.axis_size("decode")
    capacity = 2 * rows // (zones // 2)
    piece = width // slots
    near = shared_gate.shape[0]
    hidden = shared_gate.shape[1] // zones
    half = hidden // 2
    total_rows = zones * rows
    routed_width = w_gate.shape[2]
    kv_width = w_kv.shape[1]
    group = lax.axis_index("groups")
    place = jnp.stack(
        [lax.axis_index("expert"), lax.axis_index("decode"), group]
    ).astype(jnp.int32)

    first = call(
        lambda *refs: first_kernel(capacity, *refs),
        [
            ((rows, width), BF16),
            ((rows + META, piece), BF16),
            ((rows, piece), BF16),
            ((near, 2 * hidden), BF16),
        ]
        + [((near, hidden), BF16)] * 3
        + [((half, piece), BF16)] * 3
        + [((near, kv_width // 2), BF16), ((hidden, piece), BF16)],
        [SMEM] + [VMEM] * 4 + [ANY] * 4,
        [pltpu.SemaphoreType.DMA((15,))],
        moved=6 << 20,
        name="first",
        vmem=58,
    )(
        place,
        resid,
        moe_gain.reshape(1, width),
        gate_score.reshape(1, rows),
        expert_ids.reshape(1, rows),
        shared_gate,
        shared_up,
        shared_down,
        w_kv,
    )
    moe_in, message, resid_share, own_weights = first[:4]
    weight_messages, down_messages, kv_half, own_down = first[4:7], first[7:10], *first[10:]

    arrived = [to_shift(message, s) for s in SHIFTS]
    got = [to_shift(values, s) for values, s in zip(weight_messages, SHIFTS)]
    joined = join(*got)
    other = swap_groups(joined)

    across = [lax.ppermute(values, "decode", SWAP_CHIP) for values in arrived]
    (token_half,) = call(
        half_kernel,
        [((total_rows, 2 * piece), BF16)],
        [SMEM] + [VMEM] * 7,
        name="half",
    )(after(place, joined), moe_in, *arrived, *across)
    token_rest = lax.ppermute(token_half, "decode", SWAP_CORE)

    down_got = [to_shift(values, s) for values, s in zip(down_messages, SHIFTS)]
    down_other = swap_groups(join(*down_got))

    kv_half = after(kv_half, *down_got)
    kv_got = [to_shift(kv_half, s) for s in SHIFTS]
    tokens, routed_hidden = call(
        routed_up_kernel,
        [((total_rows, width), BF16), ((total_rows, routed_width), BF16)],
        [SMEM] + [VMEM] * 4,
        flops=4 * total_rows * width * routed_width,
        moved=10 << 20,
        name="routed_up",
        vmem=22,
    )(place, token_half, token_rest, w_gate, w_up)
    (routed,) = call(
        routed_down_kernel,
        [((total_rows, width), BF16)],
        [SMEM] + [VMEM] * 6,
        flops=2 * total_rows * width * routed_width,
        moved=6 << 20,
        name="routed_down",
        vmem=16,
    )(
        place,
        routed_hidden,
        message,
        *[arrived[SHIFTS.index(s)] for s in range(1, zones)],
        w_down,
    )

    (first_half,) = call(
        gate_up_first_kernel,
        [((total_rows, half), BF16)],
        [SMEM] + [VMEM] * 5,
        flops=2 * total_rows * width * hidden,
        moved=4 << 20,
        name="gate_up_first",
        vmem=12,
    )(place, tokens, own_weights, *got)
    (shared_hidden,) = call(
        gate_up_second_kernel,
        [((total_rows, hidden), BF16)],
        [SMEM] + [VMEM] * 4,
        flops=2 * total_rows * width * hidden,
        moved=4 << 20,
        name="gate_up_second",
        vmem=12,
    )(after(place, *down_got), tokens, own_weights, first_half, other)
    kv_joined = join(*lax.optimization_barrier(tuple(kv_got) + (routed, shared_hidden))[:3])
    send, keep = call(
        down_kernel,
        [((total_rows, 2 * piece), BF16), ((total_rows, 2 * piece), F32)],
        [SMEM] + [VMEM] * 7,
        [pltpu.VMEM((hidden, width), BF16)],
        name="down",
        vmem=14,
    )(after(place, kv_joined), routed, shared_hidden, own_down, down_other, *down_got)
    beside = lax.ppermute(send, "decode", SWAP_CORE)
    kv_other = swap_groups(kv_joined)
    passed = call(
        pass_kernel,
        [((rows, piece), F32)] * 4 + [((rows, piece), BF16)] * 4,
        [VMEM] * 2,
        name="pass",
    )(keep, beside)
    crossed = {s: lax.ppermute(passed[4 + s], "decode", SWAP_CHIP) for s in SHIFTS + (0,)}
    returned = []
    for s in SHIFTS:
        (summed,) = call(add_kernel, [((rows, piece), BF16)], [VMEM] * 2, name="add")(
            passed[s], crossed[s]
        )
        returned.append(to_shift(summed, -s))
    (layer_out,) = call(
        layer_kernel, [((rows, piece), BF16)], [VMEM] * 6, name="layer"
    )(resid_share, passed[0], crossed[0], *returned)

    handed = call(
        kv_kernel,
        [((QCAP * BLOCK, kv_width), BF16)] * 4,
        [SMEM] * 3 + [VMEM] * 10,
        [
            pltpu.VMEM((rows, width), F32),
            pltpu.VMEM((rows, kv_width), BF16),
            pltpu.VMEM((rows, width), BF16),
        ],
        name="kv",
        vmem=10,
    )(
        place,
        req_owner,
        req_blocks,
        attn_gain.reshape(1, width),
        *spread(layer_out),
        w_kv,
        *kv_got,
        kv_other,
    )
    received = [handed[0]] + [
        lax.ppermute(values, "decode", pairs)
        for values, pairs in zip(handed[1:], (SWAP_CORE, SWAP_CHIP, SWAP_FAR))
    ]
    (kv_handed,) = call(
        hand_kernel,
        [((QCAP * BLOCK, slots, kv_width), BF16)],
        [SMEM] + [VMEM] * 4,
        name="hand",
    )(place, *received)
    return layer_out, kv_handed[None, None]


def on_device(*operands):
    resid = operands[0]
    zones = lax.axis_size("expert")
    holders = lax.axis_size("decode")
    fits = 2 * resid.shape[0] // (zones // 2) >= resid.shape[0]
    square = zones == holders == 4 and lax.axis_size("tensor") == 1
    if fits and square and lax.axis_size("groups") == 2:
        return near_plan(*operands)
    return wide_plan(*operands)


def solution(mesh):
    return jax.shard_map(
        on_device,
        mesh=mesh,
        in_specs=(
            P(("groups", "expert"), None),
            P(),
            P(),
            P(("groups", "expert")),
            P(("groups", "expert"), None),
            P("expert", None, ("decode", "tensor")),
            P("expert", None, ("decode", "tensor")),
            P("expert", ("decode", "tensor"), None),
            P("expert", ("decode", "tensor")),
            P("expert", ("decode", "tensor")),
            P(("decode", "tensor"), "expert"),
            P("expert", ("decode", "tensor")),
            P(("groups", "expert"), None),
            P(("groups", "expert"), None),
        ),
        out_specs=(
            P(("groups", "expert"), ("decode", "tensor")),
            P(("groups", "expert"), "decode", None, None, "tensor"),
        ),
        check_vma=False,
    )
```

```python
import jax
import jax.numpy as jnp
from jax import lax
from jax.experimental import pallas as pl
from jax.experimental.pallas import tpu as pltpu
from jax.sharding import PartitionSpec as P

BLOCK = 16
QCAP = 4


def rms_scale(values, gain):
    return values * lax.rsqrt(jnp.mean(values * values, axis=-1, keepdims=True) + 1e-05) * gain


def unpermute(slot_values, row_index):
    padded = jnp.concatenate(
        [slot_values, jnp.zeros((1, slot_values.shape[1]), jnp.float32)], axis=0
    )
    return padded[row_index]


def hand_over(key_value, req_owner, req_blocks):
    tok_rows, kv_width = key_value.shape
    owner_count = req_owner.shape[1]
    block_count = tok_rows // BLOCK
    owners = req_owner[0]
    counts = req_blocks[0]
    starts = jnp.cumsum(counts) - counts
    owner_index = jnp.arange(owner_count, dtype=jnp.int32)
    slot_index = jnp.arange(QCAP, dtype=jnp.int32)
    block_index = jnp.arange(block_count, dtype=jnp.int32)
    chosen = owners[:, None, None, None] == owner_index[None, :, None, None]
    chosen = chosen & (slot_index[None, None, :, None] < counts[:, None, None, None])
    chosen = chosen & (
        block_index[None, None, None, :]
        == starts[:, None, None, None] + slot_index[None, None, :, None]
    )
    choose = jnp.sum(chosen.astype(jnp.int32), axis=0).astype(jnp.bfloat16)
    kv_blocks = key_value.reshape(block_count, BLOCK, kv_width)
    sending = jnp.einsum(
        "oqb,bjw->qjow", choose, kv_blocks, preferred_element_type=jnp.float32
    ).astype(jnp.bfloat16)
    sending = sending.reshape(QCAP * BLOCK, owner_count, kv_width)
    received = lax.all_to_all(sending, "decode", split_axis=1, concat_axis=1, tiled=True)
    kv_handed = received.reshape(1, 1, QCAP * BLOCK, owner_count, kv_width)
    return kv_handed


def wide_plan(
    resid,
    moe_gain,
    attn_gain,
    gate_score,
    expert_ids,
    w_gate,
    w_up,
    w_down,
    shared_gate,
    shared_up,
    shared_down,
    w_kv,
    req_owner,
    req_blocks,
):
    tok_rows, feature_width = resid.shape
    expert_count = lax.axis_size("expert")
    pair_count = expert_count // 2
    capacity = 2 * tok_rows // pair_count
    group_size = lax.axis_size(("decode", "tensor"))
    piece_width = feature_width // group_size
    feature_start = lax.axis_index(("decode", "tensor")) * piece_width
    moe_in = rms_scale(resid.astype(jnp.float32), moe_gain).astype(jnp.bfloat16)
    routes = expert_ids[:, 0]
    onehot = (routes[:, None] == jnp.arange(pair_count, dtype=jnp.int32)[None, :]).astype(jnp.int32)
    slots = jnp.sum((jnp.cumsum(onehot, axis=0) - 1) * onehot, axis=1)
    kept = slots < capacity
    position = routes * capacity + slots
    row_index = jnp.where(kept, position, pair_count * capacity)
    selector = (
        position[None, :] == jnp.arange(pair_count * capacity, dtype=jnp.int32)[:, None]
    ) & kept[None, :]
    select_bf = selector.astype(jnp.bfloat16)
    packed = jnp.dot(select_bf, moe_in, preferred_element_type=jnp.float32).astype(jnp.bfloat16)
    packed = packed.reshape(pair_count, capacity, feature_width)
    outgoing = jnp.repeat(packed, 2, axis=0)
    incoming = lax.all_to_all(outgoing, "expert", split_axis=0, concat_axis=0, tiled=True)
    flat_in = incoming.reshape(expert_count * capacity, feature_width)
    gate_val = jnp.dot(flat_in, w_gate[0], preferred_element_type=jnp.float32)
    up_val = jnp.dot(flat_in, w_up[0], preferred_element_type=jnp.float32)
    hidden = (jax.nn.silu(gate_val) * up_val).astype(jnp.bfloat16)
    partial_flat = jnp.dot(hidden, w_down[0], preferred_element_type=jnp.float32).astype(
        jnp.bfloat16
    )
    returned = lax.all_to_all(
        partial_flat.reshape(expert_count, capacity, feature_width),
        "expert",
        split_axis=0,
        concat_axis=0,
        tiled=True,
    )
    pair_sums = jnp.sum(
        returned.reshape(pair_count, 2, capacity, feature_width).astype(jnp.float32), axis=1
    )
    routed_full = (
        unpermute(pair_sums.reshape(pair_count * capacity, feature_width), row_index)
        * gate_score[:, None]
    )
    columns = moe_in
    shared_gate_val = jnp.dot(
        columns,
        lax.all_gather(shared_gate, "expert", axis=0, tiled=True),
        preferred_element_type=jnp.float32,
    )
    shared_up_val = jnp.dot(
        columns,
        lax.all_gather(shared_up, "expert", axis=0, tiled=True),
        preferred_element_type=jnp.float32,
    )
    shared_hidden = (jax.nn.silu(shared_gate_val) * shared_up_val).astype(jnp.bfloat16)
    shared_out = jnp.dot(
        shared_hidden,
        lax.all_gather(shared_down, "expert", axis=1, tiled=True),
        preferred_element_type=jnp.float32,
    )
    total_terms = routed_full + shared_out
    summed_share = lax.psum_scatter(
        total_terms.astype(jnp.bfloat16), ("decode", "tensor"), scatter_dimension=1, tiled=True
    ).astype(jnp.float32)
    resid_share = lax.dynamic_slice_in_dim(resid, feature_start, piece_width, 1)
    layer_out = (resid_share.astype(jnp.float32) + summed_share).astype(jnp.bfloat16)
    full_rows = lax.all_gather(layer_out, ("decode", "tensor"), axis=1, tiled=True)
    attn_in = rms_scale(full_rows.astype(jnp.float32), attn_gain).astype(jnp.bfloat16)
    kv_width = w_kv.shape[1]
    columns = attn_in
    key_value = jnp.dot(
        columns,
        lax.all_gather(w_kv, "expert", axis=0, tiled=True),
        preferred_element_type=jnp.float32,
    ).astype(jnp.bfloat16)
    return layer_out, hand_over(key_value, req_owner, req_blocks)


SWAP_CORE = [(0, 1), (1, 0), (2, 3), (3, 2)]
SWAP_CHIP = [(0, 2), (2, 0), (1, 3), (3, 1)]
SWAP_FAR = [(0, 3), (3, 0), (1, 2), (2, 1)]
SWAP_GROUP = [(0, 1), (1, 0)]
SHIFTS = (2, 1, 3)
BF16 = jnp.bfloat16
F32 = jnp.float32
VMEM = pl.BlockSpec(memory_space=pltpu.VMEM)
SMEM = pl.BlockSpec(memory_space=pltpu.SMEM)
ANY = pl.BlockSpec(memory_space=pl.ANY)
META = 16


def call(body, outs, in_specs, scratch=(), flops=0, moved=0, name=None, vmem=8):
    return pl.pallas_call(
        body,
        out_shape=[jax.ShapeDtypeStruct(shape, kind) for shape, kind in outs],
        in_specs=in_specs,
        out_specs=[VMEM] * len(outs),
        scratch_shapes=list(scratch),
        compiler_params=pltpu.CompilerParams(vmem_limit_bytes=vmem << 20),
        cost_estimate=pl.CostEstimate(flops=flops, bytes_accessed=moved, transcendentals=0),
        name=name,
    )


def to_shift(values, shift):
    count = lax.axis_size("expert")
    return lax.ppermute(values, "expert", [(i, (i + shift) % count) for i in range(count)])


def after(values, *others):
    return lax.optimization_barrier((values,) + others)[0]


def swap_groups(values):
    return lax.ppermute(values, "groups", SWAP_GROUP)


def spread(values):
    across = lax.ppermute(values, "decode", SWAP_CHIP)
    beside = lax.ppermute(values, "decode", SWAP_CORE)
    far = lax.ppermute(across, "decode", SWAP_CORE)
    return values, beside, across, far


def lanes(index, size):
    return pl.ds(pl.multiple_of(index * size, 128), size)


def dot(a, b):
    return jnp.dot(a, b, preferred_element_type=F32)


def first_kernel(
    capacity, place, resid, gain, score, ids, gate, up, down, kv, moe_in, message, share, own, *rest
):
    messages, both, kv_half, own_down, sem = rest[:3], rest[3:6], rest[6], rest[7], rest[8]
    top = message.shape[0]
    zone, slot, group = place[0], place[1], place[2]
    count = 4
    hidden = gate.shape[1] // count
    half = hidden // 2
    copies = []

    def move(source, target):
        copies.append(pltpu.make_async_copy(source, target, sem.at[len(copies)]))

    for i, shift in enumerate(SHIFTS):
        start = lax.rem(zone + shift, count) * hidden + group * half
        for j, weights in enumerate((gate, up)):
            move(
                weights.at[:, pl.ds(pl.multiple_of(start, 128), half)],
                messages[i].at[:, j * half : (j + 1) * half],
            )
    for i, shift in enumerate(SHIFTS):
        start = lax.rem(zone + shift, count) * hidden + group * half
        move(down.at[pl.ds(pl.multiple_of(start, 128), half), :], both[i].at[top:, :])
    move(down.at[pl.ds(pl.multiple_of(zone * hidden, 128), hidden), :], own_down)
    start = group * kv_half.shape[1]
    move(kv.at[:, pl.ds(pl.multiple_of(start, 128), kv_half.shape[1])], kv_half)
    for part in range(2):
        start = zone * hidden + (group ^ part) * half
        for j, weights in enumerate((gate, up)):
            move(
                weights.at[:, pl.ds(pl.multiple_of(start, 128), half)],
                own.at[:, (2 * part + j) * half : (2 * part + j + 1) * half],
            )
    for copy in copies:
        copy.start()

    rows, width = resid.shape
    piece = message.shape[1]
    values = resid[...].astype(F32)
    power = jnp.mean(values * values, axis=-1, keepdims=True)
    moe_in[...] = (values * lax.rsqrt(power + 1e-05) * gain[...][None, :]).astype(BF16)
    message[:rows, :] = moe_in[:, lanes(slot, piece)]
    share[...] = resid[:, lanes(slot, piece)]
    first = lax.broadcasted_iota(jnp.int32, (rows, rows), 0)
    second = lax.broadcasted_iota(jnp.int32, (rows, rows), 1)
    across = jnp.broadcast_to(ids[...].astype(F32), (rows, rows))
    along = jnp.sum(jnp.where(first == second, across, 0.0), axis=1, keepdims=True)
    same = (along == across) & (first < second)
    slots = jnp.sum(jnp.where(same, 1.0, 0.0), axis=0, keepdims=True)
    scale = jnp.where(slots < capacity, score[...], 0.0)
    high = scale.astype(BF16)
    rest = scale - high.astype(F32)
    middle = rest.astype(BF16)
    low = (rest - middle.astype(F32)).astype(BF16)
    message[rows:, :] = jnp.zeros((META, piece), BF16)
    for i, part in enumerate((high, middle, low, ids[...].astype(F32).astype(BF16))):
        message[rows:, i * rows : (i + 1) * rows] = jnp.broadcast_to(part, (META, rows))
    for target in both:
        target[:top, :] = message[...]
    for copy in copies:
        copy.wait()


def silu(values):
    return values / (1.0 + jnp.exp(-values))


def join_kernel(*refs):
    out, row = refs[-1], 0
    for part in refs[:-1]:
        out[row : row + part.shape[0], :] = part[...]
        row += part.shape[0]


def join(*parts):
    rows = sum(part.shape[0] for part in parts)
    return call(
        join_kernel, [((rows, parts[0].shape[1]), BF16)], [VMEM] * len(parts), name="join"
    )(*parts)[0]


def half_kernel(place, moe_in, *rest):
    own, across, out = rest[:3], rest[3:6], rest[6]
    rows = moe_in.shape[0]
    piece = out.shape[1] // 2
    out[:rows, :piece] = moe_in[:, lanes(place[1], piece)]
    out[:rows, piece:] = moe_in[:, lanes(place[1] ^ 2, piece)]
    for i, shift in enumerate(SHIFTS):
        span = slice(shift * rows, (shift + 1) * rows)
        out[span, :piece] = own[i][:rows, :]
        out[span, piece:] = across[i][:rows, :]


def routed_up_kernel(place, mine, theirs, gate, up, tokens, hidden):
    slot = place[1]
    piece = mine.shape[1] // 2
    for j in range(4):
        source = theirs if j % 2 else mine
        tokens[:, lanes(slot ^ j, piece)] = source[:, (j // 2) * piece : (j // 2 + 1) * piece]
    width = hidden.shape[1]
    step = 256
    for n in range(width // step):
        cols = slice(n * step, (n + 1) * step)
        gate_val = dot(tokens[...], gate[0, :, cols])
        up_val = dot(tokens[...], up[0, :, cols])
        hidden[:, cols] = (silu(gate_val) * up_val).astype(BF16)


def routed_down_kernel(place, hidden, *rest):
    messages, down, out = rest[:4], rest[4], rest[5]
    zone = place[0]
    rows = messages[0].shape[0] - META
    piece = messages[0].shape[1]
    diagonal = lax.broadcasted_iota(jnp.int32, (rows, rows), 0) == lax.broadcasted_iota(
        jnp.int32, (rows, rows), 1
    )
    mine = (zone // 2).astype(F32)
    scales = []
    for source in messages:
        info = source[rows : rows + META, :].astype(F32)[:1]
        value = info[:, :rows] + info[:, rows : 2 * rows] + info[:, 2 * rows : 3 * rows]
        value = jnp.where(info[:, 3 * rows : 4 * rows] == mine, value, 0.0)
        scales.append(jnp.sum(jnp.where(diagonal, value, 0.0), axis=1, keepdims=True))
    scale = jnp.concatenate(scales, axis=0)
    for n in range(out.shape[1] // piece):
        cols = slice(n * piece, (n + 1) * piece)
        out[:, cols] = (dot(hidden[...], down[0, :, cols]) * scale).astype(BF16)


def gate_up_half(place, tokens, own, pieces, part):
    zone = place[0]
    near = own.shape[0]
    width = own.shape[1] // 2
    half = width // 2
    both = dot(tokens[:, lanes(zone, near)], own[:, part * width : (part + 1) * width])
    for i, shift in enumerate(SHIFTS):
        source = lax.rem(zone - shift + 4, 4)
        both = both + dot(tokens[:, lanes(source, near)], pieces[i][...])
    return (silu(both[:, :half]) * both[:, half:]).astype(BF16)


def gate_up_first_kernel(place, tokens, own, a, b, c, hidden):
    hidden[...] = gate_up_half(place, tokens, own, (a, b, c), 0)


def gate_up_second_kernel(place, tokens, own, first, rest, hidden):
    half = first.shape[1]
    near = own.shape[0]
    a, b, c = [rest.at[i * near : (i + 1) * near, :] for i in range(3)]
    hidden[:, lanes(place[2], half)] = first[...]
    hidden[:, lanes(1 - place[2], half)] = gate_up_half(place, tokens, own, (a, b, c), 1)


def down_kernel(place, routed, hidden, own, other, a, b, c, send, keep, weights):
    zone, slot, group = place[0], place[1], place[2]
    piece = own.shape[1]
    half = own.shape[0] // 2
    weights[:, lanes(zone, piece)] = own[...]
    for i, (shift, part) in enumerate(zip(SHIFTS, (a, b, c))):
        cols = lanes(lax.rem(zone - shift + 4, 4), piece)
        weights[pl.ds(pl.multiple_of(group * half, 128), half), cols] = part[...]
        weights[pl.ds(pl.multiple_of((1 - group) * half, 128), half), cols] = other[
            i * half : (i + 1) * half, :
        ]
    for target, parts in ((send, (1, 3)), (keep, (0, 2))):
        for i, j in enumerate(parts):
            cols = lanes(slot ^ j, piece)
            value = routed[:, cols].astype(F32) + dot(hidden[...], weights[:, cols])
            target[:, i * piece : (i + 1) * piece] = value.astype(target.dtype)


def pass_kernel(keep, beside, *outs):
    rows, piece = outs[0].shape
    for shard in range(4):
        span = slice(shard * rows, (shard + 1) * rows)
        value = keep[span, :].astype(F32) + beside[span, :].astype(F32)
        outs[shard][...] = value[:, :piece]
        outs[4 + shard][...] = value[:, piece:].astype(BF16)


def add_kernel(a, b, out):
    out[...] = (a[...] + b[...].astype(F32)).astype(BF16)


def layer_kernel(resid, own, crossed, a, b, c, out):
    value = own[...] + crossed[...].astype(F32) + a[...].astype(F32) + b[...].astype(F32) + c[...].astype(F32)
    value = value + resid[...].astype(F32)
    out[...] = value.astype(BF16)


def kv_kernel(place, owner, blocks, gain, a, b, c, d, own, *rest):
    got, outs = rest[:3], rest[4:8]
    full, key_value, ready = rest[8:]
    rows = own.shape[0]
    other = [rest[3].at[i * rows : (i + 1) * rows, :] for i in range(3)]
    zone, slot, group = place[0], place[1], place[2]
    piece = a.shape[1]
    for j, part in enumerate((a, b, c, d)):
        full[:, lanes(slot ^ j, piece)] = part[...].astype(F32)
    values = full[...]
    power = jnp.mean(values * values, axis=-1, keepdims=True)
    ready[...] = (values * lax.rsqrt(power + 1e-05) * gain[...][None, :]).astype(BF16)
    near = own.shape[0]
    half = own.shape[1] // 2
    for part, pieces in ((0, got), (1, other)):
        value = dot(ready[:, lanes(zone, near)], own[:, lanes(group ^ part, half)])
        for i, shift in enumerate(SHIFTS):
            source = lax.rem(zone - shift + 4, 4)
            value = value + dot(ready[:, lanes(source, near)], pieces[i][...])
        key_value[:, lanes(group ^ part, half)] = value.astype(BF16)
    held = full.shape[0] // BLOCK
    width = key_value.shape[1]
    for j in range(4):
        start, amount, begin = 0, 0, 0
        for r in range(4):
            here = owner[0, r] == (slot ^ j)
            amount = jnp.where(here, blocks[0, r], amount)
            begin = jnp.where(here, start, begin)
            start = start + blocks[0, r]
        for q in range(QCAP):
            row = jnp.clip(begin + q, 0, held - 1) * BLOCK
            chosen = key_value[pl.ds(pl.multiple_of(row, BLOCK), BLOCK), :]
            outs[j][q * BLOCK : (q + 1) * BLOCK, :] = jnp.where(
                q < amount, chosen, jnp.zeros((BLOCK, width), BF16)
            )


def hand_kernel(place, a, b, c, d, out):
    parts = [part[...].astype(F32) for part in (a, b, c, d)]
    ordered = []
    for source in range(4):
        j = place[1] ^ source
        value = jnp.where(j == 0, parts[0], parts[1])
        ordered.append(jnp.where(j < 2, value, jnp.where(j == 2, parts[2], parts[3])))
    out[...] = jnp.stack(ordered, axis=1).astype(BF16)


def near_plan(
    resid,
    moe_gain,
    attn_gain,
    gate_score,
    expert_ids,
    w_gate,
    w_up,
    w_down,
    shared_gate,
    shared_up,
    shared_down,
    w_kv,
    req_owner,
    req_blocks,
):
    rows, width = resid.shape
    zones = lax.axis_size("expert")
    slots = lax.axis_size("decode")
    capacity = 2 * rows // (zones // 2)
    piece = width // slots
    near = shared_gate.shape[0]
    hidden = shared_gate.shape[1] // zones
    half = hidden // 2
    total_rows = zones * rows
    routed_width = w_gate.shape[2]
    kv_width = w_kv.shape[1]
    group = lax.axis_index("groups")
    place = jnp.stack(
        [lax.axis_index("expert"), lax.axis_index("decode"), group]
    ).astype(jnp.int32)

    first = call(
        lambda *refs: first_kernel(capacity, *refs),
        [
            ((rows, width), BF16),
            ((rows + META, piece), BF16),
            ((rows, piece), BF16),
            ((near, 2 * hidden), BF16),
        ]
        + [((near, hidden), BF16)] * 3
        + [((rows + META + half, piece), BF16)] * 3
        + [((near, kv_width // 2), BF16), ((hidden, piece), BF16)],
        [SMEM] + [VMEM] * 4 + [ANY] * 4,
        [pltpu.SemaphoreType.DMA((15,))],
        moved=6 << 20,
        name="first",
        vmem=58,
    )(
        place,
        resid,
        moe_gain,
        gate_score.reshape(1, rows),
        expert_ids.reshape(1, rows),
        shared_gate,
        shared_up,
        shared_down,
        w_kv,
    )
    moe_in, message, resid_share, own_weights = first[:4]
    weight_messages, mixed_messages, kv_half, own_down = first[4:7], first[7:10], *first[10:]

    mixed = [to_shift(values, s) for values, s in zip(mixed_messages, SHIFTS)]
    top = rows + META
    arrived = [values[:top] for values in mixed]
    got = [to_shift(values, s) for values, s in zip(weight_messages, SHIFTS)]
    joined = join(*got)
    other = swap_groups(joined)

    down_got = [values[top:] for values in mixed]
    down_other = swap_groups(join(*down_got))

    across = [lax.ppermute(values, "decode", SWAP_CHIP) for values in arrived]
    (token_half,) = call(
        half_kernel,
        [((total_rows, 2 * piece), BF16)],
        [SMEM] + [VMEM] * 7,
        name="half",
    )(after(place, joined), moe_in, *arrived, *across)
    token_rest = lax.ppermute(token_half, "decode", SWAP_CORE)

    kv_half = after(kv_half, joined)
    kv_got = [to_shift(kv_half, s) for s in SHIFTS]
    tokens, routed_hidden = call(
        routed_up_kernel,
        [((total_rows, width), BF16), ((total_rows, routed_width), BF16)],
        [SMEM] + [VMEM] * 4,
        flops=4 * total_rows * width * routed_width,
        moved=10 << 20,
        name="routed_up",
        vmem=22,
    )(place, token_half, token_rest, w_gate, w_up)
    (routed,) = call(
        routed_down_kernel,
        [((total_rows, width), BF16)],
        [SMEM] + [VMEM] * 6,
        flops=2 * total_rows * width * routed_width,
        moved=6 << 20,
        name="routed_down",
        vmem=16,
    )(
        place,
        routed_hidden,
        message,
        *[arrived[SHIFTS.index(s)] for s in range(1, zones)],
        w_down,
    )

    (first_half,) = call(
        gate_up_first_kernel,
        [((total_rows, half), BF16)],
        [SMEM] + [VMEM] * 5,
        flops=2 * total_rows * width * hidden,
        moved=4 << 20,
        name="gate_up_first",
        vmem=12,
    )(after(place, routed), tokens, own_weights, *got)
    (shared_hidden,) = call(
        gate_up_second_kernel,
        [((total_rows, hidden), BF16)],
        [SMEM] + [VMEM] * 4,
        flops=2 * total_rows * width * hidden,
        moved=4 << 20,
        name="gate_up_second",
        vmem=12,
    )(place, tokens, own_weights, first_half, other)
    kv_joined = join(*lax.optimization_barrier(tuple(kv_got) + (routed, shared_hidden))[:3])
    send, keep = call(
        down_kernel,
        [((total_rows, 2 * piece), BF16), ((total_rows, 2 * piece), F32)],
        [SMEM] + [VMEM] * 7,
        [pltpu.VMEM((hidden, width), BF16)],
        name="down",
        vmem=14,
    )(after(place, kv_joined), routed, shared_hidden, own_down, down_other, *down_got)
    beside = lax.ppermute(send, "decode", SWAP_CORE)
    kv_other = swap_groups(kv_joined)
    passed = call(
        pass_kernel,
        [((rows, piece), F32)] * 4 + [((rows, piece), BF16)] * 4,
        [VMEM] * 2,
        name="pass",
    )(keep, beside)
    crossed = {s: lax.ppermute(passed[4 + s], "decode", SWAP_CHIP) for s in SHIFTS + (0,)}
    returned = []
    for s in SHIFTS:
        (summed,) = call(add_kernel, [((rows, piece), BF16)], [VMEM] * 2, name="add")(
            passed[s], crossed[s]
        )
        returned.append(to_shift(summed, -s))
    (layer_out,) = call(
        layer_kernel, [((rows, piece), BF16)], [VMEM] * 6, name="layer"
    )(resid_share, passed[0], crossed[0], *returned)

    handed = call(
        kv_kernel,
        [((QCAP * BLOCK, kv_width), BF16)] * 4,
        [SMEM] * 3 + [VMEM] * 10,
        [
            pltpu.VMEM((rows, width), F32),
            pltpu.VMEM((rows, kv_width), BF16),
            pltpu.VMEM((rows, width), BF16),
        ],
        name="kv",
        vmem=10,
    )(
        place,
        req_owner,
        req_blocks,
        attn_gain,
        *spread(layer_out),
        w_kv,
        *kv_got,
        kv_other,
    )
    received = [handed[0]] + [
        lax.ppermute(values, "decode", pairs)
        for values, pairs in zip(handed[1:], (SWAP_CORE, SWAP_CHIP, SWAP_FAR))
    ]
    (kv_handed,) = call(
        hand_kernel,
        [((QCAP * BLOCK, slots, kv_width), BF16)],
        [SMEM] + [VMEM] * 4,
        name="hand",
    )(place, *received)
    return layer_out, kv_handed[None, None]


def on_device(*operands):
    resid = operands[0]
    zones = lax.axis_size("expert")
    holders = lax.axis_size("decode")
    fits = 2 * resid.shape[0] // (zones // 2) >= resid.shape[0]
    square = zones == holders == 4 and lax.axis_size("tensor") == 1
    if fits and square and lax.axis_size("groups") == 2:
        return near_plan(*operands)
    return wide_plan(*operands)


def solution(mesh):
    return jax.shard_map(
        on_device,
        mesh=mesh,
        in_specs=(
            P(("groups", "expert"), None),
            P(),
            P(),
            P(("groups", "expert")),
            P(("groups", "expert"), None),
            P("expert", None, ("decode", "tensor")),
            P("expert", None, ("decode", "tensor")),
            P("expert", ("decode", "tensor"), None),
            P("expert", ("decode", "tensor")),
            P("expert", ("decode", "tensor")),
            P(("decode", "tensor"), "expert"),
            P("expert", ("decode", "tensor")),
            P(("groups", "expert"), None),
            P(("groups", "expert"), None),
        ),
        out_specs=(
            P(("groups", "expert"), ("decode", "tensor")),
            P(("groups", "expert"), "decode", None, None, "tensor"),
        ),
        check_vma=False,
    )
```

```python
import jax
import jax.numpy as jnp
from jax import lax
from jax.experimental import pallas as pl
from jax.experimental.pallas import tpu as pltpu
from jax.sharding import PartitionSpec as P

BLOCK = 16
QCAP = 4


def rms_scale(values, gain):
    return values * lax.rsqrt(jnp.mean(values * values, axis=-1, keepdims=True) + 1e-05) * gain


def unpermute(slot_values, row_index):
    padded = jnp.concatenate(
        [slot_values, jnp.zeros((1, slot_values.shape[1]), jnp.float32)], axis=0
    )
    return padded[row_index]


def hand_over(key_value, req_owner, req_blocks):
    tok_rows, kv_width = key_value.shape
    owner_count = req_owner.shape[1]
    block_count = tok_rows // BLOCK
    owners = req_owner[0]
    counts = req_blocks[0]
    starts = jnp.cumsum(counts) - counts
    owner_index = jnp.arange(owner_count, dtype=jnp.int32)
    slot_index = jnp.arange(QCAP, dtype=jnp.int32)
    block_index = jnp.arange(block_count, dtype=jnp.int32)
    chosen = owners[:, None, None, None] == owner_index[None, :, None, None]
    chosen = chosen & (slot_index[None, None, :, None] < counts[:, None, None, None])
    chosen = chosen & (
        block_index[None, None, None, :]
        == starts[:, None, None, None] + slot_index[None, None, :, None]
    )
    choose = jnp.sum(chosen.astype(jnp.int32), axis=0).astype(jnp.bfloat16)
    kv_blocks = key_value.reshape(block_count, BLOCK, kv_width)
    sending = jnp.einsum(
        "oqb,bjw->qjow", choose, kv_blocks, preferred_element_type=jnp.float32
    ).astype(jnp.bfloat16)
    sending = sending.reshape(QCAP * BLOCK, owner_count, kv_width)
    received = lax.all_to_all(sending, "decode", split_axis=1, concat_axis=1, tiled=True)
    kv_handed = received.reshape(1, 1, QCAP * BLOCK, owner_count, kv_width)
    return kv_handed


def wide_plan(
    resid,
    moe_gain,
    attn_gain,
    gate_score,
    expert_ids,
    w_gate,
    w_up,
    w_down,
    shared_gate,
    shared_up,
    shared_down,
    w_kv,
    req_owner,
    req_blocks,
):
    tok_rows, feature_width = resid.shape
    expert_count = lax.axis_size("expert")
    pair_count = expert_count // 2
    capacity = 2 * tok_rows // pair_count
    group_size = lax.axis_size(("decode", "tensor"))
    piece_width = feature_width // group_size
    feature_start = lax.axis_index(("decode", "tensor")) * piece_width
    moe_in = rms_scale(resid.astype(jnp.float32), moe_gain).astype(jnp.bfloat16)
    routes = expert_ids[:, 0]
    onehot = (routes[:, None] == jnp.arange(pair_count, dtype=jnp.int32)[None, :]).astype(jnp.int32)
    slots = jnp.sum((jnp.cumsum(onehot, axis=0) - 1) * onehot, axis=1)
    kept = slots < capacity
    position = routes * capacity + slots
    row_index = jnp.where(kept, position, pair_count * capacity)
    selector = (
        position[None, :] == jnp.arange(pair_count * capacity, dtype=jnp.int32)[:, None]
    ) & kept[None, :]
    select_bf = selector.astype(jnp.bfloat16)
    packed = jnp.dot(select_bf, moe_in, preferred_element_type=jnp.float32).astype(jnp.bfloat16)
    packed = packed.reshape(pair_count, capacity, feature_width)
    outgoing = jnp.repeat(packed, 2, axis=0)
    incoming = lax.all_to_all(outgoing, "expert", split_axis=0, concat_axis=0, tiled=True)
    flat_in = incoming.reshape(expert_count * capacity, feature_width)
    gate_val = jnp.dot(flat_in, w_gate[0], preferred_element_type=jnp.float32)
    up_val = jnp.dot(flat_in, w_up[0], preferred_element_type=jnp.float32)
    hidden = (jax.nn.silu(gate_val) * up_val).astype(jnp.bfloat16)
    partial_flat = jnp.dot(hidden, w_down[0], preferred_element_type=jnp.float32).astype(
        jnp.bfloat16
    )
    returned = lax.all_to_all(
        partial_flat.reshape(expert_count, capacity, feature_width),
        "expert",
        split_axis=0,
        concat_axis=0,
        tiled=True,
    )
    pair_sums = jnp.sum(
        returned.reshape(pair_count, 2, capacity, feature_width).astype(jnp.float32), axis=1
    )
    routed_full = (
        unpermute(pair_sums.reshape(pair_count * capacity, feature_width), row_index)
        * gate_score[:, None]
    )
    columns = moe_in
    shared_gate_val = jnp.dot(
        columns,
        lax.all_gather(shared_gate, "expert", axis=0, tiled=True),
        preferred_element_type=jnp.float32,
    )
    shared_up_val = jnp.dot(
        columns,
        lax.all_gather(shared_up, "expert", axis=0, tiled=True),
        preferred_element_type=jnp.float32,
    )
    shared_hidden = (jax.nn.silu(shared_gate_val) * shared_up_val).astype(jnp.bfloat16)
    shared_out = jnp.dot(
        shared_hidden,
        lax.all_gather(shared_down, "expert", axis=1, tiled=True),
        preferred_element_type=jnp.float32,
    )
    total_terms = routed_full + shared_out
    summed_share = lax.psum_scatter(
        total_terms.astype(jnp.bfloat16), ("decode", "tensor"), scatter_dimension=1, tiled=True
    ).astype(jnp.float32)
    resid_share = lax.dynamic_slice_in_dim(resid, feature_start, piece_width, 1)
    layer_out = (resid_share.astype(jnp.float32) + summed_share).astype(jnp.bfloat16)
    full_rows = lax.all_gather(layer_out, ("decode", "tensor"), axis=1, tiled=True)
    attn_in = rms_scale(full_rows.astype(jnp.float32), attn_gain).astype(jnp.bfloat16)
    kv_width = w_kv.shape[1]
    columns = attn_in
    key_value = jnp.dot(
        columns,
        lax.all_gather(w_kv, "expert", axis=0, tiled=True),
        preferred_element_type=jnp.float32,
    ).astype(jnp.bfloat16)
    return layer_out, hand_over(key_value, req_owner, req_blocks)


SWAP_CORE = [(0, 1), (1, 0), (2, 3), (3, 2)]
SWAP_CHIP = [(0, 2), (2, 0), (1, 3), (3, 1)]
SWAP_FAR = [(0, 3), (3, 0), (1, 2), (2, 1)]
SWAP_GROUP = [(0, 1), (1, 0)]
SHIFTS = (2, 1, 3)
BF16 = jnp.bfloat16
F32 = jnp.float32
VMEM = pl.BlockSpec(memory_space=pltpu.VMEM)
SMEM = pl.BlockSpec(memory_space=pltpu.SMEM)
ANY = pl.BlockSpec(memory_space=pl.ANY)
META = 16


def call(body, outs, in_specs, scratch=(), flops=0, moved=0, name=None, vmem=8):
    return pl.pallas_call(
        body,
        out_shape=[jax.ShapeDtypeStruct(shape, kind) for shape, kind in outs],
        in_specs=in_specs,
        out_specs=[VMEM] * len(outs),
        scratch_shapes=list(scratch),
        compiler_params=pltpu.CompilerParams(vmem_limit_bytes=vmem << 20),
        cost_estimate=pl.CostEstimate(flops=0, bytes_accessed=0, transcendentals=0),
        name=name,
    )


def to_shift(values, shift):
    count = lax.axis_size("expert")
    return lax.ppermute(values, "expert", [(i, (i + shift) % count) for i in range(count)])


def after(values, *others):
    return lax.optimization_barrier((values,) + others)[0]


def swap_groups(values):
    return lax.ppermute(values, "groups", SWAP_GROUP)


def spread(values):
    across = lax.ppermute(values, "decode", SWAP_CHIP)
    beside = lax.ppermute(values, "decode", SWAP_CORE)
    far = lax.ppermute(across, "decode", SWAP_CORE)
    return values, beside, across, far


def lanes(index, size):
    return pl.ds(pl.multiple_of(index * size, 128), size)


def dot(a, b):
    return jnp.dot(a, b, preferred_element_type=F32)


def first_kernel(
    capacity, place, resid, gain, score, ids, down, moe_in, message, share, *rest
):
    both, sem = rest[:3], rest[3]
    top = message.shape[0]
    zone, slot, group = place[0], place[1], place[2]
    count = 4
    hidden = down.shape[0] // count
    half = hidden // 2
    copies = []

    def move(source, target):
        copies.append(pltpu.make_async_copy(source, target, sem.at[len(copies)]))

    for i, shift in enumerate(SHIFTS):
        start = lax.rem(zone + shift, count) * hidden + group * half
        move(down.at[pl.ds(pl.multiple_of(start, 128), half), :], both[i].at[top:, :])
    for copy in copies:
        copy.start()

    rows, width = resid.shape
    piece = message.shape[1]
    values = resid[...].astype(F32)
    power = jnp.mean(values * values, axis=-1, keepdims=True)
    moe_in[...] = (values * lax.rsqrt(power + 1e-05) * gain[...][None, :]).astype(BF16)
    message[:rows, :] = moe_in[:, lanes(slot, piece)]
    share[...] = resid[:, lanes(slot, piece)]
    first = lax.broadcasted_iota(jnp.int32, (rows, rows), 0)
    second = lax.broadcasted_iota(jnp.int32, (rows, rows), 1)
    across = jnp.broadcast_to(ids[...].astype(F32), (rows, rows))
    along = jnp.sum(jnp.where(first == second, across, 0.0), axis=1, keepdims=True)
    same = (along == across) & (first < second)
    slots = jnp.sum(jnp.where(same, 1.0, 0.0), axis=0, keepdims=True)
    scale = jnp.where(slots < capacity, score[...], 0.0)
    high = scale.astype(BF16)
    rest = scale - high.astype(F32)
    middle = rest.astype(BF16)
    low = (rest - middle.astype(F32)).astype(BF16)
    message[rows:, :] = jnp.zeros((META, piece), BF16)
    for i, part in enumerate((high, middle, low, ids[...].astype(F32).astype(BF16))):
        message[rows:, i * rows : (i + 1) * rows] = jnp.broadcast_to(part, (META, rows))
    for target in both:
        target[:top, :] = message[...]
    for copy in copies:
        copy.wait()


def second_kernel(place, gate, up, down, kv, own, own_down, *rest):
    messages, kv_half, sem = rest[:3], rest[3], rest[4]
    count = 4
    zone, group = place[0], place[2]
    hidden = gate.shape[1] // 4
    half = hidden // 2
    copies = []

    def move(source, target):
        copies.append(pltpu.make_async_copy(source, target, sem.at[len(copies)]))

    move(down.at[pl.ds(pl.multiple_of(zone * hidden, 128), hidden), :], own_down)
    for i, shift in enumerate(SHIFTS):
        start = lax.rem(zone + shift, count) * hidden + group * half
        for j, weights in enumerate((gate, up)):
            move(
                weights.at[:, pl.ds(pl.multiple_of(start, 128), half)],
                messages[i].at[:, j * half : (j + 1) * half],
            )
    start = group * kv_half.shape[1]
    move(kv.at[:, pl.ds(pl.multiple_of(start, 128), kv_half.shape[1])], kv_half)
    for part in range(2):
        start = zone * hidden + (group ^ part) * half
        for j, weights in enumerate((gate, up)):
            move(
                weights.at[:, pl.ds(pl.multiple_of(start, 128), half)],
                own.at[:, (2 * part + j) * half : (2 * part + j + 1) * half],
            )
    for copy in copies:
        copy.start()
    for copy in copies:
        copy.wait()


def silu(values):
    return values / (1.0 + jnp.exp(-values))


def join_kernel(*refs):
    out, row = refs[-1], 0
    for part in refs[:-1]:
        out[row : row + part.shape[0], :] = part[...]
        row += part.shape[0]


def join(*parts):
    rows = sum(part.shape[0] for part in parts)
    return call(
        join_kernel, [((rows, parts[0].shape[1]), BF16)], [VMEM] * len(parts), name="join"
    )(*parts)[0]


def half_kernel(place, moe_in, *rest):
    own, across, out = rest[:3], rest[3:6], rest[6]
    rows = moe_in.shape[0]
    piece = out.shape[1] // 2
    out[:rows, :piece] = moe_in[:, lanes(place[1], piece)]
    out[:rows, piece:] = moe_in[:, lanes(place[1] ^ 2, piece)]
    for i, shift in enumerate(SHIFTS):
        span = slice(shift * rows, (shift + 1) * rows)
        out[span, :piece] = own[i][:rows, :]
        out[span, piece:] = across[i][:rows, :]


def routed_up_kernel(place, mine, theirs, gate, up, tokens, hidden):
    slot = place[1]
    piece = mine.shape[1] // 2
    for j in range(4):
        source = theirs if j % 2 else mine
        tokens[:, lanes(slot ^ j, piece)] = source[:, (j // 2) * piece : (j // 2 + 1) * piece]
    width = hidden.shape[1]
    step = 256
    for n in range(width // step):
        cols = slice(n * step, (n + 1) * step)
        gate_val = dot(tokens[...], gate[0, :, cols])
        up_val = dot(tokens[...], up[0, :, cols])
        hidden[:, cols] = (silu(gate_val) * up_val).astype(BF16)


def routed_down_kernel(place, hidden, *rest):
    messages, down, out = rest[:4], rest[4], rest[5]
    zone = place[0]
    rows = messages[0].shape[0] - META
    piece = messages[0].shape[1]
    diagonal = lax.broadcasted_iota(jnp.int32, (rows, rows), 0) == lax.broadcasted_iota(
        jnp.int32, (rows, rows), 1
    )
    mine = (zone // 2).astype(F32)
    scales = []
    for source in messages:
        info = source[rows : rows + META, :].astype(F32)[:1]
        value = info[:, :rows] + info[:, rows : 2 * rows] + info[:, 2 * rows : 3 * rows]
        value = jnp.where(info[:, 3 * rows : 4 * rows] == mine, value, 0.0)
        scales.append(jnp.sum(jnp.where(diagonal, value, 0.0), axis=1, keepdims=True))
    scale = jnp.concatenate(scales, axis=0)
    for n in range(out.shape[1] // piece):
        cols = slice(n * piece, (n + 1) * piece)
        out[:, cols] = (dot(hidden[...], down[0, :, cols]) * scale).astype(BF16)


def gate_up_half(place, tokens, own, pieces, part):
    zone = place[0]
    near = own.shape[0]
    width = own.shape[1] // 2
    half = width // 2
    both = dot(tokens[:, lanes(zone, near)], own[:, part * width : (part + 1) * width])
    for i, shift in enumerate(SHIFTS):
        source = lax.rem(zone - shift + 4, 4)
        both = both + dot(tokens[:, lanes(source, near)], pieces[i][...])
    return (silu(both[:, :half]) * both[:, half:]).astype(BF16)


def gate_up_first_kernel(place, tokens, own, a, b, c, hidden):
    hidden[...] = gate_up_half(place, tokens, own, (a, b, c), 0)


def gate_up_second_kernel(place, tokens, own, first, rest, hidden):
    half = first.shape[1]
    near = own.shape[0]
    a, b, c = [rest.at[i * near : (i + 1) * near, :] for i in range(3)]
    hidden[:, lanes(place[2], half)] = first[...]
    hidden[:, lanes(1 - place[2], half)] = gate_up_half(place, tokens, own, (a, b, c), 1)


def down_kernel(place, routed, hidden, own, other, a, b, c, send, keep, weights):
    zone, slot, group = place[0], place[1], place[2]
    piece = own.shape[1]
    half = own.shape[0] // 2
    weights[:, lanes(zone, piece)] = own[...]
    for i, (shift, part) in enumerate(zip(SHIFTS, (a, b, c))):
        cols = lanes(lax.rem(zone - shift + 4, 4), piece)
        weights[pl.ds(pl.multiple_of(group * half, 128), half), cols] = part[...]
        weights[pl.ds(pl.multiple_of((1 - group) * half, 128), half), cols] = other[
            i * half : (i + 1) * half, :
        ]
    for target, parts in ((send, (1, 3)), (keep, (0, 2))):
        for i, j in enumerate(parts):
            cols = lanes(slot ^ j, piece)
            value = routed[:, cols].astype(F32) + dot(hidden[...], weights[:, cols])
            target[:, i * piece : (i + 1) * piece] = value.astype(target.dtype)


def pass_kernel(keep, beside, *outs):
    rows, piece = outs[0].shape
    for shard in range(4):
        span = slice(shard * rows, (shard + 1) * rows)
        value = keep[span, :].astype(F32) + beside[span, :].astype(F32)
        outs[shard][...] = value[:, :piece]
        outs[4 + shard][...] = value[:, piece:].astype(BF16)


def add_kernel(a, b, out):
    out[...] = (a[...] + b[...].astype(F32)).astype(BF16)


def layer_kernel(resid, own, crossed, a, b, c, out, again):
    value = own[...] + crossed[...].astype(F32) + a[...].astype(F32) + b[...].astype(F32) + c[...].astype(F32)
    value = value + resid[...].astype(F32)
    out[...] = value.astype(BF16)
    again[...] = out[...]


def kv_kernel(place, owner, blocks, gain, a, b, c, d, own, *rest):
    got, outs = rest[:3], rest[4:8]
    full, key_value, ready = rest[8:]
    rows = own.shape[0]
    other = [rest[3].at[i * rows : (i + 1) * rows, :] for i in range(3)]
    zone, slot, group = place[0], place[1], place[2]
    piece = a.shape[1]
    for j, part in enumerate((a, b, c, d)):
        full[:, lanes(slot ^ j, piece)] = part[...].astype(F32)
    values = full[...]
    power = jnp.mean(values * values, axis=-1, keepdims=True)
    ready[...] = (values * lax.rsqrt(power + 1e-05) * gain[...][None, :]).astype(BF16)
    near = own.shape[0]
    half = own.shape[1] // 2
    for part, pieces in ((0, got), (1, other)):
        value = dot(ready[:, lanes(zone, near)], own[:, lanes(group ^ part, half)])
        for i, shift in enumerate(SHIFTS):
            source = lax.rem(zone - shift + 4, 4)
            value = value + dot(ready[:, lanes(source, near)], pieces[i][...])
        key_value[:, lanes(group ^ part, half)] = value.astype(BF16)
    held = full.shape[0] // BLOCK
    width = key_value.shape[1]
    for j in range(4):
        start, amount, begin = 0, 0, 0
        for r in range(4):
            here = owner[0, r] == (slot ^ j)
            amount = jnp.where(here, blocks[0, r], amount)
            begin = jnp.where(here, start, begin)
            start = start + blocks[0, r]
        for q in range(QCAP):
            row = jnp.clip(begin + q, 0, held - 1) * BLOCK
            chosen = key_value[pl.ds(pl.multiple_of(row, BLOCK), BLOCK), :]
            outs[j][q * BLOCK : (q + 1) * BLOCK, :] = jnp.where(
                q < amount, chosen, jnp.zeros((BLOCK, width), BF16)
            )


def hand_kernel(place, a, b, c, d, out):
    parts = [part[...].astype(F32) for part in (a, b, c, d)]
    ordered = []
    for source in range(4):
        j = place[1] ^ source
        value = jnp.where(j == 0, parts[0], parts[1])
        ordered.append(jnp.where(j < 2, value, jnp.where(j == 2, parts[2], parts[3])))
    out[...] = jnp.stack(ordered, axis=1).astype(BF16)


def near_plan(
    resid,
    moe_gain,
    attn_gain,
    gate_score,
    expert_ids,
    w_gate,
    w_up,
    w_down,
    shared_gate,
    shared_up,
    shared_down,
    w_kv,
    req_owner,
    req_blocks,
):
    rows, width = resid.shape
    zones = lax.axis_size("expert")
    slots = lax.axis_size("decode")
    capacity = 2 * rows // (zones // 2)
    piece = width // slots
    near = shared_gate.shape[0]
    hidden = shared_gate.shape[1] // zones
    half = hidden // 2
    total_rows = zones * rows
    routed_width = w_gate.shape[2]
    kv_width = w_kv.shape[1]
    group = lax.axis_index("groups")
    place = jnp.stack(
        [lax.axis_index("expert"), lax.axis_index("decode"), group]
    ).astype(jnp.int32)

    first = call(
        lambda *refs: first_kernel(capacity, *refs),
        [
            ((rows, width), BF16),
            ((rows + META, piece), BF16),
            ((rows, piece), BF16),
        ]
        + [((rows + META + half, piece), BF16)] * 3,
        [SMEM] + [VMEM] * 4 + [ANY],
        [pltpu.SemaphoreType.DMA((3,))],
        moved=6 << 20,
        name="first",
        vmem=58,
    )(
        place,
        resid,
        moe_gain,
        gate_score.reshape(1, rows),
        expert_ids.reshape(1, rows),
        shared_down,
    )
    moe_in, message, resid_share = first[:3]
    mixed_messages = first[3:6]
    second = call(
        second_kernel,
        [((near, 2 * hidden), BF16), ((hidden, piece), BF16)]
        + [((near, hidden), BF16)] * 3
        + [((near, kv_width // 2), BF16)],
        [SMEM] + [ANY] * 4,
        [pltpu.SemaphoreType.DMA((12,))],
        name="second",
        vmem=58,
    )(place, shared_gate, shared_up, shared_down, w_kv)
    own_weights, own_down, weight_messages, kv_half = second[0], second[1], second[2:5], second[5]

    mixed = [to_shift(values, s) for values, s in zip(mixed_messages, SHIFTS)]
    top = rows + META
    arrived = [values[:top] for values in mixed]
    got = [to_shift(values, s) for values, s in zip(weight_messages, SHIFTS)]
    joined = join(*got)
    other = swap_groups(joined)

    down_got = [values[top:] for values in mixed]
    down_other = swap_groups(join(*down_got))

    across = [lax.ppermute(values, "decode", SWAP_CHIP) for values in arrived]
    (token_half,) = call(
        half_kernel,
        [((total_rows, 2 * piece), BF16)],
        [SMEM] + [VMEM] * 7,
        name="half",
    )(after(place, joined), moe_in, *arrived, *across)
    token_rest = lax.ppermute(token_half, "decode", SWAP_CORE)

    kv_half = after(kv_half, joined)
    kv_got = [to_shift(kv_half, s) for s in SHIFTS]
    tokens, routed_hidden = call(
        routed_up_kernel,
        [((total_rows, width), BF16), ((total_rows, routed_width), BF16)],
        [SMEM] + [VMEM] * 4,
        flops=4 * total_rows * width * routed_width,
        moved=10 << 20,
        name="routed_up",
        vmem=22,
    )(place, token_half, token_rest, w_gate, w_up)
    (routed,) = call(
        routed_down_kernel,
        [((total_rows, width), BF16)],
        [SMEM] + [VMEM] * 6,
        flops=2 * total_rows * width * routed_width,
        moved=6 << 20,
        name="routed_down",
        vmem=16,
    )(
        place,
        routed_hidden,
        message,
        *[arrived[SHIFTS.index(s)] for s in range(1, zones)],
        w_down,
    )

    (first_half,) = call(
        gate_up_first_kernel,
        [((total_rows, half), BF16)],
        [SMEM] + [VMEM] * 5,
        flops=2 * total_rows * width * hidden,
        moved=4 << 20,
        name="gate_up_first",
        vmem=12,
    )(after(place, routed), tokens, own_weights, *got)
    (shared_hidden,) = call(
        gate_up_second_kernel,
        [((total_rows, hidden), BF16)],
        [SMEM] + [VMEM] * 4,
        flops=2 * total_rows * width * hidden,
        moved=4 << 20,
        name="gate_up_second",
        vmem=12,
    )(place, tokens, own_weights, first_half, other)
    kv_joined = join(*lax.optimization_barrier(tuple(kv_got) + (routed, shared_hidden))[:3])
    send, keep = call(
        down_kernel,
        [((total_rows, 2 * piece), BF16), ((total_rows, 2 * piece), F32)],
        [SMEM] + [VMEM] * 7,
        [pltpu.VMEM((hidden, width), BF16)],
        name="down",
        vmem=14,
    )(after(place, kv_joined), routed, shared_hidden, own_down, down_other, *down_got)
    beside = lax.ppermute(send, "decode", SWAP_CORE)
    kv_other = swap_groups(kv_joined)
    passed = call(
        pass_kernel,
        [((rows, piece), F32)] * 4 + [((rows, piece), BF16)] * 4,
        [VMEM] * 2,
        name="pass",
    )(keep, beside)
    crossed = {s: lax.ppermute(passed[4 + s], "decode", SWAP_CHIP) for s in SHIFTS + (0,)}
    returned = []
    for s in SHIFTS:
        (summed,) = call(add_kernel, [((rows, piece), BF16)], [VMEM] * 2, name="add")(
            passed[s], crossed[s]
        )
        returned.append(to_shift(summed, -s))
    layer_out, layer_rows = call(
        layer_kernel, [((rows, piece), BF16)] * 2, [VMEM] * 6, name="layer"
    )(resid_share, passed[0], crossed[0], *returned)

    handed = call(
        kv_kernel,
        [((QCAP * BLOCK, kv_width), BF16)] * 4,
        [SMEM] * 3 + [VMEM] * 10,
        [
            pltpu.VMEM((rows, width), F32),
            pltpu.VMEM((rows, kv_width), BF16),
            pltpu.VMEM((rows, width), BF16),
        ],
        name="kv",
        vmem=10,
    )(
        place,
        req_owner,
        req_blocks,
        attn_gain,
        *spread(layer_rows),
        w_kv,
        *kv_got,
        kv_other,
    )
    received = [handed[0]] + [
        lax.ppermute(values, "decode", pairs)
        for values, pairs in zip(handed[1:], (SWAP_CORE, SWAP_CHIP, SWAP_FAR))
    ]
    (kv_handed,) = call(
        hand_kernel,
        [((QCAP * BLOCK, slots, kv_width), BF16)],
        [SMEM] + [VMEM] * 4,
        name="hand",
    )(place, *received)
    return layer_out, kv_handed[None, None]


def on_device(*operands):
    resid = operands[0]
    zones = lax.axis_size("expert")
    holders = lax.axis_size("decode")
    fits = 2 * resid.shape[0] // (zones // 2) >= resid.shape[0]
    square = zones == holders == 4 and lax.axis_size("tensor") == 1
    if fits and square and lax.axis_size("groups") == 2:
        return near_plan(*operands)
    return wide_plan(*operands)


def solution(mesh):
    return jax.shard_map(
        on_device,
        mesh=mesh,
        in_specs=(
            P(("groups", "expert"), None),
            P(),
            P(),
            P(("groups", "expert")),
            P(("groups", "expert"), None),
            P("expert", None, ("decode", "tensor")),
            P("expert", None, ("decode", "tensor")),
            P("expert", ("decode", "tensor"), None),
            P("expert", ("decode", "tensor")),
            P("expert", ("decode", "tensor")),
            P(("decode", "tensor"), "expert"),
            P("expert", ("decode", "tensor")),
            P(("groups", "expert"), None),
            P(("groups", "expert"), None),
        ),
        out_specs=(
            P(("groups", "expert"), ("decode", "tensor")),
            P(("groups", "expert"), "decode", None, None, "tensor"),
        ),
        check_vma=False,
    )
```

```python
import jax
import jax.numpy as jnp
from jax import lax
from jax.experimental import pallas as pl
from jax.experimental.pallas import tpu as pltpu
from jax.sharding import PartitionSpec as P

BLOCK = 16
QCAP = 4


def rms_scale(values, gain):
    return values * lax.rsqrt(jnp.mean(values * values, axis=-1, keepdims=True) + 1e-05) * gain


def unpermute(slot_values, row_index):
    padded = jnp.concatenate(
        [slot_values, jnp.zeros((1, slot_values.shape[1]), jnp.float32)], axis=0
    )
    return padded[row_index]


def hand_over(key_value, req_owner, req_blocks):
    tok_rows, kv_width = key_value.shape
    owner_count = req_owner.shape[1]
    block_count = tok_rows // BLOCK
    owners = req_owner[0]
    counts = req_blocks[0]
    starts = jnp.cumsum(counts) - counts
    owner_index = jnp.arange(owner_count, dtype=jnp.int32)
    slot_index = jnp.arange(QCAP, dtype=jnp.int32)
    block_index = jnp.arange(block_count, dtype=jnp.int32)
    chosen = owners[:, None, None, None] == owner_index[None, :, None, None]
    chosen = chosen & (slot_index[None, None, :, None] < counts[:, None, None, None])
    chosen = chosen & (
        block_index[None, None, None, :]
        == starts[:, None, None, None] + slot_index[None, None, :, None]
    )
    choose = jnp.sum(chosen.astype(jnp.int32), axis=0).astype(jnp.bfloat16)
    kv_blocks = key_value.reshape(block_count, BLOCK, kv_width)
    sending = jnp.einsum(
        "oqb,bjw->qjow", choose, kv_blocks, preferred_element_type=jnp.float32
    ).astype(jnp.bfloat16)
    sending = sending.reshape(QCAP * BLOCK, owner_count, kv_width)
    received = lax.all_to_all(sending, "decode", split_axis=1, concat_axis=1, tiled=True)
    kv_handed = received.reshape(1, 1, QCAP * BLOCK, owner_count, kv_width)
    return kv_handed


def wide_plan(
    resid,
    moe_gain,
    attn_gain,
    gate_score,
    expert_ids,
    w_gate,
    w_up,
    w_down,
    shared_gate,
    shared_up,
    shared_down,
    w_kv,
    req_owner,
    req_blocks,
):
    tok_rows, feature_width = resid.shape
    expert_count = lax.axis_size("expert")
    pair_count = expert_count // 2
    capacity = 2 * tok_rows // pair_count
    group_size = lax.axis_size(("decode", "tensor"))
    piece_width = feature_width // group_size
    feature_start = lax.axis_index(("decode", "tensor")) * piece_width
    moe_in = rms_scale(resid.astype(jnp.float32), moe_gain).astype(jnp.bfloat16)
    routes = expert_ids[:, 0]
    onehot = (routes[:, None] == jnp.arange(pair_count, dtype=jnp.int32)[None, :]).astype(jnp.int32)
    slots = jnp.sum((jnp.cumsum(onehot, axis=0) - 1) * onehot, axis=1)
    kept = slots < capacity
    position = routes * capacity + slots
    row_index = jnp.where(kept, position, pair_count * capacity)
    selector = (
        position[None, :] == jnp.arange(pair_count * capacity, dtype=jnp.int32)[:, None]
    ) & kept[None, :]
    select_bf = selector.astype(jnp.bfloat16)
    packed = jnp.dot(select_bf, moe_in, preferred_element_type=jnp.float32).astype(jnp.bfloat16)
    packed = packed.reshape(pair_count, capacity, feature_width)
    outgoing = jnp.repeat(packed, 2, axis=0)
    incoming = lax.all_to_all(outgoing, "expert", split_axis=0, concat_axis=0, tiled=True)
    flat_in = incoming.reshape(expert_count * capacity, feature_width)
    gate_val = jnp.dot(flat_in, w_gate[0], preferred_element_type=jnp.float32)
    up_val = jnp.dot(flat_in, w_up[0], preferred_element_type=jnp.float32)
    hidden = (jax.nn.silu(gate_val) * up_val).astype(jnp.bfloat16)
    partial_flat = jnp.dot(hidden, w_down[0], preferred_element_type=jnp.float32).astype(
        jnp.bfloat16
    )
    returned = lax.all_to_all(
        partial_flat.reshape(expert_count, capacity, feature_width),
        "expert",
        split_axis=0,
        concat_axis=0,
        tiled=True,
    )
    pair_sums = jnp.sum(
        returned.reshape(pair_count, 2, capacity, feature_width).astype(jnp.float32), axis=1
    )
    routed_full = (
        unpermute(pair_sums.reshape(pair_count * capacity, feature_width), row_index)
        * gate_score[:, None]
    )
    columns = moe_in
    shared_gate_val = jnp.dot(
        columns,
        lax.all_gather(shared_gate, "expert", axis=0, tiled=True),
        preferred_element_type=jnp.float32,
    )
    shared_up_val = jnp.dot(
        columns,
        lax.all_gather(shared_up, "expert", axis=0, tiled=True),
        preferred_element_type=jnp.float32,
    )
    shared_hidden = (jax.nn.silu(shared_gate_val) * shared_up_val).astype(jnp.bfloat16)
    shared_out = jnp.dot(
        shared_hidden,
        lax.all_gather(shared_down, "expert", axis=1, tiled=True),
        preferred_element_type=jnp.float32,
    )
    total_terms = routed_full + shared_out
    summed_share = lax.psum_scatter(
        total_terms.astype(jnp.bfloat16), ("decode", "tensor"), scatter_dimension=1, tiled=True
    ).astype(jnp.float32)
    resid_share = lax.dynamic_slice_in_dim(resid, feature_start, piece_width, 1)
    layer_out = (resid_share.astype(jnp.float32) + summed_share).astype(jnp.bfloat16)
    full_rows = lax.all_gather(layer_out, ("decode", "tensor"), axis=1, tiled=True)
    attn_in = rms_scale(full_rows.astype(jnp.float32), attn_gain).astype(jnp.bfloat16)
    kv_width = w_kv.shape[1]
    columns = attn_in
    key_value = jnp.dot(
        columns,
        lax.all_gather(w_kv, "expert", axis=0, tiled=True),
        preferred_element_type=jnp.float32,
    ).astype(jnp.bfloat16)
    return layer_out, hand_over(key_value, req_owner, req_blocks)


SWAP_CORE = [(0, 1), (1, 0), (2, 3), (3, 2)]
SWAP_CHIP = [(0, 2), (2, 0), (1, 3), (3, 1)]
SWAP_FAR = [(0, 3), (3, 0), (1, 2), (2, 1)]
SWAP_GROUP = [(0, 1), (1, 0)]
SHIFTS = (2, 1, 3)
BF16 = jnp.bfloat16
F32 = jnp.float32
VMEM = pl.BlockSpec(memory_space=pltpu.VMEM)
SMEM = pl.BlockSpec(memory_space=pltpu.SMEM)
ANY = pl.BlockSpec(memory_space=pl.ANY)
META = 16


def call(body, outs, in_specs, scratch=(), flops=0, moved=0, name=None, vmem=8):
    return pl.pallas_call(
        body,
        out_shape=[jax.ShapeDtypeStruct(shape, kind) for shape, kind in outs],
        in_specs=in_specs,
        out_specs=[VMEM] * len(outs),
        scratch_shapes=list(scratch),
        compiler_params=pltpu.CompilerParams(vmem_limit_bytes=vmem << 20),
        cost_estimate=pl.CostEstimate(flops=0, bytes_accessed=0, transcendentals=0),
        name=name,
    )


def to_shift(values, shift):
    count = lax.axis_size("expert")
    return lax.ppermute(values, "expert", [(i, (i + shift) % count) for i in range(count)])


def after(values, *others):
    return lax.optimization_barrier((values,) + others)[0]


def swap_groups(values):
    return lax.ppermute(values, "groups", SWAP_GROUP)


def spread(values):
    across = lax.ppermute(values, "decode", SWAP_CHIP)
    beside = lax.ppermute(values, "decode", SWAP_CORE)
    far = lax.ppermute(across, "decode", SWAP_CORE)
    return values, beside, across, far


def lanes(index, size):
    return pl.ds(pl.multiple_of(index * size, 128), size)


def dot(a, b):
    return jnp.dot(a, b, preferred_element_type=F32)


def first_kernel(
    capacity, place, resid, gain, score, ids, down, moe_in, message, share, *rest
):
    both, sem = rest[:3], rest[3]
    top = message.shape[0]
    zone, slot, group = place[0], place[1], place[2]
    count = 4
    hidden = down.shape[0] // count
    half = hidden // 2
    copies = []

    def move(source, target):
        copies.append(pltpu.make_async_copy(source, target, sem.at[len(copies)]))

    for i, shift in enumerate(SHIFTS):
        start = lax.rem(zone + shift, count) * hidden + group * half
        move(down.at[pl.ds(pl.multiple_of(start, 128), half), :], both[i].at[top:, :])
    for copy in copies:
        copy.start()

    rows, width = resid.shape
    piece = message.shape[1]
    values = resid[...].astype(F32)
    power = jnp.mean(values * values, axis=-1, keepdims=True)
    moe_in[...] = (values * lax.rsqrt(power + 1e-05) * gain[...][None, :]).astype(BF16)
    message[:rows, :] = moe_in[:, lanes(slot, piece)]
    share[...] = resid[:, lanes(slot, piece)]
    first = lax.broadcasted_iota(jnp.int32, (rows, rows), 0)
    second = lax.broadcasted_iota(jnp.int32, (rows, rows), 1)
    across = jnp.broadcast_to(ids[...].astype(F32), (rows, rows))
    along = jnp.sum(jnp.where(first == second, across, 0.0), axis=1, keepdims=True)
    same = (along == across) & (first < second)
    slots = jnp.sum(jnp.where(same, 1.0, 0.0), axis=0, keepdims=True)
    scale = jnp.where(slots < capacity, score[...], 0.0)
    high = scale.astype(BF16)
    rest = scale - high.astype(F32)
    middle = rest.astype(BF16)
    low = (rest - middle.astype(F32)).astype(BF16)
    message[rows:, :] = jnp.zeros((META, piece), BF16)
    for i, part in enumerate((high, middle, low, ids[...].astype(F32).astype(BF16))):
        message[rows:, i * rows : (i + 1) * rows] = jnp.broadcast_to(part, (META, rows))
    for target in both:
        target[:top, :] = message[...]
    for copy in copies:
        copy.wait()


def second_kernel(place, gate, up, down, kv, own, own_down, *rest):
    messages, kv_half, sem = rest[:3], rest[3], rest[4]
    count = 4
    zone, group = place[0], place[2]
    hidden = gate.shape[1] // 4
    half = hidden // 2
    copies = []

    def move(source, target):
        copies.append(pltpu.make_async_copy(source, target, sem.at[len(copies)]))

    move(down.at[pl.ds(pl.multiple_of(zone * hidden, 128), hidden), :], own_down)
    for i, shift in enumerate(SHIFTS):
        start = lax.rem(zone + shift, count) * hidden + group * half
        for j, weights in enumerate((gate, up)):
            move(
                weights.at[:, pl.ds(pl.multiple_of(start, 128), half)],
                messages[i].at[:, j * half : (j + 1) * half],
            )
    start = group * kv_half.shape[1]
    move(kv.at[:, pl.ds(pl.multiple_of(start, 128), kv_half.shape[1])], kv_half)
    for part in range(2):
        start = zone * hidden + (group ^ part) * half
        for j, weights in enumerate((gate, up)):
            move(
                weights.at[:, pl.ds(pl.multiple_of(start, 128), half)],
                own.at[:, (2 * part + j) * half : (2 * part + j + 1) * half],
            )
    for copy in copies:
        copy.start()
    for copy in copies:
        copy.wait()


def silu(values):
    return values / (1.0 + jnp.exp(-values))


def join_kernel(*refs):
    out, row = refs[-1], 0
    for part in refs[:-1]:
        out[row : row + part.shape[0], :] = part[...]
        row += part.shape[0]


def join(*parts):
    rows = sum(part.shape[0] for part in parts)
    return call(
        join_kernel, [((rows, parts[0].shape[1]), BF16)], [VMEM] * len(parts), name="join"
    )(*parts)[0]


def part_kernel(a, b, c, tops, downs):
    top = tops.shape[0] // 3
    low = downs.shape[0] // 3
    for i, part in enumerate((a, b, c)):
        tops[i * top : (i + 1) * top, :] = part[:top, :]
        downs[i * low : (i + 1) * low, :] = part[top:, :]


def half_kernel(place, moe_in, a, b, c, across, out):
    own = (a, b, c)
    rows = moe_in.shape[0]
    top = across.shape[0] // 3
    piece = out.shape[1] // 2
    out[:rows, :piece] = moe_in[:, lanes(place[1], piece)]
    out[:rows, piece:] = moe_in[:, lanes(place[1] ^ 2, piece)]
    for i, shift in enumerate(SHIFTS):
        span = slice(shift * rows, (shift + 1) * rows)
        out[span, :piece] = own[i][:rows, :]
        out[span, piece:] = across[i * top : i * top + rows, :]


def routed_up_kernel(place, mine, theirs, gate, up, tokens, hidden):
    slot = place[1]
    piece = mine.shape[1] // 2
    for j in range(4):
        source = theirs if j % 2 else mine
        tokens[:, lanes(slot ^ j, piece)] = source[:, (j // 2) * piece : (j // 2 + 1) * piece]
    width = hidden.shape[1]
    step = 256
    for n in range(width // step):
        cols = slice(n * step, (n + 1) * step)
        gate_val = dot(tokens[...], gate[0, :, cols])
        up_val = dot(tokens[...], up[0, :, cols])
        hidden[:, cols] = (silu(gate_val) * up_val).astype(BF16)


def routed_down_kernel(place, hidden, *rest):
    messages, down, out = rest[:4], rest[4], rest[5]
    zone = place[0]
    rows = messages[0].shape[0] - META
    piece = messages[0].shape[1]
    diagonal = lax.broadcasted_iota(jnp.int32, (rows, rows), 0) == lax.broadcasted_iota(
        jnp.int32, (rows, rows), 1
    )
    mine = (zone // 2).astype(F32)
    scales = []
    for source in messages:
        info = source[rows : rows + META, :].astype(F32)[:1]
        value = info[:, :rows] + info[:, rows : 2 * rows] + info[:, 2 * rows : 3 * rows]
        value = jnp.where(info[:, 3 * rows : 4 * rows] == mine, value, 0.0)
        scales.append(jnp.sum(jnp.where(diagonal, value, 0.0), axis=1, keepdims=True))
    scale = jnp.concatenate(scales, axis=0)
    for n in range(out.shape[1] // piece):
        cols = slice(n * piece, (n + 1) * piece)
        out[:, cols] = (dot(hidden[...], down[0, :, cols]) * scale).astype(BF16)


def gate_up_half(place, tokens, own, pieces, part):
    zone = place[0]
    near = own.shape[0]
    width = own.shape[1] // 2
    half = width // 2
    both = dot(tokens[:, lanes(zone, near)], own[:, part * width : (part + 1) * width])
    for i, shift in enumerate(SHIFTS):
        source = lax.rem(zone - shift + 4, 4)
        both = both + dot(tokens[:, lanes(source, near)], pieces[i][...])
    return (silu(both[:, :half]) * both[:, half:]).astype(BF16)


def gate_up_first_kernel(place, tokens, own, a, b, c, hidden):
    hidden[...] = gate_up_half(place, tokens, own, (a, b, c), 0)


def gate_up_second_kernel(place, tokens, own, first, rest, hidden):
    half = first.shape[1]
    near = own.shape[0]
    a, b, c = [rest.at[i * near : (i + 1) * near, :] for i in range(3)]
    hidden[:, lanes(place[2], half)] = first[...]
    hidden[:, lanes(1 - place[2], half)] = gate_up_half(place, tokens, own, (a, b, c), 1)


def down_kernel(place, routed, hidden, own, other, a, b, c, send, keep, weights):
    zone, slot, group = place[0], place[1], place[2]
    piece = own.shape[1]
    half = own.shape[0] // 2
    weights[:, lanes(zone, piece)] = own[...]
    for i, (shift, part) in enumerate(zip(SHIFTS, (a, b, c))):
        cols = lanes(lax.rem(zone - shift + 4, 4), piece)
        weights[pl.ds(pl.multiple_of(group * half, 128), half), cols] = part[-half:, :]
        weights[pl.ds(pl.multiple_of((1 - group) * half, 128), half), cols] = other[
            i * half : (i + 1) * half, :
        ]
    for target, parts in ((send, (1, 3)), (keep, (0, 2))):
        for i, j in enumerate(parts):
            cols = lanes(slot ^ j, piece)
            value = routed[:, cols].astype(F32) + dot(hidden[...], weights[:, cols])
            target[:, i * piece : (i + 1) * piece] = value.astype(target.dtype)


def pass_kernel(keep, beside, *outs):
    rows, piece = outs[0].shape
    for shard in range(4):
        span = slice(shard * rows, (shard + 1) * rows)
        value = keep[span, :].astype(F32) + beside[span, :].astype(F32)
        outs[shard][...] = value[:, :piece]
        outs[4 + shard][...] = value[:, piece:].astype(BF16)


def add_kernel(a, b, out):
    out[...] = (a[...] + b[...].astype(F32)).astype(BF16)


def layer_kernel(resid, own, crossed, a, b, c, out, again):
    value = own[...] + crossed[...].astype(F32) + a[...].astype(F32) + b[...].astype(F32) + c[...].astype(F32)
    value = value + resid[...].astype(F32)
    out[...] = value.astype(BF16)
    again[...] = out[...]


def kv_kernel(place, owner, blocks, gain, a, b, c, d, own, *rest):
    got, outs = rest[:3], rest[4:8]
    full, key_value, ready = rest[8:]
    rows = own.shape[0]
    other = [rest[3].at[i * rows : (i + 1) * rows, :] for i in range(3)]
    zone, slot, group = place[0], place[1], place[2]
    piece = a.shape[1]
    for j, part in enumerate((a, b, c, d)):
        full[:, lanes(slot ^ j, piece)] = part[...].astype(F32)
    values = full[...]
    power = jnp.mean(values * values, axis=-1, keepdims=True)
    ready[...] = (values * lax.rsqrt(power + 1e-05) * gain[...][None, :]).astype(BF16)
    near = own.shape[0]
    half = own.shape[1] // 2
    for part, pieces in ((0, got), (1, other)):
        value = dot(ready[:, lanes(zone, near)], own[:, lanes(group ^ part, half)])
        for i, shift in enumerate(SHIFTS):
            source = zone ^ shift
            value = value + dot(ready[:, lanes(source, near)], pieces[i][...])
        key_value[:, lanes(group ^ part, half)] = value.astype(BF16)
    held = full.shape[0] // BLOCK
    width = key_value.shape[1]
    for j in range(4):
        start, amount, begin = 0, 0, 0
        for r in range(4):
            here = owner[0, r] == (slot ^ j)
            amount = jnp.where(here, blocks[0, r], amount)
            begin = jnp.where(here, start, begin)
            start = start + blocks[0, r]
        for q in range(QCAP):
            row = jnp.clip(begin + q, 0, held - 1) * BLOCK
            chosen = key_value[pl.ds(pl.multiple_of(row, BLOCK), BLOCK), :]
            outs[j][q * BLOCK : (q + 1) * BLOCK, :] = jnp.where(
                q < amount, chosen, jnp.zeros((BLOCK, width), BF16)
            )


def hand_kernel(place, a, b, c, d, out):
    parts = [part[...].astype(F32) for part in (a, b, c, d)]
    ordered = []
    for source in range(4):
        j = place[1] ^ source
        value = jnp.where(j == 0, parts[0], parts[1])
        ordered.append(jnp.where(j < 2, value, jnp.where(j == 2, parts[2], parts[3])))
    out[...] = jnp.stack(ordered, axis=1).astype(BF16)


def near_plan(
    resid,
    moe_gain,
    attn_gain,
    gate_score,
    expert_ids,
    w_gate,
    w_up,
    w_down,
    shared_gate,
    shared_up,
    shared_down,
    w_kv,
    req_owner,
    req_blocks,
):
    rows, width = resid.shape
    zones = lax.axis_size("expert")
    slots = lax.axis_size("decode")
    capacity = 2 * rows // (zones // 2)
    piece = width // slots
    near = shared_gate.shape[0]
    hidden = shared_gate.shape[1] // zones
    half = hidden // 2
    total_rows = zones * rows
    routed_width = w_gate.shape[2]
    kv_width = w_kv.shape[1]
    group = lax.axis_index("groups")
    place = jnp.stack(
        [lax.axis_index("expert"), lax.axis_index("decode"), group]
    ).astype(jnp.int32)

    first = call(
        lambda *refs: first_kernel(capacity, *refs),
        [
            ((rows, width), BF16),
            ((rows + META, piece), BF16),
            ((rows, piece), BF16),
        ]
        + [((rows + META + half, piece), BF16)] * 3,
        [SMEM] + [VMEM] * 4 + [ANY],
        [pltpu.SemaphoreType.DMA((3,))],
        moved=6 << 20,
        name="first",
        vmem=58,
    )(
        place,
        resid,
        moe_gain,
        gate_score.reshape(1, rows),
        expert_ids.reshape(1, rows),
        shared_down,
    )
    moe_in, message, resid_share = first[:3]
    mixed_messages = first[3:6]
    second = call(
        second_kernel,
        [((near, 2 * hidden), BF16), ((hidden, piece), BF16)]
        + [((near, hidden), BF16)] * 3
        + [((near, kv_width // 2), BF16)],
        [SMEM] + [ANY] * 4,
        [pltpu.SemaphoreType.DMA((12,))],
        name="second",
        vmem=58,
    )(place, shared_gate, shared_up, shared_down, w_kv)
    own_weights, own_down, weight_messages, kv_half = second[0], second[1], second[2:5], second[5]

    mixed = [to_shift(values, s) for values, s in zip(mixed_messages, SHIFTS)]
    got = [to_shift(values, s) for values, s in zip(weight_messages, SHIFTS)]
    tops, downs = call(
        part_kernel,
        [((3 * (rows + META), piece), BF16), ((3 * half, piece), BF16)],
        [VMEM] * 3,
        name="part",
    )(*lax.optimization_barrier((*mixed, got[0]))[:3])
    down_other = swap_groups(downs)
    joined = join(*lax.optimization_barrier(tuple(got) + (down_other,))[:3])
    other = swap_groups(joined)


    across = lax.ppermute(tops, "decode", SWAP_CHIP)
    (token_half,) = call(
        half_kernel,
        [((total_rows, 2 * piece), BF16)],
        [SMEM] + [VMEM] * 5,
        name="half",
    )(after(place, joined), moe_in, *mixed, across)
    token_rest = lax.ppermute(token_half, "decode", SWAP_CORE)

    tokens, routed_hidden = call(
        routed_up_kernel,
        [((total_rows, width), BF16), ((total_rows, routed_width), BF16)],
        [SMEM] + [VMEM] * 4,
        flops=4 * total_rows * width * routed_width,
        moved=10 << 20,
        name="routed_up",
        vmem=22,
    )(place, token_half, token_rest, w_gate, w_up)
    (routed,) = call(
        routed_down_kernel,
        [((total_rows, width), BF16)],
        [SMEM] + [VMEM] * 6,
        flops=2 * total_rows * width * routed_width,
        moved=6 << 20,
        name="routed_down",
        vmem=16,
    )(
        place,
        routed_hidden,
        message,
        *[mixed[SHIFTS.index(s)] for s in range(1, zones)],
        w_down,
    )

    (first_half,) = call(
        gate_up_first_kernel,
        [((total_rows, half), BF16)],
        [SMEM] + [VMEM] * 5,
        flops=2 * total_rows * width * hidden,
        moved=4 << 20,
        name="gate_up_first",
        vmem=12,
    )(after(place, routed), tokens, own_weights, *got)
    kv_half = after(kv_half, joined)
    kv_far = lax.ppermute(kv_half, "expert", SWAP_CHIP)
    kv_near = lax.ppermute(kv_half, "expert", SWAP_CORE)
    kv_got = [kv_far, kv_near, lax.ppermute(after(kv_far, first_half), "expert", SWAP_CORE)]
    (shared_hidden,) = call(
        gate_up_second_kernel,
        [((total_rows, hidden), BF16)],
        [SMEM] + [VMEM] * 4,
        flops=2 * total_rows * width * hidden,
        moved=4 << 20,
        name="gate_up_second",
        vmem=12,
    )(place, tokens, own_weights, first_half, other)
    kv_joined = join(*lax.optimization_barrier(tuple(kv_got) + (routed, shared_hidden))[:3])
    send, keep = call(
        down_kernel,
        [((total_rows, 2 * piece), BF16), ((total_rows, 2 * piece), F32)],
        [SMEM] + [VMEM] * 7,
        [pltpu.VMEM((hidden, width), BF16)],
        name="down",
        vmem=14,
    )(after(place, kv_joined), routed, shared_hidden, own_down, down_other, *mixed)
    beside = lax.ppermute(send, "decode", SWAP_CORE)
    kv_other = swap_groups(kv_joined)
    passed = call(
        pass_kernel,
        [((rows, piece), F32)] * 4 + [((rows, piece), BF16)] * 4,
        [VMEM] * 2,
        name="pass",
    )(keep, beside)
    crossed = {s: lax.ppermute(passed[4 + s], "decode", SWAP_CHIP) for s in SHIFTS + (0,)}
    returned = []
    for s in SHIFTS:
        (summed,) = call(add_kernel, [((rows, piece), BF16)], [VMEM] * 2, name="add")(
            passed[s], crossed[s]
        )
        returned.append(to_shift(summed, -s))
    layer_out, layer_rows = call(
        layer_kernel, [((rows, piece), BF16)] * 2, [VMEM] * 6, name="layer"
    )(resid_share, passed[0], crossed[0], *returned)

    handed = call(
        kv_kernel,
        [((QCAP * BLOCK, kv_width), BF16)] * 4,
        [SMEM] * 3 + [VMEM] * 10,
        [
            pltpu.VMEM((rows, width), F32),
            pltpu.VMEM((rows, kv_width), BF16),
            pltpu.VMEM((rows, width), BF16),
        ],
        name="kv",
        vmem=10,
    )(
        place,
        req_owner,
        req_blocks,
        attn_gain,
        *spread(layer_rows),
        w_kv,
        *kv_got,
        kv_other,
    )
    received = [handed[0]] + [
        lax.ppermute(values, "decode", pairs)
        for values, pairs in zip(handed[1:], (SWAP_CORE, SWAP_CHIP, SWAP_FAR))
    ]
    (kv_handed,) = call(
        hand_kernel,
        [((QCAP * BLOCK, slots, kv_width), BF16)],
        [SMEM] + [VMEM] * 4,
        name="hand",
    )(place, *received)
    return layer_out, kv_handed[None, None]


def on_device(*operands):
    resid = operands[0]
    zones = lax.axis_size("expert")
    holders = lax.axis_size("decode")
    fits = 2 * resid.shape[0] // (zones // 2) >= resid.shape[0]
    square = zones == holders == 4 and lax.axis_size("tensor") == 1
    if fits and square and lax.axis_size("groups") == 2:
        return near_plan(*operands)
    return wide_plan(*operands)


def solution(mesh):
    return jax.shard_map(
        on_device,
        mesh=mesh,
        in_specs=(
            P(("groups", "expert"), None),
            P(),
            P(),
            P(("groups", "expert")),
            P(("groups", "expert"), None),
            P("expert", None, ("decode", "tensor")),
            P("expert", None, ("decode", "tensor")),
            P("expert", ("decode", "tensor"), None),
            P("expert", ("decode", "tensor")),
            P("expert", ("decode", "tensor")),
            P(("decode", "tensor"), "expert"),
            P("expert", ("decode", "tensor")),
            P(("groups", "expert"), None),
            P(("groups", "expert"), None),
        ),
        out_specs=(
            P(("groups", "expert"), ("decode", "tensor")),
            P(("groups", "expert"), "decode", None, None, "tensor"),
        ),
        check_vma=False,
    )
```

```python
import jax
import jax.numpy as jnp
from jax import lax
from jax.experimental import pallas as pl
from jax.experimental.pallas import tpu as pltpu
from jax.sharding import PartitionSpec as P

BLOCK = 16
QCAP = 4


def rms_scale(values, gain):
    return values * lax.rsqrt(jnp.mean(values * values, axis=-1, keepdims=True) + 1e-05) * gain


def unpermute(slot_values, row_index):
    padded = jnp.concatenate(
        [slot_values, jnp.zeros((1, slot_values.shape[1]), jnp.float32)], axis=0
    )
    return padded[row_index]


def hand_over(key_value, req_owner, req_blocks):
    tok_rows, kv_width = key_value.shape
    owner_count = req_owner.shape[1]
    block_count = tok_rows // BLOCK
    owners = req_owner[0]
    counts = req_blocks[0]
    starts = jnp.cumsum(counts) - counts
    owner_index = jnp.arange(owner_count, dtype=jnp.int32)
    slot_index = jnp.arange(QCAP, dtype=jnp.int32)
    block_index = jnp.arange(block_count, dtype=jnp.int32)
    chosen = owners[:, None, None, None] == owner_index[None, :, None, None]
    chosen = chosen & (slot_index[None, None, :, None] < counts[:, None, None, None])
    chosen = chosen & (
        block_index[None, None, None, :]
        == starts[:, None, None, None] + slot_index[None, None, :, None]
    )
    choose = jnp.sum(chosen.astype(jnp.int32), axis=0).astype(jnp.bfloat16)
    kv_blocks = key_value.reshape(block_count, BLOCK, kv_width)
    sending = jnp.einsum(
        "oqb,bjw->qjow", choose, kv_blocks, preferred_element_type=jnp.float32
    ).astype(jnp.bfloat16)
    sending = sending.reshape(QCAP * BLOCK, owner_count, kv_width)
    received = lax.all_to_all(sending, "decode", split_axis=1, concat_axis=1, tiled=True)
    kv_handed = received.reshape(1, 1, QCAP * BLOCK, owner_count, kv_width)
    return kv_handed


def wide_plan(
    resid,
    moe_gain,
    attn_gain,
    gate_score,
    expert_ids,
    w_gate,
    w_up,
    w_down,
    shared_gate,
    shared_up,
    shared_down,
    w_kv,
    req_owner,
    req_blocks,
):
    tok_rows, feature_width = resid.shape
    expert_count = lax.axis_size("expert")
    pair_count = expert_count // 2
    capacity = 2 * tok_rows // pair_count
    group_size = lax.axis_size(("decode", "tensor"))
    piece_width = feature_width // group_size
    feature_start = lax.axis_index(("decode", "tensor")) * piece_width
    moe_in = rms_scale(resid.astype(jnp.float32), moe_gain).astype(jnp.bfloat16)
    routes = expert_ids[:, 0]
    onehot = (routes[:, None] == jnp.arange(pair_count, dtype=jnp.int32)[None, :]).astype(jnp.int32)
    slots = jnp.sum((jnp.cumsum(onehot, axis=0) - 1) * onehot, axis=1)
    kept = slots < capacity
    position = routes * capacity + slots
    row_index = jnp.where(kept, position, pair_count * capacity)
    selector = (
        position[None, :] == jnp.arange(pair_count * capacity, dtype=jnp.int32)[:, None]
    ) & kept[None, :]
    select_bf = selector.astype(jnp.bfloat16)
    packed = jnp.dot(select_bf, moe_in, preferred_element_type=jnp.float32).astype(jnp.bfloat16)
    packed = packed.reshape(pair_count, capacity, feature_width)
    outgoing = jnp.repeat(packed, 2, axis=0)
    incoming = lax.all_to_all(outgoing, "expert", split_axis=0, concat_axis=0, tiled=True)
    flat_in = incoming.reshape(expert_count * capacity, feature_width)
    gate_val = jnp.dot(flat_in, w_gate[0], preferred_element_type=jnp.float32)
    up_val = jnp.dot(flat_in, w_up[0], preferred_element_type=jnp.float32)
    hidden = (jax.nn.silu(gate_val) * up_val).astype(jnp.bfloat16)
    partial_flat = jnp.dot(hidden, w_down[0], preferred_element_type=jnp.float32).astype(
        jnp.bfloat16
    )
    returned = lax.all_to_all(
        partial_flat.reshape(expert_count, capacity, feature_width),
        "expert",
        split_axis=0,
        concat_axis=0,
        tiled=True,
    )
    pair_sums = jnp.sum(
        returned.reshape(pair_count, 2, capacity, feature_width).astype(jnp.float32), axis=1
    )
    routed_full = (
        unpermute(pair_sums.reshape(pair_count * capacity, feature_width), row_index)
        * gate_score[:, None]
    )
    columns = moe_in
    shared_gate_val = jnp.dot(
        columns,
        lax.all_gather(shared_gate, "expert", axis=0, tiled=True),
        preferred_element_type=jnp.float32,
    )
    shared_up_val = jnp.dot(
        columns,
        lax.all_gather(shared_up, "expert", axis=0, tiled=True),
        preferred_element_type=jnp.float32,
    )
    shared_hidden = (jax.nn.silu(shared_gate_val) * shared_up_val).astype(jnp.bfloat16)
    shared_out = jnp.dot(
        shared_hidden,
        lax.all_gather(shared_down, "expert", axis=1, tiled=True),
        preferred_element_type=jnp.float32,
    )
    total_terms = routed_full + shared_out
    summed_share = lax.psum_scatter(
        total_terms.astype(jnp.bfloat16), ("decode", "tensor"), scatter_dimension=1, tiled=True
    ).astype(jnp.float32)
    resid_share = lax.dynamic_slice_in_dim(resid, feature_start, piece_width, 1)
    layer_out = (resid_share.astype(jnp.float32) + summed_share).astype(jnp.bfloat16)
    full_rows = lax.all_gather(layer_out, ("decode", "tensor"), axis=1, tiled=True)
    attn_in = rms_scale(full_rows.astype(jnp.float32), attn_gain).astype(jnp.bfloat16)
    kv_width = w_kv.shape[1]
    columns = attn_in
    key_value = jnp.dot(
        columns,
        lax.all_gather(w_kv, "expert", axis=0, tiled=True),
        preferred_element_type=jnp.float32,
    ).astype(jnp.bfloat16)
    return layer_out, hand_over(key_value, req_owner, req_blocks)


SWAP_CORE = [(0, 1), (1, 0), (2, 3), (3, 2)]
SWAP_CHIP = [(0, 2), (2, 0), (1, 3), (3, 1)]
SWAP_FAR = [(0, 3), (3, 0), (1, 2), (2, 1)]
SWAP_GROUP = [(0, 1), (1, 0)]
SHIFTS = (2, 1, 3)
BF16 = jnp.bfloat16
F32 = jnp.float32
VMEM = pl.BlockSpec(memory_space=pltpu.VMEM)
SMEM = pl.BlockSpec(memory_space=pltpu.SMEM)
ANY = pl.BlockSpec(memory_space=pl.ANY)
META = 16


def call(body, outs, in_specs, scratch=(), flops=0, moved=0, name=None, vmem=8):
    return pl.pallas_call(
        body,
        out_shape=[jax.ShapeDtypeStruct(shape, kind) for shape, kind in outs],
        in_specs=in_specs,
        out_specs=[VMEM] * len(outs),
        scratch_shapes=list(scratch),
        compiler_params=pltpu.CompilerParams(vmem_limit_bytes=vmem << 20),
        cost_estimate=pl.CostEstimate(flops=0, bytes_accessed=0, transcendentals=0),
        name=name,
    )


def to_shift(values, shift):
    count = lax.axis_size("expert")
    return lax.ppermute(values, "expert", [(i, (i + shift) % count) for i in range(count)])


def after(values, *others):
    return lax.optimization_barrier((values,) + others)[0]


def swap_groups(values):
    return lax.ppermute(values, "groups", SWAP_GROUP)


def spread(values):
    across = lax.ppermute(values, "decode", SWAP_CHIP)
    beside = lax.ppermute(values, "decode", SWAP_CORE)
    far = lax.ppermute(across, "decode", SWAP_CORE)
    return values, beside, across, far


def lanes(index, size):
    return pl.ds(pl.multiple_of(index * size, 128), size)


def dot(a, b):
    return jnp.dot(a, b, preferred_element_type=F32)


def first_kernel(
    capacity, place, resid, gain, score, ids, down, moe_in, message, share, *rest
):
    both, sem = rest[:3], rest[3]
    top = message.shape[0]
    zone, slot, group = place[0], place[1], place[2]
    count = 4
    hidden = down.shape[0] // count
    half = hidden // 2
    copies = []

    def move(source, target):
        copies.append(pltpu.make_async_copy(source, target, sem.at[len(copies)]))

    for i, shift in enumerate(SHIFTS):
        start = lax.rem(zone + shift, count) * hidden + group * half
        move(down.at[pl.ds(pl.multiple_of(start, 128), half), :], both[i].at[top:, :])
    for copy in copies:
        copy.start()

    rows, width = resid.shape
    piece = message.shape[1]
    values = resid[...].astype(F32)
    power = jnp.mean(values * values, axis=-1, keepdims=True)
    moe_in[...] = (values * lax.rsqrt(power + 1e-05) * gain[...][None, :]).astype(BF16)
    message[:rows, :] = moe_in[:, lanes(slot, piece)]
    share[...] = resid[:, lanes(slot, piece)]
    first = lax.broadcasted_iota(jnp.int32, (rows, rows), 0)
    second = lax.broadcasted_iota(jnp.int32, (rows, rows), 1)
    across = jnp.broadcast_to(ids[...].astype(F32), (rows, rows))
    along = jnp.sum(jnp.where(first == second, across, 0.0), axis=1, keepdims=True)
    same = (along == across) & (first < second)
    slots = jnp.sum(jnp.where(same, 1.0, 0.0), axis=0, keepdims=True)
    scale = jnp.where(slots < capacity, score[...], 0.0)
    high = scale.astype(BF16)
    rest = scale - high.astype(F32)
    middle = rest.astype(BF16)
    low = (rest - middle.astype(F32)).astype(BF16)
    message[rows:, :] = jnp.zeros((META, piece), BF16)
    for i, part in enumerate((high, middle, low, ids[...].astype(F32).astype(BF16))):
        message[rows:, i * rows : (i + 1) * rows] = jnp.broadcast_to(part, (META, rows))
    for target in both:
        target[:top, :] = message[...]
    for copy in copies:
        copy.wait()


def second_kernel(place, gate, up, down, kv, own, own_down, *rest):
    messages, kv_half, sem = rest[:3], rest[3], rest[4]
    count = 4
    zone, group = place[0], place[2]
    hidden = gate.shape[1] // 4
    half = hidden // 2
    copies = []

    def move(source, target):
        copies.append(pltpu.make_async_copy(source, target, sem.at[len(copies)]))

    move(down.at[pl.ds(pl.multiple_of(zone * hidden, 128), hidden), :], own_down)
    for i, shift in enumerate(SHIFTS):
        start = lax.rem(zone + shift, count) * hidden + group * half
        for j, weights in enumerate((gate, up)):
            move(
                weights.at[:, pl.ds(pl.multiple_of(start, 128), half)],
                messages[i].at[:, j * half : (j + 1) * half],
            )
    start = group * kv_half.shape[1]
    move(kv.at[:, pl.ds(pl.multiple_of(start, 128), kv_half.shape[1])], kv_half)
    for part in range(2):
        start = zone * hidden + (group ^ part) * half
        for j, weights in enumerate((gate, up)):
            move(
                weights.at[:, pl.ds(pl.multiple_of(start, 128), half)],
                own.at[:, (2 * part + j) * half : (2 * part + j + 1) * half],
            )
    for copy in copies:
        copy.start()
    for copy in copies:
        copy.wait()


def silu(values):
    return values / (1.0 + jnp.exp(-values))


def join_kernel(*refs):
    out, row = refs[-1], 0
    for part in refs[:-1]:
        out[row : row + part.shape[0], :] = part[...]
        row += part.shape[0]


def join(*parts):
    rows = sum(part.shape[0] for part in parts)
    return call(
        join_kernel, [((rows, parts[0].shape[1]), BF16)], [VMEM] * len(parts), name="join"
    )(*parts)[0]


def part_kernel(a, b, c, tops, downs):
    top = tops.shape[0] // 3
    low = downs.shape[0] // 3
    for i, part in enumerate((a, b, c)):
        tops[i * top : (i + 1) * top, :] = part[:top, :]
        downs[i * low : (i + 1) * low, :] = part[top:, :]


def half_kernel(place, moe_in, a, b, c, across, out):
    own = (a, b, c)
    rows = moe_in.shape[0]
    top = across.shape[0] // 3
    piece = out.shape[1] // 2
    out[:rows, :piece] = moe_in[:, lanes(place[1], piece)]
    out[:rows, piece:] = moe_in[:, lanes(place[1] ^ 2, piece)]
    for i, shift in enumerate(SHIFTS):
        span = slice(shift * rows, (shift + 1) * rows)
        out[span, :piece] = own[i][:rows, :]
        out[span, piece:] = across[i * top : i * top + rows, :]


def routed_up_kernel(place, mine, theirs, gate, up, tokens, hidden):
    slot = place[1]
    piece = mine.shape[1] // 2
    for j in range(4):
        source = theirs if j % 2 else mine
        tokens[:, lanes(slot ^ j, piece)] = source[:, (j // 2) * piece : (j // 2 + 1) * piece]
    width = hidden.shape[1]
    step = 256
    for n in range(width // step):
        cols = slice(n * step, (n + 1) * step)
        gate_val = dot(tokens[...], gate[0, :, cols])
        up_val = dot(tokens[...], up[0, :, cols])
        hidden[:, cols] = (silu(gate_val) * up_val).astype(BF16)


def routed_down_kernel(place, hidden, *rest):
    messages, down, out = rest[:4], rest[4], rest[5]
    zone = place[0]
    rows = messages[0].shape[0] - META
    piece = messages[0].shape[1]
    diagonal = lax.broadcasted_iota(jnp.int32, (rows, rows), 0) == lax.broadcasted_iota(
        jnp.int32, (rows, rows), 1
    )
    mine = (zone // 2).astype(F32)
    scales = []
    for source in messages:
        info = source[rows : rows + META, :].astype(F32)[:1]
        value = info[:, :rows] + info[:, rows : 2 * rows] + info[:, 2 * rows : 3 * rows]
        value = jnp.where(info[:, 3 * rows : 4 * rows] == mine, value, 0.0)
        scales.append(jnp.sum(jnp.where(diagonal, value, 0.0), axis=1, keepdims=True))
    scale = jnp.concatenate(scales, axis=0)
    for n in range(out.shape[1] // piece):
        cols = slice(n * piece, (n + 1) * piece)
        out[:, cols] = (dot(hidden[...], down[0, :, cols]) * scale).astype(BF16)


def gate_up_half(place, tokens, own, pieces, part):
    zone = place[0]
    near = own.shape[0]
    width = own.shape[1] // 2
    half = width // 2
    both = dot(tokens[:, lanes(zone, near)], own[:, part * width : (part + 1) * width])
    for i, shift in enumerate(SHIFTS):
        source = lax.rem(zone - shift + 4, 4)
        both = both + dot(tokens[:, lanes(source, near)], pieces[i][...])
    return (silu(both[:, :half]) * both[:, half:]).astype(BF16)


def gate_up_first_kernel(place, tokens, own, a, b, c, hidden):
    hidden[...] = gate_up_half(place, tokens, own, (a, b, c), 0)


def gate_up_second_kernel(place, tokens, own, first, a, rest, hidden):
    half = first.shape[1]
    near = own.shape[0]
    b, c = rest.at[:near, :], rest.at[near:, :]
    hidden[:, lanes(place[2], half)] = first[...]
    hidden[:, lanes(1 - place[2], half)] = gate_up_half(place, tokens, own, (a, b, c), 1)


def down_kernel(place, routed, hidden, own, other, a, b, c, send, keep, weights):
    zone, slot, group = place[0], place[1], place[2]
    piece = own.shape[1]
    half = own.shape[0] // 2
    weights[:, lanes(zone, piece)] = own[...]
    for i, (shift, part) in enumerate(zip(SHIFTS, (a, b, c))):
        cols = lanes(lax.rem(zone - shift + 4, 4), piece)
        weights[pl.ds(pl.multiple_of(group * half, 128), half), cols] = part[-half:, :]
        weights[pl.ds(pl.multiple_of((1 - group) * half, 128), half), cols] = other[
            i * half : (i + 1) * half, :
        ]
    for target, parts in ((send, (1, 3)), (keep, (0, 2))):
        for i, j in enumerate(parts):
            cols = lanes(slot ^ j, piece)
            value = routed[:, cols].astype(F32) + dot(hidden[...], weights[:, cols])
            target[:, i * piece : (i + 1) * piece] = value.astype(target.dtype)


def pass_kernel(keep, beside, *outs):
    rows, piece = outs[0].shape
    for shard in range(4):
        span = slice(shard * rows, (shard + 1) * rows)
        value = keep[span, :].astype(F32) + beside[span, :].astype(F32)
        outs[shard][...] = value[:, :piece]
        outs[4 + shard][...] = value[:, piece:].astype(BF16)


def add_kernel(a, b, out):
    out[...] = (a[...] + b[...].astype(F32)).astype(BF16)


def layer_kernel(resid, own, crossed, a, b, c, out, again):
    value = own[...] + crossed[...].astype(F32) + a[...].astype(F32) + b[...].astype(F32) + c[...].astype(F32)
    value = value + resid[...].astype(F32)
    out[...] = value.astype(BF16)
    again[...] = out[...]


def kv_kernel(place, owner, blocks, gain, a, b, c, d, own, *rest):
    got, outs = rest[:3], rest[5:9]
    full, key_value, ready = rest[9:]
    rows = own.shape[0]
    other = [rest[3].at[:rows, :], rest[3].at[rows:, :], rest[4]]
    zone, slot, group = place[0], place[1], place[2]
    piece = a.shape[1]
    for j, part in enumerate((a, b, c, d)):
        full[:, lanes(slot ^ j, piece)] = part[...].astype(F32)
    values = full[...]
    power = jnp.mean(values * values, axis=-1, keepdims=True)
    ready[...] = (values * lax.rsqrt(power + 1e-05) * gain[...][None, :]).astype(BF16)
    near = own.shape[0]
    half = own.shape[1] // 2
    for part, pieces in ((0, got), (1, other)):
        value = dot(ready[:, lanes(zone, near)], own[:, lanes(group ^ part, half)])
        for i, shift in enumerate(SHIFTS):
            source = zone ^ shift
            value = value + dot(ready[:, lanes(source, near)], pieces[i][...])
        key_value[:, lanes(group ^ part, half)] = value.astype(BF16)
    held = full.shape[0] // BLOCK
    width = key_value.shape[1]
    for j in range(4):
        start, amount, begin = 0, 0, 0
        for r in range(4):
            here = owner[0, r] == (slot ^ j)
            amount = jnp.where(here, blocks[0, r], amount)
            begin = jnp.where(here, start, begin)
            start = start + blocks[0, r]
        for q in range(QCAP):
            row = jnp.clip(begin + q, 0, held - 1) * BLOCK
            chosen = key_value[pl.ds(pl.multiple_of(row, BLOCK), BLOCK), :]
            outs[j][q * BLOCK : (q + 1) * BLOCK, :] = jnp.where(
                q < amount, chosen, jnp.zeros((BLOCK, width), BF16)
            )


def hand_kernel(place, a, b, c, d, out):
    parts = [part[...].astype(F32) for part in (a, b, c, d)]
    ordered = []
    for source in range(4):
        j = place[1] ^ source
        value = jnp.where(j == 0, parts[0], parts[1])
        ordered.append(jnp.where(j < 2, value, jnp.where(j == 2, parts[2], parts[3])))
    out[...] = jnp.stack(ordered, axis=1).astype(BF16)


def near_plan(
    resid,
    moe_gain,
    attn_gain,
    gate_score,
    expert_ids,
    w_gate,
    w_up,
    w_down,
    shared_gate,
    shared_up,
    shared_down,
    w_kv,
    req_owner,
    req_blocks,
):
    rows, width = resid.shape
    zones = lax.axis_size("expert")
    slots = lax.axis_size("decode")
    capacity = 2 * rows // (zones // 2)
    piece = width // slots
    near = shared_gate.shape[0]
    hidden = shared_gate.shape[1] // zones
    half = hidden // 2
    total_rows = zones * rows
    routed_width = w_gate.shape[2]
    kv_width = w_kv.shape[1]
    group = lax.axis_index("groups")
    place = jnp.stack(
        [lax.axis_index("expert"), lax.axis_index("decode"), group]
    ).astype(jnp.int32)

    first = call(
        lambda *refs: first_kernel(capacity, *refs),
        [
            ((rows, width), BF16),
            ((rows + META, piece), BF16),
            ((rows, piece), BF16),
        ]
        + [((rows + META + half, piece), BF16)] * 3,
        [SMEM] + [VMEM] * 4 + [ANY],
        [pltpu.SemaphoreType.DMA((3,))],
        moved=6 << 20,
        name="first",
        vmem=58,
    )(
        place,
        resid,
        moe_gain,
        gate_score.reshape(1, rows),
        expert_ids.reshape(1, rows),
        shared_down,
    )
    moe_in, message, resid_share = first[:3]
    mixed_messages = first[3:6]
    second = call(
        second_kernel,
        [((near, 2 * hidden), BF16), ((hidden, piece), BF16)]
        + [((near, hidden), BF16)] * 3
        + [((near, kv_width // 2), BF16)],
        [SMEM] + [ANY] * 4,
        [pltpu.SemaphoreType.DMA((12,))],
        name="second",
        vmem=58,
    )(place, shared_gate, shared_up, shared_down, w_kv)
    own_weights, own_down, weight_messages, kv_half = second[0], second[1], second[2:5], second[5]

    mixed = [to_shift(values, s) for values, s in zip(mixed_messages, SHIFTS)]
    got = [to_shift(values, s) for values, s in zip(weight_messages, SHIFTS)]
    tops, downs = call(
        part_kernel,
        [((3 * (rows + META), piece), BF16), ((3 * half, piece), BF16)],
        [VMEM] * 3,
        name="part",
    )(*lax.optimization_barrier((*mixed, got[0]))[:3])
    down_other = swap_groups(downs)
    other_far = swap_groups(got[0])
    joined = join(*lax.optimization_barrier((got[1], got[2], down_other))[:2])
    other_rest = swap_groups(joined)


    across = lax.ppermute(tops, "decode", SWAP_CHIP)
    (token_half,) = call(
        half_kernel,
        [((total_rows, 2 * piece), BF16)],
        [SMEM] + [VMEM] * 5,
        name="half",
    )(after(place, joined, other_far), moe_in, *mixed, across)
    token_rest = lax.ppermute(token_half, "decode", SWAP_CORE)

    tokens, routed_hidden = call(
        routed_up_kernel,
        [((total_rows, width), BF16), ((total_rows, routed_width), BF16)],
        [SMEM] + [VMEM] * 4,
        flops=4 * total_rows * width * routed_width,
        moved=10 << 20,
        name="routed_up",
        vmem=22,
    )(place, token_half, token_rest, w_gate, w_up)
    (routed,) = call(
        routed_down_kernel,
        [((total_rows, width), BF16)],
        [SMEM] + [VMEM] * 6,
        flops=2 * total_rows * width * routed_width,
        moved=6 << 20,
        name="routed_down",
        vmem=16,
    )(
        place,
        routed_hidden,
        message,
        *[mixed[SHIFTS.index(s)] for s in range(1, zones)],
        w_down,
    )

    (first_half,) = call(
        gate_up_first_kernel,
        [((total_rows, half), BF16)],
        [SMEM] + [VMEM] * 5,
        flops=2 * total_rows * width * hidden,
        moved=4 << 20,
        name="gate_up_first",
        vmem=12,
    )(after(place, routed), tokens, own_weights, *got)
    kv_half = after(kv_half, joined)
    kv_far = lax.ppermute(kv_half, "expert", SWAP_CHIP)
    kv_near = lax.ppermute(kv_half, "expert", SWAP_CORE)
    kv_passed = lax.ppermute(kv_far, "expert", SWAP_CORE)
    (shared_hidden,) = call(
        gate_up_second_kernel,
        [((total_rows, hidden), BF16)],
        [SMEM] + [VMEM] * 5,
        flops=2 * total_rows * width * hidden,
        moved=4 << 20,
        name="gate_up_second",
        vmem=12,
    )(place, tokens, own_weights, first_half, other_far, other_rest)
    kv_joined = join(*lax.optimization_barrier((kv_far, kv_near, routed, shared_hidden))[:2])
    send, keep = call(
        down_kernel,
        [((total_rows, 2 * piece), BF16), ((total_rows, 2 * piece), F32)],
        [SMEM] + [VMEM] * 7,
        [pltpu.VMEM((hidden, width), BF16)],
        name="down",
        vmem=14,
    )(after(place, kv_joined), routed, shared_hidden, own_down, down_other, *mixed)
    beside = lax.ppermute(send, "decode", SWAP_CORE)
    kv_other = swap_groups(kv_joined)
    passed = call(
        pass_kernel,
        [((rows, piece), F32)] * 4 + [((rows, piece), BF16)] * 4,
        [VMEM] * 2,
        name="pass",
    )(keep, beside)
    crossed = {s: lax.ppermute(passed[4 + s], "decode", SWAP_CHIP) for s in SHIFTS + (0,)}
    kv_passed = after(kv_passed, crossed[SHIFTS[0]])
    kv_other_passed = swap_groups(kv_passed)
    returned = []
    for s in SHIFTS:
        (summed,) = call(add_kernel, [((rows, piece), BF16)], [VMEM] * 2, name="add")(
            passed[s], crossed[s]
        )
        returned.append(to_shift(summed, -s))
    layer_out, layer_rows = call(
        layer_kernel, [((rows, piece), BF16)] * 2, [VMEM] * 6, name="layer"
    )(resid_share, passed[0], crossed[0], *returned)

    handed = call(
        kv_kernel,
        [((QCAP * BLOCK, kv_width), BF16)] * 4,
        [SMEM] * 3 + [VMEM] * 11,
        [
            pltpu.VMEM((rows, width), F32),
            pltpu.VMEM((rows, kv_width), BF16),
            pltpu.VMEM((rows, width), BF16),
        ],
        name="kv",
        vmem=10,
    )(
        place,
        req_owner,
        req_blocks,
        attn_gain,
        *spread(layer_rows),
        w_kv,
        kv_far,
        kv_near,
        kv_passed,
        kv_other,
        kv_other_passed,
    )
    received = [handed[0]] + [
        lax.ppermute(values, "decode", pairs)
        for values, pairs in zip(handed[1:], (SWAP_CORE, SWAP_CHIP, SWAP_FAR))
    ]
    (kv_handed,) = call(
        hand_kernel,
        [((QCAP * BLOCK, slots, kv_width), BF16)],
        [SMEM] + [VMEM] * 4,
        name="hand",
    )(place, *received)
    return layer_out, kv_handed[None, None]


def on_device(*operands):
    resid = operands[0]
    zones = lax.axis_size("expert")
    holders = lax.axis_size("decode")
    fits = 2 * resid.shape[0] // (zones // 2) >= resid.shape[0]
    square = zones == holders == 4 and lax.axis_size("tensor") == 1
    if fits and square and lax.axis_size("groups") == 2:
        return near_plan(*operands)
    return wide_plan(*operands)


def solution(mesh):
    return jax.shard_map(
        on_device,
        mesh=mesh,
        in_specs=(
            P(("groups", "expert"), None),
            P(),
            P(),
            P(("groups", "expert")),
            P(("groups", "expert"), None),
            P("expert", None, ("decode", "tensor")),
            P("expert", None, ("decode", "tensor")),
            P("expert", ("decode", "tensor"), None),
            P("expert", ("decode", "tensor")),
            P("expert", ("decode", "tensor")),
            P(("decode", "tensor"), "expert"),
            P("expert", ("decode", "tensor")),
            P(("groups", "expert"), None),
            P(("groups", "expert"), None),
        ),
        out_specs=(
            P(("groups", "expert"), ("decode", "tensor")),
            P(("groups", "expert"), "decode", None, None, "tensor"),
        ),
        check_vma=False,
    )
```

```python
import jax
import jax.numpy as jnp
from jax import lax
from jax.experimental import pallas as pl
from jax.experimental.pallas import tpu as pltpu
from jax.sharding import PartitionSpec as P

BLOCK = 16
QCAP = 4


def rms_scale(values, gain):
    return values * lax.rsqrt(jnp.mean(values * values, axis=-1, keepdims=True) + 1e-05) * gain


def unpermute(slot_values, row_index):
    padded = jnp.concatenate(
        [slot_values, jnp.zeros((1, slot_values.shape[1]), jnp.float32)], axis=0
    )
    return padded[row_index]


def hand_over(key_value, req_owner, req_blocks):
    tok_rows, kv_width = key_value.shape
    owner_count = req_owner.shape[1]
    block_count = tok_rows // BLOCK
    owners = req_owner[0]
    counts = req_blocks[0]
    starts = jnp.cumsum(counts) - counts
    owner_index = jnp.arange(owner_count, dtype=jnp.int32)
    slot_index = jnp.arange(QCAP, dtype=jnp.int32)
    block_index = jnp.arange(block_count, dtype=jnp.int32)
    chosen = owners[:, None, None, None] == owner_index[None, :, None, None]
    chosen = chosen & (slot_index[None, None, :, None] < counts[:, None, None, None])
    chosen = chosen & (
        block_index[None, None, None, :]
        == starts[:, None, None, None] + slot_index[None, None, :, None]
    )
    choose = jnp.sum(chosen.astype(jnp.int32), axis=0).astype(jnp.bfloat16)
    kv_blocks = key_value.reshape(block_count, BLOCK, kv_width)
    sending = jnp.einsum(
        "oqb,bjw->qjow", choose, kv_blocks, preferred_element_type=jnp.float32
    ).astype(jnp.bfloat16)
    sending = sending.reshape(QCAP * BLOCK, owner_count, kv_width)
    received = lax.all_to_all(sending, "decode", split_axis=1, concat_axis=1, tiled=True)
    kv_handed = received.reshape(1, 1, QCAP * BLOCK, owner_count, kv_width)
    return kv_handed


def wide_plan(
    resid,
    moe_gain,
    attn_gain,
    gate_score,
    expert_ids,
    w_gate,
    w_up,
    w_down,
    shared_gate,
    shared_up,
    shared_down,
    w_kv,
    req_owner,
    req_blocks,
):
    tok_rows, feature_width = resid.shape
    expert_count = lax.axis_size("expert")
    pair_count = expert_count // 2
    capacity = 2 * tok_rows // pair_count
    group_size = lax.axis_size(("decode", "tensor"))
    piece_width = feature_width // group_size
    feature_start = lax.axis_index(("decode", "tensor")) * piece_width
    moe_in = rms_scale(resid.astype(jnp.float32), moe_gain).astype(jnp.bfloat16)
    routes = expert_ids[:, 0]
    onehot = (routes[:, None] == jnp.arange(pair_count, dtype=jnp.int32)[None, :]).astype(jnp.int32)
    slots = jnp.sum((jnp.cumsum(onehot, axis=0) - 1) * onehot, axis=1)
    kept = slots < capacity
    position = routes * capacity + slots
    row_index = jnp.where(kept, position, pair_count * capacity)
    selector = (
        position[None, :] == jnp.arange(pair_count * capacity, dtype=jnp.int32)[:, None]
    ) & kept[None, :]
    select_bf = selector.astype(jnp.bfloat16)
    packed = jnp.dot(select_bf, moe_in, preferred_element_type=jnp.float32).astype(jnp.bfloat16)
    packed = packed.reshape(pair_count, capacity, feature_width)
    outgoing = jnp.repeat(packed, 2, axis=0)
    incoming = lax.all_to_all(outgoing, "expert", split_axis=0, concat_axis=0, tiled=True)
    flat_in = incoming.reshape(expert_count * capacity, feature_width)
    gate_val = jnp.dot(flat_in, w_gate[0], preferred_element_type=jnp.float32)
    up_val = jnp.dot(flat_in, w_up[0], preferred_element_type=jnp.float32)
    hidden = (jax.nn.silu(gate_val) * up_val).astype(jnp.bfloat16)
    partial_flat = jnp.dot(hidden, w_down[0], preferred_element_type=jnp.float32).astype(
        jnp.bfloat16
    )
    returned = lax.all_to_all(
        partial_flat.reshape(expert_count, capacity, feature_width),
        "expert",
        split_axis=0,
        concat_axis=0,
        tiled=True,
    )
    pair_sums = jnp.sum(
        returned.reshape(pair_count, 2, capacity, feature_width).astype(jnp.float32), axis=1
    )
    routed_full = (
        unpermute(pair_sums.reshape(pair_count * capacity, feature_width), row_index)
        * gate_score[:, None]
    )
    columns = moe_in
    shared_gate_val = jnp.dot(
        columns,
        lax.all_gather(shared_gate, "expert", axis=0, tiled=True),
        preferred_element_type=jnp.float32,
    )
    shared_up_val = jnp.dot(
        columns,
        lax.all_gather(shared_up, "expert", axis=0, tiled=True),
        preferred_element_type=jnp.float32,
    )
    shared_hidden = (jax.nn.silu(shared_gate_val) * shared_up_val).astype(jnp.bfloat16)
    shared_out = jnp.dot(
        shared_hidden,
        lax.all_gather(shared_down, "expert", axis=1, tiled=True),
        preferred_element_type=jnp.float32,
    )
    total_terms = routed_full + shared_out
    summed_share = lax.psum_scatter(
        total_terms.astype(jnp.bfloat16), ("decode", "tensor"), scatter_dimension=1, tiled=True
    ).astype(jnp.float32)
    resid_share = lax.dynamic_slice_in_dim(resid, feature_start, piece_width, 1)
    layer_out = (resid_share.astype(jnp.float32) + summed_share).astype(jnp.bfloat16)
    full_rows = lax.all_gather(layer_out, ("decode", "tensor"), axis=1, tiled=True)
    attn_in = rms_scale(full_rows.astype(jnp.float32), attn_gain).astype(jnp.bfloat16)
    kv_width = w_kv.shape[1]
    columns = attn_in
    key_value = jnp.dot(
        columns,
        lax.all_gather(w_kv, "expert", axis=0, tiled=True),
        preferred_element_type=jnp.float32,
    ).astype(jnp.bfloat16)
    return layer_out, hand_over(key_value, req_owner, req_blocks)


SWAP_CORE = [(0, 1), (1, 0), (2, 3), (3, 2)]
SWAP_CHIP = [(0, 2), (2, 0), (1, 3), (3, 1)]
SWAP_FAR = [(0, 3), (3, 0), (1, 2), (2, 1)]
SWAP_GROUP = [(0, 1), (1, 0)]
SHIFTS = (2, 1, 3)
BF16 = jnp.bfloat16
F32 = jnp.float32
VMEM = pl.BlockSpec(memory_space=pltpu.VMEM)
SMEM = pl.BlockSpec(memory_space=pltpu.SMEM)
ANY = pl.BlockSpec(memory_space=pl.ANY)
META = 16


def call(body, outs, in_specs, scratch=(), flops=0, moved=0, name=None, vmem=8):
    return pl.pallas_call(
        body,
        out_shape=[jax.ShapeDtypeStruct(shape, kind) for shape, kind in outs],
        in_specs=in_specs,
        out_specs=[VMEM] * len(outs),
        scratch_shapes=list(scratch),
        compiler_params=pltpu.CompilerParams(vmem_limit_bytes=vmem << 20),
        cost_estimate=pl.CostEstimate(flops=0, bytes_accessed=0, transcendentals=0),
        name=name,
    )


def to_shift(values, shift):
    count = lax.axis_size("expert")
    return lax.ppermute(values, "expert", [(i, (i + shift) % count) for i in range(count)])


def after(values, *others):
    return lax.optimization_barrier((values,) + others)[0]


def swap_groups(values):
    return lax.ppermute(values, "groups", SWAP_GROUP)


def spread(values):
    across = lax.ppermute(values, "decode", SWAP_CHIP)
    beside = lax.ppermute(values, "decode", SWAP_CORE)
    far = lax.ppermute(across, "decode", SWAP_CORE)
    return values, beside, across, far


def lanes(index, size):
    return pl.ds(pl.multiple_of(index * size, 128), size)


def dot(a, b):
    return jnp.dot(a, b, preferred_element_type=F32)


def first_kernel(
    capacity, place, resid, gain, score, ids, down, moe_in, message, share, *rest
):
    both, sem = rest[:3], rest[3]
    top = message.shape[0]
    zone, slot, group = place[0], place[1], place[2]
    count = 4
    hidden = down.shape[0] // count
    half = hidden // 2
    copies = []

    def move(source, target):
        copies.append(pltpu.make_async_copy(source, target, sem.at[len(copies)]))

    for i, shift in enumerate(SHIFTS):
        start = lax.rem(zone + shift, count) * hidden + group * half
        move(down.at[pl.ds(pl.multiple_of(start, 128), half), :], both[i].at[top:, :])
    for copy in copies:
        copy.start()

    rows, width = resid.shape
    piece = message.shape[1]
    values = resid[...].astype(F32)
    power = jnp.mean(values * values, axis=-1, keepdims=True)
    moe_in[...] = (values * lax.rsqrt(power + 1e-05) * gain[...][None, :]).astype(BF16)
    message[:rows, :] = moe_in[:, lanes(slot, piece)]
    share[...] = resid[:, lanes(slot, piece)]
    first = lax.broadcasted_iota(jnp.int32, (rows, rows), 0)
    second = lax.broadcasted_iota(jnp.int32, (rows, rows), 1)
    across = jnp.broadcast_to(ids[...].astype(F32), (rows, rows))
    along = jnp.sum(jnp.where(first == second, across, 0.0), axis=1, keepdims=True)
    same = (along == across) & (first < second)
    slots = jnp.sum(jnp.where(same, 1.0, 0.0), axis=0, keepdims=True)
    scale = jnp.where(slots < capacity, score[...], 0.0)
    high = scale.astype(BF16)
    rest = scale - high.astype(F32)
    middle = rest.astype(BF16)
    low = (rest - middle.astype(F32)).astype(BF16)
    message[rows:, :] = jnp.zeros((META, piece), BF16)
    for i, part in enumerate((high, middle, low, ids[...].astype(F32).astype(BF16))):
        message[rows:, i * rows : (i + 1) * rows] = jnp.broadcast_to(part, (META, rows))
    for target in both:
        target[:top, :] = message[...]
    for copy in copies:
        copy.wait()


def second_kernel(place, gate, up, down, kv, own, own_down, *rest):
    messages, kv_half, sem = rest[:3], rest[3], rest[4]
    count = 4
    zone, group = place[0], place[2]
    hidden = gate.shape[1] // 4
    half = hidden // 2
    copies = []

    def move(source, target):
        copies.append(pltpu.make_async_copy(source, target, sem.at[len(copies)]))

    move(down.at[pl.ds(pl.multiple_of(zone * hidden, 128), hidden), :], own_down)
    for i, shift in enumerate(SHIFTS):
        start = lax.rem(zone + shift, count) * hidden + group * half
        for j, weights in enumerate((gate, up)):
            move(
                weights.at[:, pl.ds(pl.multiple_of(start, 128), half)],
                messages[i].at[:, j * half : (j + 1) * half],
            )
    start = group * kv_half.shape[1]
    move(kv.at[:, pl.ds(pl.multiple_of(start, 128), kv_half.shape[1])], kv_half)
    for part in range(2):
        start = zone * hidden + (group ^ part) * half
        for j, weights in enumerate((gate, up)):
            move(
                weights.at[:, pl.ds(pl.multiple_of(start, 128), half)],
                own.at[:, (2 * part + j) * half : (2 * part + j + 1) * half],
            )
    for copy in copies:
        copy.start()
    for copy in copies:
        copy.wait()


def silu(values):
    return values / (1.0 + jnp.exp(-values))


def join_kernel(*refs):
    out, row = refs[-1], 0
    for part in refs[:-1]:
        out[row : row + part.shape[0], :] = part[...]
        row += part.shape[0]


def join(*parts):
    rows = sum(part.shape[0] for part in parts)
    return call(
        join_kernel, [((rows, parts[0].shape[1]), BF16)], [VMEM] * len(parts), name="join"
    )(*parts)[0]


def part_kernel(a, b, c, tops, downs):
    top = tops.shape[0] // 3
    low = downs.shape[0] // 3
    for i, part in enumerate((a, b, c)):
        tops[i * top : (i + 1) * top, :] = part[:top, :]
        downs[i * low : (i + 1) * low, :] = part[top:, :]


def half_kernel(place, moe_in, a, b, c, across, out):
    own = (a, b, c)
    rows = moe_in.shape[0]
    top = across.shape[0] // 3
    piece = out.shape[1] // 2
    out[:rows, :piece] = moe_in[:, lanes(place[1], piece)]
    out[:rows, piece:] = moe_in[:, lanes(place[1] ^ 2, piece)]
    for i, shift in enumerate(SHIFTS):
        span = slice(shift * rows, (shift + 1) * rows)
        out[span, :piece] = own[i][:rows, :]
        out[span, piece:] = across[i * top : i * top + rows, :]


def routed_up_kernel(place, mine, theirs, gate, up, tokens, hidden):
    slot = place[1]
    piece = mine.shape[1] // 2
    for j in range(4):
        source = theirs if j % 2 else mine
        tokens[:, lanes(slot ^ j, piece)] = source[:, (j // 2) * piece : (j // 2 + 1) * piece]
    width = hidden.shape[1]
    step = 256
    for n in range(width // step):
        cols = slice(n * step, (n + 1) * step)
        gate_val = dot(tokens[...], gate[0, :, cols])
        up_val = dot(tokens[...], up[0, :, cols])
        hidden[:, cols] = (silu(gate_val) * up_val).astype(BF16)


def routed_down_kernel(place, hidden, *rest):
    messages, down, out = rest[:4], rest[4], rest[5]
    zone = place[0]
    rows = messages[0].shape[0] - META
    piece = messages[0].shape[1]
    diagonal = lax.broadcasted_iota(jnp.int32, (rows, rows), 0) == lax.broadcasted_iota(
        jnp.int32, (rows, rows), 1
    )
    mine = (zone // 2).astype(F32)
    scales = []
    for source in messages:
        info = source[rows : rows + META, :].astype(F32)[:1]
        value = info[:, :rows] + info[:, rows : 2 * rows] + info[:, 2 * rows : 3 * rows]
        value = jnp.where(info[:, 3 * rows : 4 * rows] == mine, value, 0.0)
        scales.append(jnp.sum(jnp.where(diagonal, value, 0.0), axis=1, keepdims=True))
    scale = jnp.concatenate(scales, axis=0)
    for n in range(out.shape[1] // piece):
        cols = slice(n * piece, (n + 1) * piece)
        out[:, cols] = (dot(hidden[...], down[0, :, cols]) * scale).astype(BF16)


def gate_up_half(place, tokens, own, pieces, part):
    zone = place[0]
    near = own.shape[0]
    width = own.shape[1] // 2
    half = width // 2
    both = dot(tokens[:, lanes(zone, near)], own[:, part * width : (part + 1) * width])
    for i, shift in enumerate(SHIFTS):
        source = lax.rem(zone - shift + 4, 4)
        both = both + dot(tokens[:, lanes(source, near)], pieces[i][...])
    return (silu(both[:, :half]) * both[:, half:]).astype(BF16)


def gate_up_first_kernel(place, tokens, own, a, b, c, hidden):
    hidden[...] = gate_up_half(place, tokens, own, (a, b, c), 0)


def gate_up_second_kernel(place, tokens, own, first, a, rest, hidden):
    half = first.shape[1]
    near = own.shape[0]
    b, c = rest.at[:near, :], rest.at[near:, :]
    hidden[:, lanes(place[2], half)] = first[...]
    hidden[:, lanes(1 - place[2], half)] = gate_up_half(place, tokens, own, (a, b, c), 1)


def down_kernel(place, routed, hidden, own, other, a, b, c, send, keep, weights):
    zone, slot, group = place[0], place[1], place[2]
    piece = own.shape[1]
    half = own.shape[0] // 2
    weights[:, lanes(zone, piece)] = own[...]
    for i, (shift, part) in enumerate(zip(SHIFTS, (a, b, c))):
        cols = lanes(lax.rem(zone - shift + 4, 4), piece)
        weights[pl.ds(pl.multiple_of(group * half, 128), half), cols] = part[-half:, :]
        weights[pl.ds(pl.multiple_of((1 - group) * half, 128), half), cols] = other[
            i * half : (i + 1) * half, :
        ]
    for target, parts in ((send, (1, 3)), (keep, (0, 2))):
        for i, j in enumerate(parts):
            cols = lanes(slot ^ j, piece)
            value = routed[:, cols].astype(F32) + dot(hidden[...], weights[:, cols])
            target[:, i * piece : (i + 1) * piece] = value.astype(target.dtype)


def pass_kernel(keep, beside, *outs):
    rows, piece = outs[0].shape
    for shard in range(4):
        span = slice(shard * rows, (shard + 1) * rows)
        value = keep[span, :].astype(F32) + beside[span, :].astype(F32)
        outs[shard][...] = value[:, :piece]
        outs[4 + shard][...] = value[:, piece:].astype(BF16)


def add_kernel(a, b, out):
    out[...] = (a[...] + b[...].astype(F32)).astype(BF16)


def layer_kernel(resid, own, crossed, a, b, c, out, again):
    value = own[...] + crossed[...].astype(F32) + a[...].astype(F32) + b[...].astype(F32) + c[...].astype(F32)
    value = value + resid[...].astype(F32)
    out[...] = value.astype(BF16)
    again[...] = out[...]


def kv_kernel(place, owner, blocks, gain, a, b, c, d, own, *rest):
    got, outs = rest[:3], rest[5:9]
    full, key_value, ready = rest[9:]
    rows = own.shape[0]
    other = [rest[3].at[:rows, :], rest[3].at[rows:, :], rest[4]]
    zone, slot, group = place[0], place[1], place[2]
    piece = a.shape[1]
    for j, part in enumerate((a, b, c, d)):
        full[:, lanes(slot ^ j, piece)] = part[...].astype(F32)
    values = full[...]
    power = jnp.mean(values * values, axis=-1, keepdims=True)
    ready[...] = (values * lax.rsqrt(power + 1e-05) * gain[...][None, :]).astype(BF16)
    near = own.shape[0]
    half = own.shape[1] // 2
    for part, pieces in ((0, got), (1, other)):
        value = dot(ready[:, lanes(zone, near)], own[:, lanes(group ^ part, half)])
        for i, shift in enumerate(SHIFTS):
            source = zone ^ shift
            value = value + dot(ready[:, lanes(source, near)], pieces[i][...])
        key_value[:, lanes(group ^ part, half)] = value.astype(BF16)
    held = full.shape[0] // BLOCK
    width = key_value.shape[1]
    for j in range(4):
        start, amount, begin = 0, 0, 0
        for r in range(4):
            here = owner[0, r] == (slot ^ j)
            amount = jnp.where(here, blocks[0, r], amount)
            begin = jnp.where(here, start, begin)
            start = start + blocks[0, r]
        for q in range(QCAP):
            row = jnp.clip(begin + q, 0, held - 1) * BLOCK
            chosen = key_value[pl.ds(pl.multiple_of(row, BLOCK), BLOCK), :]
            outs[j][q * BLOCK : (q + 1) * BLOCK, :] = jnp.where(
                q < amount, chosen, jnp.zeros((BLOCK, width), BF16)
            )


def hand_kernel(place, a, b, c, d, out):
    parts = [part[...].astype(F32) for part in (a, b, c, d)]
    ordered = []
    for source in range(4):
        j = place[1] ^ source
        value = jnp.where(j == 0, parts[0], parts[1])
        ordered.append(jnp.where(j < 2, value, jnp.where(j == 2, parts[2], parts[3])))
    out[...] = jnp.stack(ordered, axis=1).astype(BF16)


def near_plan(
    resid,
    moe_gain,
    attn_gain,
    gate_score,
    expert_ids,
    w_gate,
    w_up,
    w_down,
    shared_gate,
    shared_up,
    shared_down,
    w_kv,
    req_owner,
    req_blocks,
):
    rows, width = resid.shape
    zones = lax.axis_size("expert")
    slots = lax.axis_size("decode")
    capacity = 2 * rows // (zones // 2)
    piece = width // slots
    near = shared_gate.shape[0]
    hidden = shared_gate.shape[1] // zones
    half = hidden // 2
    total_rows = zones * rows
    routed_width = w_gate.shape[2]
    kv_width = w_kv.shape[1]
    group = lax.axis_index("groups")
    place = jnp.stack(
        [lax.axis_index("expert"), lax.axis_index("decode"), group]
    ).astype(jnp.int32)

    first = call(
        lambda *refs: first_kernel(capacity, *refs),
        [
            ((rows, width), BF16),
            ((rows + META, piece), BF16),
            ((rows, piece), BF16),
        ]
        + [((rows + META + half, piece), BF16)] * 3,
        [SMEM] + [VMEM] * 4 + [ANY],
        [pltpu.SemaphoreType.DMA((3,))],
        moved=6 << 20,
        name="first",
        vmem=58,
    )(
        place,
        resid,
        moe_gain,
        gate_score.reshape(1, rows),
        expert_ids.reshape(1, rows),
        shared_down,
    )
    moe_in, message, resid_share = first[:3]
    mixed_messages = first[3:6]
    second = call(
        second_kernel,
        [((near, 2 * hidden), BF16), ((hidden, piece), BF16)]
        + [((near, hidden), BF16)] * 3
        + [((near, kv_width // 2), BF16)],
        [SMEM] + [ANY] * 4,
        [pltpu.SemaphoreType.DMA((12,))],
        name="second",
        vmem=58,
    )(place, shared_gate, shared_up, shared_down, w_kv)
    own_weights, own_down, weight_messages, kv_half = second[0], second[1], second[2:5], second[5]

    mixed = [to_shift(values, s) for values, s in zip(mixed_messages, SHIFTS)]
    got = [to_shift(values, s) for values, s in zip(weight_messages, SHIFTS)]
    tops, downs = call(
        part_kernel,
        [((3 * (rows + META), piece), BF16), ((3 * half, piece), BF16)],
        [VMEM] * 3,
        name="part",
    )(*lax.optimization_barrier((*mixed, got[0]))[:3])
    down_other = swap_groups(downs)
    other_far = swap_groups(got[0])
    joined = join(*lax.optimization_barrier((got[1], got[2], down_other))[:2])
    other_rest = swap_groups(joined)


    across = lax.ppermute(tops, "decode", SWAP_CHIP)
    (token_half,) = call(
        half_kernel,
        [((total_rows, 2 * piece), BF16)],
        [SMEM] + [VMEM] * 5,
        name="half",
    )(after(place, joined, other_far), moe_in, *mixed, across)
    token_rest = lax.ppermute(token_half, "decode", SWAP_CORE)

    tokens, routed_hidden = call(
        routed_up_kernel,
        [((total_rows, width), BF16), ((total_rows, routed_width), BF16)],
        [SMEM] + [VMEM] * 4,
        flops=4 * total_rows * width * routed_width,
        moved=10 << 20,
        name="routed_up",
        vmem=22,
    )(place, token_half, token_rest, w_gate, w_up)
    (routed,) = call(
        routed_down_kernel,
        [((total_rows, width), BF16)],
        [SMEM] + [VMEM] * 6,
        flops=2 * total_rows * width * routed_width,
        moved=6 << 20,
        name="routed_down",
        vmem=16,
    )(
        place,
        routed_hidden,
        message,
        *[mixed[SHIFTS.index(s)] for s in range(1, zones)],
        w_down,
    )

    (first_half,) = call(
        gate_up_first_kernel,
        [((total_rows, half), BF16)],
        [SMEM] + [VMEM] * 5,
        flops=2 * total_rows * width * hidden,
        moved=4 << 20,
        name="gate_up_first",
        vmem=12,
    )(after(place, routed), tokens, own_weights, *got)
    kv_half = after(kv_half, joined)
    kv_far = lax.ppermute(kv_half, "expert", SWAP_CHIP)
    kv_near = lax.ppermute(kv_half, "expert", SWAP_CORE)
    kv_passed = lax.ppermute(kv_far, "expert", SWAP_CORE)
    (shared_hidden,) = call(
        gate_up_second_kernel,
        [((total_rows, hidden), BF16)],
        [SMEM] + [VMEM] * 5,
        flops=2 * total_rows * width * hidden,
        moved=4 << 20,
        name="gate_up_second",
        vmem=12,
    )(place, tokens, own_weights, first_half, other_far, other_rest)
    kv_joined = join(*lax.optimization_barrier((kv_far, kv_near, routed, shared_hidden))[:2])
    send, keep = call(
        down_kernel,
        [((total_rows, 2 * piece), BF16), ((total_rows, 2 * piece), F32)],
        [SMEM] + [VMEM] * 7,
        [pltpu.VMEM((hidden, width), BF16)],
        name="down",
        vmem=14,
    )(after(place, kv_joined), routed, shared_hidden, own_down, down_other, *mixed)
    beside = lax.ppermute(send, "decode", SWAP_CORE)
    kv_other = swap_groups(kv_joined)
    passed = call(
        pass_kernel,
        [((rows, piece), F32)] * 4 + [((rows, piece), BF16)] * 4,
        [VMEM] * 2,
        name="pass",
    )(keep, beside)
    crossed = {s: lax.ppermute(passed[4 + s], "decode", SWAP_CHIP) for s in SHIFTS}
    crossed[0] = lax.ppermute(after(passed[4], crossed[SHIFTS[1]]), "decode", SWAP_CHIP)
    kv_passed = after(kv_passed, crossed[SHIFTS[0]])
    kv_other_passed = swap_groups(kv_passed)
    returned = []
    for s in SHIFTS:
        (summed,) = call(add_kernel, [((rows, piece), BF16)], [VMEM] * 2, name="add")(
            passed[s], crossed[s]
        )
        returned.append(to_shift(summed, -s))
    layer_out, layer_rows = call(
        layer_kernel, [((rows, piece), BF16)] * 2, [VMEM] * 6, name="layer"
    )(resid_share, passed[0], crossed[0], *returned)

    handed = call(
        kv_kernel,
        [((QCAP * BLOCK, kv_width), BF16)] * 4,
        [SMEM] * 3 + [VMEM] * 11,
        [
            pltpu.VMEM((rows, width), F32),
            pltpu.VMEM((rows, kv_width), BF16),
            pltpu.VMEM((rows, width), BF16),
        ],
        name="kv",
        vmem=10,
    )(
        place,
        req_owner,
        req_blocks,
        attn_gain,
        *spread(layer_rows),
        w_kv,
        kv_far,
        kv_near,
        kv_passed,
        kv_other,
        kv_other_passed,
    )
    received = [handed[0]] + [
        lax.ppermute(values, "decode", pairs)
        for values, pairs in zip(handed[1:], (SWAP_CORE, SWAP_CHIP, SWAP_FAR))
    ]
    (kv_handed,) = call(
        hand_kernel,
        [((QCAP * BLOCK, slots, kv_width), BF16)],
        [SMEM] + [VMEM] * 4,
        name="hand",
    )(place, *received)
    return layer_out, kv_handed[None, None]


def on_device(*operands):
    resid = operands[0]
    zones = lax.axis_size("expert")
    holders = lax.axis_size("decode")
    fits = 2 * resid.shape[0] // (zones // 2) >= resid.shape[0]
    square = zones == holders == 4 and lax.axis_size("tensor") == 1
    if fits and square and lax.axis_size("groups") == 2:
        return near_plan(*operands)
    return wide_plan(*operands)


def solution(mesh):
    return jax.shard_map(
        on_device,
        mesh=mesh,
        in_specs=(
            P(("groups", "expert"), None),
            P(),
            P(),
            P(("groups", "expert")),
            P(("groups", "expert"), None),
            P("expert", None, ("decode", "tensor")),
            P("expert", None, ("decode", "tensor")),
            P("expert", ("decode", "tensor"), None),
            P("expert", ("decode", "tensor")),
            P("expert", ("decode", "tensor")),
            P(("decode", "tensor"), "expert"),
            P("expert", ("decode", "tensor")),
            P(("groups", "expert"), None),
            P(("groups", "expert"), None),
        ),
        out_specs=(
            P(("groups", "expert"), ("decode", "tensor")),
            P(("groups", "expert"), "decode", None, None, "tensor"),
        ),
        check_vma=False,
    )
```

```python
import jax
import jax.numpy as jnp
from jax import lax
from jax.experimental import pallas as pl
from jax.experimental.pallas import tpu as pltpu
from jax.sharding import PartitionSpec as P

BLOCK = 16
QCAP = 4


def rms_scale(values, gain):
    return values * lax.rsqrt(jnp.mean(values * values, axis=-1, keepdims=True) + 1e-05) * gain


def unpermute(slot_values, row_index):
    padded = jnp.concatenate(
        [slot_values, jnp.zeros((1, slot_values.shape[1]), jnp.float32)], axis=0
    )
    return padded[row_index]


def hand_over(key_value, req_owner, req_blocks):
    tok_rows, kv_width = key_value.shape
    owner_count = req_owner.shape[1]
    block_count = tok_rows // BLOCK
    owners = req_owner[0]
    counts = req_blocks[0]
    starts = jnp.cumsum(counts) - counts
    owner_index = jnp.arange(owner_count, dtype=jnp.int32)
    slot_index = jnp.arange(QCAP, dtype=jnp.int32)
    block_index = jnp.arange(block_count, dtype=jnp.int32)
    chosen = owners[:, None, None, None] == owner_index[None, :, None, None]
    chosen = chosen & (slot_index[None, None, :, None] < counts[:, None, None, None])
    chosen = chosen & (
        block_index[None, None, None, :]
        == starts[:, None, None, None] + slot_index[None, None, :, None]
    )
    choose = jnp.sum(chosen.astype(jnp.int32), axis=0).astype(jnp.bfloat16)
    kv_blocks = key_value.reshape(block_count, BLOCK, kv_width)
    sending = jnp.einsum(
        "oqb,bjw->qjow", choose, kv_blocks, preferred_element_type=jnp.float32
    ).astype(jnp.bfloat16)
    sending = sending.reshape(QCAP * BLOCK, owner_count, kv_width)
    received = lax.all_to_all(sending, "decode", split_axis=1, concat_axis=1, tiled=True)
    kv_handed = received.reshape(1, 1, QCAP * BLOCK, owner_count, kv_width)
    return kv_handed


def wide_plan(
    resid,
    moe_gain,
    attn_gain,
    gate_score,
    expert_ids,
    w_gate,
    w_up,
    w_down,
    shared_gate,
    shared_up,
    shared_down,
    w_kv,
    req_owner,
    req_blocks,
):
    tok_rows, feature_width = resid.shape
    expert_count = lax.axis_size("expert")
    pair_count = expert_count // 2
    capacity = 2 * tok_rows // pair_count
    group_size = lax.axis_size(("decode", "tensor"))
    piece_width = feature_width // group_size
    feature_start = lax.axis_index(("decode", "tensor")) * piece_width
    moe_in = rms_scale(resid.astype(jnp.float32), moe_gain).astype(jnp.bfloat16)
    routes = expert_ids[:, 0]
    onehot = (routes[:, None] == jnp.arange(pair_count, dtype=jnp.int32)[None, :]).astype(jnp.int32)
    slots = jnp.sum((jnp.cumsum(onehot, axis=0) - 1) * onehot, axis=1)
    kept = slots < capacity
    position = routes * capacity + slots
    row_index = jnp.where(kept, position, pair_count * capacity)
    selector = (
        position[None, :] == jnp.arange(pair_count * capacity, dtype=jnp.int32)[:, None]
    ) & kept[None, :]
    select_bf = selector.astype(jnp.bfloat16)
    packed = jnp.dot(select_bf, moe_in, preferred_element_type=jnp.float32).astype(jnp.bfloat16)
    packed = packed.reshape(pair_count, capacity, feature_width)
    outgoing = jnp.repeat(packed, 2, axis=0)
    incoming = lax.all_to_all(outgoing, "expert", split_axis=0, concat_axis=0, tiled=True)
    flat_in = incoming.reshape(expert_count * capacity, feature_width)
    gate_val = jnp.dot(flat_in, w_gate[0], preferred_element_type=jnp.float32)
    up_val = jnp.dot(flat_in, w_up[0], preferred_element_type=jnp.float32)
    hidden = (jax.nn.silu(gate_val) * up_val).astype(jnp.bfloat16)
    partial_flat = jnp.dot(hidden, w_down[0], preferred_element_type=jnp.float32).astype(
        jnp.bfloat16
    )
    returned = lax.all_to_all(
        partial_flat.reshape(expert_count, capacity, feature_width),
        "expert",
        split_axis=0,
        concat_axis=0,
        tiled=True,
    )
    pair_sums = jnp.sum(
        returned.reshape(pair_count, 2, capacity, feature_width).astype(jnp.float32), axis=1
    )
    routed_full = (
        unpermute(pair_sums.reshape(pair_count * capacity, feature_width), row_index)
        * gate_score[:, None]
    )
    columns = moe_in
    shared_gate_val = jnp.dot(
        columns,
        lax.all_gather(shared_gate, "expert", axis=0, tiled=True),
        preferred_element_type=jnp.float32,
    )
    shared_up_val = jnp.dot(
        columns,
        lax.all_gather(shared_up, "expert", axis=0, tiled=True),
        preferred_element_type=jnp.float32,
    )
    shared_hidden = (jax.nn.silu(shared_gate_val) * shared_up_val).astype(jnp.bfloat16)
    shared_out = jnp.dot(
        shared_hidden,
        lax.all_gather(shared_down, "expert", axis=1, tiled=True),
        preferred_element_type=jnp.float32,
    )
    total_terms = routed_full + shared_out
    summed_share = lax.psum_scatter(
        total_terms.astype(jnp.bfloat16), ("decode", "tensor"), scatter_dimension=1, tiled=True
    ).astype(jnp.float32)
    resid_share = lax.dynamic_slice_in_dim(resid, feature_start, piece_width, 1)
    layer_out = (resid_share.astype(jnp.float32) + summed_share).astype(jnp.bfloat16)
    full_rows = lax.all_gather(layer_out, ("decode", "tensor"), axis=1, tiled=True)
    attn_in = rms_scale(full_rows.astype(jnp.float32), attn_gain).astype(jnp.bfloat16)
    kv_width = w_kv.shape[1]
    columns = attn_in
    key_value = jnp.dot(
        columns,
        lax.all_gather(w_kv, "expert", axis=0, tiled=True),
        preferred_element_type=jnp.float32,
    ).astype(jnp.bfloat16)
    return layer_out, hand_over(key_value, req_owner, req_blocks)


SWAP_CORE = [(0, 1), (1, 0), (2, 3), (3, 2)]
SWAP_CHIP = [(0, 2), (2, 0), (1, 3), (3, 1)]
SWAP_FAR = [(0, 3), (3, 0), (1, 2), (2, 1)]
SWAP_GROUP = [(0, 1), (1, 0)]
SHIFTS = (2, 1, 3)
BF16 = jnp.bfloat16
F32 = jnp.float32
VMEM = pl.BlockSpec(memory_space=pltpu.VMEM)
SMEM = pl.BlockSpec(memory_space=pltpu.SMEM)
ANY = pl.BlockSpec(memory_space=pl.ANY)
META = 16


def call(body, outs, in_specs, scratch=(), flops=0, moved=0, name=None, vmem=8):
    return pl.pallas_call(
        body,
        out_shape=[jax.ShapeDtypeStruct(shape, kind) for shape, kind in outs],
        in_specs=in_specs,
        out_specs=[VMEM] * len(outs),
        scratch_shapes=list(scratch),
        compiler_params=pltpu.CompilerParams(vmem_limit_bytes=vmem << 20),
        cost_estimate=pl.CostEstimate(flops=0, bytes_accessed=0, transcendentals=0),
        name=name,
    )


def to_shift(values, shift):
    count = lax.axis_size("expert")
    return lax.ppermute(values, "expert", [(i, (i + shift) % count) for i in range(count)])


def after(values, *others):
    return lax.optimization_barrier((values,) + others)[0]


def swap_groups(values):
    return lax.ppermute(values, "groups", SWAP_GROUP)


def spread(values):
    across = lax.ppermute(values, "decode", SWAP_CHIP)
    beside = lax.ppermute(values, "decode", SWAP_CORE)
    far = lax.ppermute(across, "decode", SWAP_CORE)
    return values, beside, across, far


def lanes(index, size):
    return pl.ds(pl.multiple_of(index * size, 128), size)


def dot(a, b):
    return jnp.dot(a, b, preferred_element_type=F32)


def first_kernel(
    capacity, resid, gain, score, ids, down, moe_in, message, share, *rest
):
    both, sem = rest[:3], rest[3]
    top = message.shape[0]
    zone, slot, group = [lax.axis_index(name) for name in ("expert", "decode", "groups")]
    count = 4
    hidden = down.shape[0] // count
    half = hidden // 2
    copies = []

    def move(source, target):
        copies.append(pltpu.make_async_copy(source, target, sem.at[len(copies)]))

    for i, shift in enumerate(SHIFTS):
        start = lax.rem(zone + shift, count) * hidden + group * half
        move(down.at[pl.ds(pl.multiple_of(start, 128), half), :], both[i].at[top:, :])
    for copy in copies:
        copy.start()

    rows, width = resid.shape
    piece = message.shape[1]
    values = resid[...].astype(F32)
    power = jnp.mean(values * values, axis=-1, keepdims=True)
    moe_in[...] = (values * lax.rsqrt(power + 1e-05) * gain[...][None, :]).astype(BF16)
    message[:rows, :] = moe_in[:, lanes(slot, piece)]
    share[...] = resid[:, lanes(slot, piece)]
    first = lax.broadcasted_iota(jnp.int32, (rows, rows), 0)
    second = lax.broadcasted_iota(jnp.int32, (rows, rows), 1)
    across = jnp.broadcast_to(ids[...].astype(F32), (rows, rows))
    along = jnp.sum(jnp.where(first == second, across, 0.0), axis=1, keepdims=True)
    same = (along == across) & (first < second)
    slots = jnp.sum(jnp.where(same, 1.0, 0.0), axis=0, keepdims=True)
    scale = jnp.where(slots < capacity, score[...], 0.0)
    high = scale.astype(BF16)
    rest = scale - high.astype(F32)
    middle = rest.astype(BF16)
    low = (rest - middle.astype(F32)).astype(BF16)
    message[rows:, :] = jnp.zeros((META, piece), BF16)
    for i, part in enumerate((high, middle, low, ids[...].astype(F32).astype(BF16))):
        message[rows:, i * rows : (i + 1) * rows] = jnp.broadcast_to(part, (META, rows))
    for target in both:
        target[:top, :] = message[...]
    for copy in copies:
        copy.wait()


def second_kernel(place, gate, up, down, kv, own, own_down, *rest):
    messages, kv_half, sem = rest[:3], rest[3], rest[4]
    count = 4
    zone, group = place[0], place[2]
    hidden = gate.shape[1] // 4
    half = hidden // 2
    copies = []

    def move(source, target):
        copies.append(pltpu.make_async_copy(source, target, sem.at[len(copies)]))

    move(down.at[pl.ds(pl.multiple_of(zone * hidden, 128), hidden), :], own_down)
    for i, shift in enumerate(SHIFTS):
        start = lax.rem(zone + shift, count) * hidden + group * half
        for j, weights in enumerate((gate, up)):
            move(
                weights.at[:, pl.ds(pl.multiple_of(start, 128), half)],
                messages[i].at[:, j * half : (j + 1) * half],
            )
    start = group * kv_half.shape[1]
    move(kv.at[:, pl.ds(pl.multiple_of(start, 128), kv_half.shape[1])], kv_half)
    for part in range(2):
        start = zone * hidden + (group ^ part) * half
        for j, weights in enumerate((gate, up)):
            move(
                weights.at[:, pl.ds(pl.multiple_of(start, 128), half)],
                own.at[:, (2 * part + j) * half : (2 * part + j + 1) * half],
            )
    for copy in copies:
        copy.start()
    for copy in copies:
        copy.wait()


def silu(values):
    return values / (1.0 + jnp.exp(-values))


def join_kernel(*refs):
    out, row = refs[-1], 0
    for part in refs[:-1]:
        out[row : row + part.shape[0], :] = part[...]
        row += part.shape[0]


def join(*parts):
    rows = sum(part.shape[0] for part in parts)
    return call(
        join_kernel, [((rows, parts[0].shape[1]), BF16)], [VMEM] * len(parts), name="join"
    )(*parts)[0]


def part_kernel(a, b, c, tops, downs):
    top = tops.shape[0] // 3
    low = downs.shape[0] // 3
    for i, part in enumerate((a, b, c)):
        tops[i * top : (i + 1) * top, :] = part[:top, :]
        downs[i * low : (i + 1) * low, :] = part[top:, :]


def half_kernel(place, moe_in, a, b, c, across, out):
    own = (a, b, c)
    rows = moe_in.shape[0]
    top = across.shape[0] // 3
    piece = out.shape[1] // 2
    out[:rows, :piece] = moe_in[:, lanes(place[1], piece)]
    out[:rows, piece:] = moe_in[:, lanes(place[1] ^ 2, piece)]
    for i, shift in enumerate(SHIFTS):
        span = slice(shift * rows, (shift + 1) * rows)
        out[span, :piece] = own[i][:rows, :]
        out[span, piece:] = across[i * top : i * top + rows, :]


def routed_up_kernel(place, mine, theirs, gate, up, tokens, hidden):
    slot = place[1]
    piece = mine.shape[1] // 2
    for j in range(4):
        source = theirs if j % 2 else mine
        tokens[:, lanes(slot ^ j, piece)] = source[:, (j // 2) * piece : (j // 2 + 1) * piece]
    width = hidden.shape[1]
    step = 256
    for n in range(width // step):
        cols = slice(n * step, (n + 1) * step)
        gate_val = dot(tokens[...], gate[0, :, cols])
        up_val = dot(tokens[...], up[0, :, cols])
        hidden[:, cols] = (silu(gate_val) * up_val).astype(BF16)


def routed_down_kernel(place, hidden, *rest):
    messages, down, out = rest[:4], rest[4], rest[5]
    zone = place[0]
    rows = messages[0].shape[0] - META
    piece = messages[0].shape[1]
    diagonal = lax.broadcasted_iota(jnp.int32, (rows, rows), 0) == lax.broadcasted_iota(
        jnp.int32, (rows, rows), 1
    )
    mine = (zone // 2).astype(F32)
    scales = []
    for source in messages:
        info = source[rows : rows + META, :].astype(F32)[:1]
        value = info[:, :rows] + info[:, rows : 2 * rows] + info[:, 2 * rows : 3 * rows]
        value = jnp.where(info[:, 3 * rows : 4 * rows] == mine, value, 0.0)
        scales.append(jnp.sum(jnp.where(diagonal, value, 0.0), axis=1, keepdims=True))
    scale = jnp.concatenate(scales, axis=0)
    for n in range(out.shape[1] // piece):
        cols = slice(n * piece, (n + 1) * piece)
        out[:, cols] = (dot(hidden[...], down[0, :, cols]) * scale).astype(BF16)


def gate_up_half(place, tokens, own, pieces, part):
    zone = place[0]
    near = own.shape[0]
    width = own.shape[1] // 2
    half = width // 2
    both = dot(tokens[:, lanes(zone, near)], own[:, part * width : (part + 1) * width])
    for i, shift in enumerate(SHIFTS):
        source = lax.rem(zone - shift + 4, 4)
        both = both + dot(tokens[:, lanes(source, near)], pieces[i][...])
    return (silu(both[:, :half]) * both[:, half:]).astype(BF16)


def gate_up_first_kernel(place, tokens, own, a, b, c, hidden):
    hidden[...] = gate_up_half(place, tokens, own, (a, b, c), 0)


def gate_up_second_kernel(place, tokens, own, first, a, rest, hidden):
    half = first.shape[1]
    near = own.shape[0]
    b, c = rest.at[:near, :], rest.at[near:, :]
    hidden[:, lanes(place[2], half)] = first[...]
    hidden[:, lanes(1 - place[2], half)] = gate_up_half(place, tokens, own, (a, b, c), 1)


def down_kernel(place, routed, hidden, own, other, a, b, c, send, keep, weights):
    zone, slot, group = place[0], place[1], place[2]
    piece = own.shape[1]
    half = own.shape[0] // 2
    weights[:, lanes(zone, piece)] = own[...]
    for i, (shift, part) in enumerate(zip(SHIFTS, (a, b, c))):
        cols = lanes(lax.rem(zone - shift + 4, 4), piece)
        weights[pl.ds(pl.multiple_of(group * half, 128), half), cols] = part[-half:, :]
        weights[pl.ds(pl.multiple_of((1 - group) * half, 128), half), cols] = other[
            i * half : (i + 1) * half, :
        ]
    for target, parts in ((send, (1, 3)), (keep, (0, 2))):
        for i, j in enumerate(parts):
            cols = lanes(slot ^ j, piece)
            value = routed[:, cols].astype(F32) + dot(hidden[...], weights[:, cols])
            target[:, i * piece : (i + 1) * piece] = value.astype(target.dtype)


def pass_kernel(keep, beside, *outs):
    rows, piece = outs[0].shape
    for shard in range(4):
        span = slice(shard * rows, (shard + 1) * rows)
        value = keep[span, :].astype(F32) + beside[span, :].astype(F32)
        outs[shard][...] = value[:, :piece]
        outs[4 + shard][...] = value[:, piece:].astype(BF16)


def add_kernel(a, b, out):
    out[...] = (a[...] + b[...].astype(F32)).astype(BF16)


def layer_kernel(resid, own, crossed, a, b, c, out, again):
    value = own[...] + crossed[...].astype(F32) + a[...].astype(F32) + b[...].astype(F32) + c[...].astype(F32)
    value = value + resid[...].astype(F32)
    out[...] = value.astype(BF16)
    again[...] = out[...]


def kv_kernel(place, owner, blocks, gain, a, b, c, d, own, *rest):
    got, outs = rest[:3], rest[5:9]
    full, key_value, ready = rest[9:]
    rows = own.shape[0]
    other = [rest[3].at[:rows, :], rest[3].at[rows:, :], rest[4]]
    zone, slot, group = place[0], place[1], place[2]
    piece = a.shape[1]
    for j, part in enumerate((a, b, c, d)):
        full[:, lanes(slot ^ j, piece)] = part[...].astype(F32)
    values = full[...]
    power = jnp.mean(values * values, axis=-1, keepdims=True)
    ready[...] = (values * lax.rsqrt(power + 1e-05) * gain[...][None, :]).astype(BF16)
    near = own.shape[0]
    half = own.shape[1] // 2
    for part, pieces in ((0, got), (1, other)):
        value = dot(ready[:, lanes(zone, near)], own[:, lanes(group ^ part, half)])
        for i, shift in enumerate(SHIFTS):
            source = zone ^ shift
            value = value + dot(ready[:, lanes(source, near)], pieces[i][...])
        key_value[:, lanes(group ^ part, half)] = value.astype(BF16)
    held = full.shape[0] // BLOCK
    width = key_value.shape[1]
    for j in range(4):
        start, amount, begin = 0, 0, 0
        for r in range(4):
            here = owner[0, r] == (slot ^ j)
            amount = jnp.where(here, blocks[0, r], amount)
            begin = jnp.where(here, start, begin)
            start = start + blocks[0, r]
        for q in range(QCAP):
            row = jnp.clip(begin + q, 0, held - 1) * BLOCK
            chosen = key_value[pl.ds(pl.multiple_of(row, BLOCK), BLOCK), :]
            outs[j][q * BLOCK : (q + 1) * BLOCK, :] = jnp.where(
                q < amount, chosen, jnp.zeros((BLOCK, width), BF16)
            )


def hand_kernel(place, a, b, c, d, out):
    parts = [part[...].astype(F32) for part in (a, b, c, d)]
    ordered = []
    for source in range(4):
        j = place[1] ^ source
        value = jnp.where(j == 0, parts[0], parts[1])
        ordered.append(jnp.where(j < 2, value, jnp.where(j == 2, parts[2], parts[3])))
    out[...] = jnp.stack(ordered, axis=1).astype(BF16)


def near_plan(
    resid,
    moe_gain,
    attn_gain,
    gate_score,
    expert_ids,
    w_gate,
    w_up,
    w_down,
    shared_gate,
    shared_up,
    shared_down,
    w_kv,
    req_owner,
    req_blocks,
):
    rows, width = resid.shape
    zones = lax.axis_size("expert")
    slots = lax.axis_size("decode")
    capacity = 2 * rows // (zones // 2)
    piece = width // slots
    near = shared_gate.shape[0]
    hidden = shared_gate.shape[1] // zones
    half = hidden // 2
    total_rows = zones * rows
    routed_width = w_gate.shape[2]
    kv_width = w_kv.shape[1]
    group = lax.axis_index("groups")
    place = jnp.stack(
        [lax.axis_index("expert"), lax.axis_index("decode"), group]
    ).astype(jnp.int32)

    first = call(
        lambda *refs: first_kernel(capacity, *refs),
        [
            ((rows, width), BF16),
            ((rows + META, piece), BF16),
            ((rows, piece), BF16),
        ]
        + [((rows + META + half, piece), BF16)] * 3,
        [VMEM] * 4 + [ANY],
        [pltpu.SemaphoreType.DMA((3,))],
        moved=6 << 20,
        name="first",
        vmem=58,
    )(
        resid,
        moe_gain,
        gate_score.reshape(1, rows),
        expert_ids.reshape(1, rows),
        shared_down,
    )
    moe_in, message, resid_share = first[:3]
    mixed_messages = first[3:6]
    second = call(
        second_kernel,
        [((near, 2 * hidden), BF16), ((hidden, piece), BF16)]
        + [((near, hidden), BF16)] * 3
        + [((near, kv_width // 2), BF16)],
        [SMEM] + [ANY] * 4,
        [pltpu.SemaphoreType.DMA((12,))],
        name="second",
        vmem=58,
    )(place, shared_gate, shared_up, shared_down, w_kv)
    own_weights, own_down, weight_messages, kv_half = second[0], second[1], second[2:5], second[5]

    mixed = [to_shift(values, s) for values, s in zip(mixed_messages, SHIFTS)]
    got = [to_shift(values, s) for values, s in zip(weight_messages, SHIFTS)]
    tops, downs = call(
        part_kernel,
        [((3 * (rows + META), piece), BF16), ((3 * half, piece), BF16)],
        [VMEM] * 3,
        name="part",
    )(*lax.optimization_barrier((*mixed, got[0]))[:3])
    down_other = swap_groups(downs)
    other_far = swap_groups(got[0])
    joined = join(*lax.optimization_barrier((got[1], got[2], down_other))[:2])
    other_rest = swap_groups(joined)


    across = lax.ppermute(tops, "decode", SWAP_CHIP)
    (token_half,) = call(
        half_kernel,
        [((total_rows, 2 * piece), BF16)],
        [SMEM] + [VMEM] * 5,
        name="half",
    )(after(place, joined, other_far), moe_in, *mixed, across)
    token_rest = lax.ppermute(token_half, "decode", SWAP_CORE)

    tokens, routed_hidden = call(
        routed_up_kernel,
        [((total_rows, width), BF16), ((total_rows, routed_width), BF16)],
        [SMEM] + [VMEM] * 4,
        flops=4 * total_rows * width * routed_width,
        moved=10 << 20,
        name="routed_up",
        vmem=22,
    )(place, token_half, token_rest, w_gate, w_up)
    (routed,) = call(
        routed_down_kernel,
        [((total_rows, width), BF16)],
        [SMEM] + [VMEM] * 6,
        flops=2 * total_rows * width * routed_width,
        moved=6 << 20,
        name="routed_down",
        vmem=16,
    )(
        place,
        routed_hidden,
        message,
        *[mixed[SHIFTS.index(s)] for s in range(1, zones)],
        w_down,
    )

    (first_half,) = call(
        gate_up_first_kernel,
        [((total_rows, half), BF16)],
        [SMEM] + [VMEM] * 5,
        flops=2 * total_rows * width * hidden,
        moved=4 << 20,
        name="gate_up_first",
        vmem=12,
    )(after(place, routed), tokens, own_weights, *got)
    kv_half = after(kv_half, joined)
    kv_far = lax.ppermute(kv_half, "expert", SWAP_CHIP)
    kv_near = lax.ppermute(kv_half, "expert", SWAP_CORE)
    kv_passed = lax.ppermute(kv_far, "expert", SWAP_CORE)
    (shared_hidden,) = call(
        gate_up_second_kernel,
        [((total_rows, hidden), BF16)],
        [SMEM] + [VMEM] * 5,
        flops=2 * total_rows * width * hidden,
        moved=4 << 20,
        name="gate_up_second",
        vmem=12,
    )(place, tokens, own_weights, first_half, other_far, other_rest)
    kv_joined = join(*lax.optimization_barrier((kv_far, kv_near, routed, shared_hidden))[:2])
    send, keep = call(
        down_kernel,
        [((total_rows, 2 * piece), BF16), ((total_rows, 2 * piece), F32)],
        [SMEM] + [VMEM] * 7,
        [pltpu.VMEM((hidden, width), BF16)],
        name="down",
        vmem=14,
    )(after(place, kv_joined), routed, shared_hidden, own_down, down_other, *mixed)
    beside = lax.ppermute(send, "decode", SWAP_CORE)
    kv_other = swap_groups(kv_joined)
    passed = call(
        pass_kernel,
        [((rows, piece), F32)] * 4 + [((rows, piece), BF16)] * 4,
        [VMEM] * 2,
        name="pass",
    )(keep, beside)
    crossed = {s: lax.ppermute(passed[4 + s], "decode", SWAP_CHIP) for s in SHIFTS}
    crossed[0] = lax.ppermute(after(passed[4], crossed[SHIFTS[1]]), "decode", SWAP_CHIP)
    kv_passed = after(kv_passed, crossed[SHIFTS[0]])
    kv_other_passed = swap_groups(kv_passed)
    returned = []
    for s in SHIFTS:
        (summed,) = call(add_kernel, [((rows, piece), BF16)], [VMEM] * 2, name="add")(
            passed[s], crossed[s]
        )
        returned.append(to_shift(summed, -s))
    layer_out, layer_rows = call(
        layer_kernel, [((rows, piece), BF16)] * 2, [VMEM] * 6, name="layer"
    )(resid_share, passed[0], crossed[0], *returned)

    handed = call(
        kv_kernel,
        [((QCAP * BLOCK, kv_width), BF16)] * 4,
        [SMEM] * 3 + [VMEM] * 11,
        [
            pltpu.VMEM((rows, width), F32),
            pltpu.VMEM((rows, kv_width), BF16),
            pltpu.VMEM((rows, width), BF16),
        ],
        name="kv",
        vmem=10,
    )(
        place,
        req_owner,
        req_blocks,
        attn_gain,
        *spread(layer_rows),
        w_kv,
        kv_far,
        kv_near,
        kv_passed,
        kv_other,
        kv_other_passed,
    )
    received = [handed[0]] + [
        lax.ppermute(values, "decode", pairs)
        for values, pairs in zip(handed[1:], (SWAP_CORE, SWAP_CHIP, SWAP_FAR))
    ]
    (kv_handed,) = call(
        hand_kernel,
        [((QCAP * BLOCK, slots, kv_width), BF16)],
        [SMEM] + [VMEM] * 4,
        name="hand",
    )(place, *received)
    return layer_out, kv_handed[None, None]


def on_device(*operands):
    resid = operands[0]
    zones = lax.axis_size("expert")
    holders = lax.axis_size("decode")
    fits = 2 * resid.shape[0] // (zones // 2) >= resid.shape[0]
    square = zones == holders == 4 and lax.axis_size("tensor") == 1
    if fits and square and lax.axis_size("groups") == 2:
        return near_plan(*operands)
    return wide_plan(*operands)


def solution(mesh):
    return jax.shard_map(
        on_device,
        mesh=mesh,
        in_specs=(
            P(("groups", "expert"), None),
            P(),
            P(),
            P(("groups", "expert")),
            P(("groups", "expert"), None),
            P("expert", None, ("decode", "tensor")),
            P("expert", None, ("decode", "tensor")),
            P("expert", ("decode", "tensor"), None),
            P("expert", ("decode", "tensor")),
            P("expert", ("decode", "tensor")),
            P(("decode", "tensor"), "expert"),
            P("expert", ("decode", "tensor")),
            P(("groups", "expert"), None),
            P(("groups", "expert"), None),
        ),
        out_specs=(
            P(("groups", "expert"), ("decode", "tensor")),
            P(("groups", "expert"), "decode", None, None, "tensor"),
        ),
        check_vma=False,
    )
```
